32 devices in a mesh: dp: 8 (over z, core), tensor: 4 (over y, x).
Axes of the slice: x: 2, y: 2, z: 4, core: 2. Of those that a mesh axis runs over, the one named last changes fastest.
Arguments:
- inputs: bfloat16 [32, 1024, 1024], P('dp', 'tensor'), may hold values from -6 to 6
- encoded: bfloat16 [32, 1024, 1024], P('dp', 'tensor'), may hold values from -6 to 6
- source_lengths: int32 [32], P('dp'), may hold values from 1 to 1024, as said below
- query_weight: bfloat16 [1024, 1024], P(None, 'tensor'), may hold values from -0.1875 to 0.1875
- key_weight: bfloat16 [1024, 1024], P(None, 'tensor'), may hold values from -0.1875 to 0.1875
- value_weight: bfloat16 [1024, 1024], P(None, 'tensor'), may hold values from -0.1875 to 0.1875
- output_weight: bfloat16 [1024, 1024], P('tensor'), may hold values from -0.75 to 0.75
- cross_query: bfloat16 [1024, 1024], P(None, 'tensor'), may hold values from -0.1875 to 0.1875
- cross_key: bfloat16 [1024, 1024], P(None, 'tensor'), may hold values from -0.1875 to 0.1875
- cross_value: bfloat16 [1024, 1024], P(None, 'tensor'), may hold values from -0.1875 to 0.1875
- cross_output: bfloat16 [1024, 1024], P('tensor'), may hold values from -0.75 to 0.75
- up_weight: bfloat16 [1024, 4096], P(None, 'tensor'), may hold values from -0.1875 to 0.1875
- down_weight: bfloat16 [4096, 1024], P('tensor'), may hold values from -0.09375 to 0.09375
- adapter_in: bfloat16 [1024, 512], P(None, 'tensor'), may hold values from -0.1875 to 0.1875
- adapter_out: bfloat16 [512, 1024], P('tensor'), may hold values from -0.125 to 0.125
- adapter_bias: float32 [512], P('tensor'), may hold values from -3 to 3
- adapter_shift: float32 [1024], replicated, may hold values from -1.2 to 1.2
- norm_gains: float32 [3, 1024], replicated, may hold values from 0.5 to 1.5
- norm_shifts: float32 [3, 1024], replicated, may hold values from -1.8 to 1.8
- output_grad: bfloat16 [32, 1024, 1024], P('dp', 'tensor'), may hold values from -6 to 6
Outputs:
- result: bfloat16 [32, 1024, 1024], P('dp', 'tensor')
- input_grad: bfloat16 [32, 1024, 1024], P('dp', 'tensor')
- encoded_grad: bfloat16 [32, 1024, 1024], P('dp', 'tensor')
- adapter_in_grad: float32 [1024, 512], P(None, 'tensor')
- adapter_out_grad: float32 [512, 1024], P('tensor')
- adapter_bias_grad: float32 [512], P('tensor')
- adapter_shift_grad: float32 [1024], replicated
- gains_grad: float32 [3, 1024], replicated
- shifts_grad: float32 [3, 1024], replicated
The draws below stay inside these ranges and needn't reach their ends.
Inputs may be any that keep to these rules, and one draw needn't show every extreme that they name: `source_lengths`: in each group of 4 consecutive sequences one has more than 1024 - 1024 // 4 live source positions.
All inputs are finite; a program needn't handle non-finite values.
Results may differ from the reference program's by a relative error of at most 0.034.
Values may be sent and summed in bfloat16 or wider, within the bound.
No kernel may reach another device: no remote copies, remote signals or barrier semaphores. Data moves between devices by JAX's collectives and lax.ppermute only.
A program may use at most 512 MiB of HBM per device.

```python
import math
import jax
import jax.numpy as jnp
from jax import lax

D = 1024
HEADS = 16
FF = 4096
ADAPT = 512
HEAD = 64
LEN = 1024
SRC = 1024
SEQ_DEV = 4
SEQS = 32
N_DP = 8
N_TENSOR = 4


def draw_source_lengths(key, part):
    key = jax.random.fold_in(key, 7)
    count = SEQ_DEV * N_DP
    power_key, trim_key, pick_key, long_key = jax.random.split(key, 4)
    powers = jax.random.randint(power_key, (count,), 0, 5)
    base = jnp.right_shift(jnp.full((count,), SRC, jnp.int32), powers)
    trimmed = base - jax.random.randint(trim_key, (count,), 0, base // 2 + 1)
    chosen = jax.random.randint(pick_key, (N_DP,), 0, SEQ_DEV)
    longest = jax.random.randint(long_key, (count,), SRC - SRC // N_TENSOR + 1, SRC + 1)
    position = lax.broadcasted_iota(jnp.int32, (count,), 0)
    owners = jnp.repeat(chosen, SEQ_DEV)
    full_one = position % SEQ_DEV == owners
    return jnp.where(full_one, longest, jnp.maximum(trimmed, 1)).astype(jnp.int32)


def levels(own_key, dims, shards, low, high):
    loudness = 1.0
    for dim, parts in shards:
        heights = jax.random.uniform(jax.random.fold_in(jax.random.fold_in(own_key, 6), dim), (parts,), jnp.float32, low / len(shards), high / len(shards))
        loudness = loudness * jnp.repeat(jnp.exp(heights), dims[dim] // parts).reshape((-1,) + (1,) * (len(dims) - 1 - dim))
    return loudness


def centred(stream_key, extent, deviation, bound, shards=(), kind=jnp.bfloat16):
    result = jax.random.normal(stream_key, extent, jnp.float32) * deviation
    if len(shards) > 0:
        result = levels(stream_key, extent, shards, -0.22, 0.18) * result
    return jnp.clip(result, min=-bound, max=bound).astype(kind)


def setup_inputs(seed: int = 0) -> dict:
    arg_keys = jax.random.split(jax.random.key(seed), 21)
    inputs = centred(arg_keys[0], (SEQS, LEN, D), 1.0, 6.0, ((0, 8), (1, 4)))
    encoded = centred(arg_keys[1], (SEQS, SRC, D), 1.0, 6.0, ((0, 8), (1, 4)))
    source_lengths = draw_source_lengths(jax.random.fold_in(arg_keys[20], 71), 0)
    query_weight = centred(arg_keys[3], (D, D), D ** -0.5, 0.1875, ((1, 4),))
    key_weight = centred(arg_keys[4], (D, D), D ** -0.5, 0.1875, ((1, 4),))
    value_weight = centred(arg_keys[5], (D, D), D ** -0.5, 0.1875, ((1, 4),))
    output_weight = centred(arg_keys[6], (D, D), (D // 16) ** -0.5, 0.75, ((0, 4),))
    cross_query = centred(arg_keys[7], (D, D), D ** -0.5, 0.1875, ((1, 4),))
    cross_key = centred(arg_keys[8], (D, D), D ** -0.5, 0.1875, ((1, 4),))
    cross_value = centred(arg_keys[9], (D, D), D ** -0.5, 0.1875, ((1, 4),))
    cross_output = centred(arg_keys[10], (D, D), (D // 16) ** -0.5, 0.75, ((0, 4),))
    up_weight = centred(arg_keys[11], (D, FF), D ** -0.5, 0.1875, ((1, 4),))
    down_weight = centred(arg_keys[12], (FF, D), FF ** -0.5, 0.09375, ((0, 4),))
    adapter_in = centred(arg_keys[13], (D, ADAPT), D ** -0.5, 0.1875, ((1, 4),))
    adapter_out = centred(arg_keys[14], (ADAPT, D), (4 * ADAPT) ** -0.5, 0.125, ((0, 4),))
    adapter_bias = centred(arg_keys[15], (ADAPT,), 0.5, 3.0, ((0, 4),), jnp.float32)
    adapter_shift = centred(arg_keys[16], (D,), 0.2, 1.2, (), jnp.float32)
    norm_gains = jnp.clip(1.0 + 0.1 * jax.random.normal(arg_keys[17], (3, D), jnp.float32), 0.5, 1.5)
    norm_shifts = centred(arg_keys[18], (3, D), 0.3, 1.8, (), jnp.float32)
    output_grad = centred(arg_keys[19], (SEQS, LEN, D), 1.0, 6.0, ((0, 8), (1, 4)))
    return dict(inputs=inputs, encoded=encoded, source_lengths=source_lengths, query_weight=query_weight, key_weight=key_weight, value_weight=value_weight, output_weight=output_weight, cross_query=cross_query, cross_key=cross_key, cross_value=cross_value, cross_output=cross_output, up_weight=up_weight, down_weight=down_weight, adapter_in=adapter_in, adapter_out=adapter_out, adapter_bias=adapter_bias, adapter_shift=adapter_shift, norm_gains=norm_gains, norm_shifts=norm_shifts, output_grad=output_grad)


@jax.custom_vjp
def low(v):
    return lax.optimization_barrier(v.astype(jnp.bfloat16)).astype(jnp.float32)

@jax.custom_vjp
def low_back(v):
    return v

def low_keep(v):
    return (low(v), None)

def low_pass(kept, grad):
    return (grad,)

def back_keep(v):
    return (v, None)

def back_low(kept, grad):
    return (low(grad),)
low.defvjp(low_keep, low_pass)
low_back.defvjp(back_keep, back_low)
highest = lax.Precision.HIGHEST

def product(left, right):
    return jnp.matmul(left, right, precision=highest)

def gelu_tanh(values):
    return jax.nn.gelu(values, approximate=True)

def layer_norm(values, gain, shift):
    center = values - lax.optimization_barrier(jnp.mean(values, axis=-1, keepdims=True))
    return center * lax.rsqrt(lax.optimization_barrier(jnp.mean(center * center, axis=-1, keepdims=True)) + 1e-05) * gain + shift

def rounded(values):
    return low(low_back(values))

def split_heads(values):
    return values.reshape(values.shape[0], values.shape[1], HEADS, HEAD)

def attention(queries, keys, values, keep, weight):
    scores = jnp.einsum('sqhe,skhe->shqk', split_heads(queries), split_heads(keys), precision=highest) * HEAD ** (-0.5)
    scores = jnp.where(keep, low_back(scores), -1000000000.0)
    top_score = lax.optimization_barrier(jnp.max(scores, axis=-1, keepdims=True))
    weights = jnp.exp(scores - top_score)
    probs = low(weights / lax.optimization_barrier(jnp.sum(weights, axis=-1, keepdims=True)))
    context = jnp.einsum('shqk,skhe->sqhe', probs, split_heads(values), precision=highest)
    context = rounded(context.reshape(queries.shape[0], queries.shape[1], HEADS * HEAD))
    return low_back(product(context, weight))

def layer(inputs, encoded, lengths, trained, frozen):
    adapter_in, adapter_out, adapter_bias, adapter_shift, gains, shifts = trained
    query_weight, key_weight, value_weight, output_weight, cross_query, cross_key, cross_value, cross_output, up_weight, down_weight = frozen
    count = inputs.shape[1]
    sources = encoded.shape[1]
    query_pos = lax.broadcasted_iota(jnp.int32, (count, count), 0)
    key_pos = lax.broadcasted_iota(jnp.int32, (count, count), 1)
    causal = (key_pos <= query_pos)[None, None]
    source_pos = lax.broadcasted_iota(jnp.int32, (lengths.shape[0], sources), 1)
    padded = (source_pos < lengths[:, None])[:, None, None, :]
    attended = attention(rounded(product(inputs, query_weight)), rounded(product(inputs, key_weight)), rounded(product(inputs, value_weight)), causal, output_weight)
    first = layer_norm(inputs + attended, gains[0], shifts[0])
    first_low = low(first)
    crossed = attention(rounded(product(first_low, cross_query)), rounded(product(encoded, cross_key)), rounded(product(encoded, cross_value)), padded, cross_output)
    second = layer_norm(first + crossed, gains[1], shifts[1])
    second_low = low(second)
    hidden = low(gelu_tanh(low_back(product(second_low, up_weight))))
    adapted = low(gelu_tanh(low_back(product(second_low, adapter_in)) + adapter_bias))
    branch = low_back(product(hidden, down_weight) + 4.0 * product(adapted, adapter_out)) + 4.0 * adapter_shift
    return layer_norm(second + branch, gains[2], shifts[2])

def add_pair(left, right):
    return left + right

def reference(inputs, encoded, source_lengths, query_weight, key_weight, value_weight, output_weight, cross_query, cross_key, cross_value, cross_output, up_weight, down_weight, adapter_in, adapter_out, adapter_bias, adapter_shift, norm_gains, norm_shifts, output_grad):
    frozen = tuple((weight.astype(jnp.float32) for weight in (query_weight, key_weight, value_weight, output_weight, cross_query, cross_key, cross_value, cross_output, up_weight, down_weight)))
    trained = (adapter_in.astype(jnp.float32), adapter_out.astype(jnp.float32), adapter_bias.astype(jnp.float32), adapter_shift.astype(jnp.float32), norm_gains.astype(jnp.float32), norm_shifts.astype(jnp.float32))
    group = math.gcd(inputs.shape[0], max(1, 2048 // LEN))
    blocks = inputs.shape[0] // group

    def regroup(values):
        return values.astype(jnp.float32).reshape((blocks, group) + values.shape[1:])

    def step(totals, pieces):
        piece_in, piece_enc, piece_len, piece_grad = pieces

        def apply(input_part, encoded_part, trained_part):
            return layer(input_part, encoded_part, piece_len, trained_part, frozen)
        outcome, pull = jax.vjp(apply, piece_in, piece_enc, trained)
        grad_in, grad_enc, grad_trained = pull(piece_grad)
        return (jax.tree.map(add_pair, totals, grad_trained), (outcome, grad_in, grad_enc))
    zeros = jax.tree.map(jnp.zeros_like, trained)
    totals, (outcomes, grads_in, grads_enc) = lax.scan(step, zeros, (regroup(inputs), regroup(encoded), source_lengths.reshape(blocks, group).astype(jnp.int32), regroup(output_grad)))
    return (outcomes.reshape(inputs.shape).astype(jnp.bfloat16), grads_in.reshape(inputs.shape).astype(jnp.bfloat16), grads_enc.reshape(encoded.shape).astype(jnp.bfloat16), totals[0], totals[1], totals[2], totals[3], totals[4], totals[5])
```

```python
import functools
import jax
import jax.numpy as jnp
from jax import lax
from jax.experimental import pallas as pl
from jax.experimental.pallas import tpu as pltpu
from jax.sharding import PartitionSpec as P

HEAD = 64
F32 = jnp.float32
BF16 = jnp.bfloat16
LOG2E = 1.4426950408889634
LN2 = 0.6931471805599453
VMEM_LIMIT = 60 * 2**20
ROWS = 256


def nn(left, right):
    return lax.dot_general(left, right, (((1,), (0,)), ((), ())), preferred_element_type=F32)


def nt(left, right):
    return lax.dot_general(left, right, (((1,), (1,)), ((), ())), preferred_element_type=F32)


def tn(left, right):
    return lax.dot_general(left, right, (((0,), (0,)), ((), ())), preferred_element_type=F32)


def norm_rows(values):
    center = values - jnp.mean(values, axis=-1, keepdims=True)
    scale = lax.rsqrt(jnp.mean(center * center, axis=-1, keepdims=True) + 1e-05)
    return center * scale, scale


def norm_back_rows(grad, normed, scale, gain):
    inner = grad * gain
    middle = jnp.mean(inner, axis=-1, keepdims=True)
    along = jnp.mean(inner * normed, axis=-1, keepdims=True)
    return scale * (inner - middle - normed * along)


def gelu_and_slope(v):
    root = 0.7978845608028654
    square = v * v
    t = jnp.tanh(v * (root + (root * 0.044715) * square))
    half = 0.5 + 0.5 * t
    slope = half + (v * half) * (1.0 - t) * (root + (3.0 * root * 0.044715) * square)
    return v * half, slope


def attend_kernel(causal, first, *refs):
    refs = list(refs)
    length_ref = None if causal else refs.pop(0)
    xq_ref = refs.pop(0)
    xkv_ref = xq_ref if causal else refs.pop(0)
    pieces = [refs.pop(0) for _ in range(4)]
    if not first:
        refs = refs[5:]
    e_ref, hd_ref, il_ref, ctx_ref, wf_ref, qkv = refs
    step = pl.program_id(0)
    span = xq_ref.shape[0]
    sources = xkv_ref.shape[0]
    part = pieces[0].shape[2]

    @pl.when(step == 0)
    def _():
        for t in range(4):
            for m in range(4):
                wf_ref[m, t * part : (t + 1) * part, :] = pieces[t][0, m]
        qkv[0] = (nt(wf_ref[0], xq_ref[...]) * (LOG2E * HEAD**-0.5)).astype(BF16)
        qkv[1] = nt(wf_ref[1], xkv_ref[...]).astype(BF16)
        qkv[2] = nt(wf_ref[2], xkv_ref[...]).astype(BF16)

    pair = pl.ds(pl.multiple_of(step * 128, 128), 128)
    q2, k2, v2 = qkv[0, pair, :], qkv[1, pair, :], qkv[2, pair, :]
    hd_ref[0], hd_ref[1], hd_ref[2] = q2, k2, v2
    block = min(512, span)
    for i in range(span // block):
        n = (i + 1) * block if causal else sources
        cols = slice(i * block, (i + 1) * block)
        scores = [
            tn(k2[h * 64 : h * 64 + 64, :n], q2[h * 64 : h * 64 + 64, cols]) for h in range(2)
        ]
        contexts = []
        for h in range(2):
            s = scores[h]
            if causal:
                key = lax.broadcasted_iota(jnp.int32, (block, block), 0)
                query = lax.broadcasted_iota(jnp.int32, (block, block), 1)
                tail = jnp.where(key <= query, s[n - block :], -1e9)
                s = jnp.concatenate([s[: n - block], tail], axis=0) if n > block else tail
            else:
                key = lax.broadcasted_iota(jnp.int32, (n, block), 0)
                s = jnp.where(key < length_ref[0], s, -1e9)
            e = jnp.exp2(s - jnp.max(s, axis=0, keepdims=True))
            inverse = 1.0 / jnp.sum(e, axis=0, keepdims=True)
            low = e.astype(BF16)
            e_ref[h, :n, cols] = low
            il_ref[h, :, cols] = inverse
            contexts.append((nn(v2[h * 64 : h * 64 + 64, :n], low) * inverse).astype(BF16))
        joined = jnp.concatenate(contexts, axis=0)
        hd_ref[3, :, cols] = joined
        ctx_ref[cols, :] = joined.T


def attend_slot(slot, length, xq, xkv, pieces, before):
    causal = xkv is None
    span, width = xq.shape
    sources = span if causal else xkv.shape[0]
    heads = width // HEAD
    part = pieces[0][0].shape[2]
    first = before is None
    whole = lambda shape: pl.BlockSpec(shape, lambda j: (0,) * len(shape), pipeline_mode=pl.Buffered(1))
    operands, specs = [], []
    if not causal:
        operands.append(length)
        specs.append(pl.BlockSpec(memory_space=pltpu.SMEM))
    operands.append(xq)
    specs.append(whole((span, width)))
    if not causal:
        operands.append(xkv)
        specs.append(whole((sources, width)))
    for array, index in pieces:
        operands.append(array)
        specs.append(
            pl.BlockSpec(
                (1, 4, part, width), lambda j, index=index: (index, 0, 0, 0), pipeline_mode=pl.Buffered(1)
            )
        )
    aliases = {}
    if not first:
        for n, buffer in enumerate(before):
            aliases[len(operands)] = n
            operands.append(buffer)
            specs.append(pl.BlockSpec(memory_space=pl.ANY))
    out_shape = (
        jax.ShapeDtypeStruct((heads, sources, span), BF16),
        jax.ShapeDtypeStruct((4, width, span), BF16),
        jax.ShapeDtypeStruct((heads, 1, span), F32),
        jax.ShapeDtypeStruct((span, width), BF16),
        jax.ShapeDtypeStruct((4, width, width), BF16),
    )
    out_specs = (
        pl.BlockSpec((2, sources, span), lambda j: (2 * slot + j, 0, 0)),
        pl.BlockSpec((4, 128, span), lambda j: (0, 2 * slot + j, 0)),
        pl.BlockSpec((2, 1, span), lambda j: (2 * slot + j, 0, 0)),
        pl.BlockSpec((span, 128), lambda j: (0, 2 * slot + j)),
        pl.BlockSpec((4, 4 * part, width), lambda j: (0, slot, 0)),
    )
    return pl.pallas_call(
        functools.partial(attend_kernel, causal, first),
        grid=(2,),
        in_specs=specs,
        out_specs=out_specs,
        out_shape=out_shape,
        scratch_shapes=[pltpu.VMEM((3, 4 * part, max(span, sources)), BF16)],
        input_output_aliases=aliases,
        compiler_params=pltpu.CompilerParams(vmem_limit_bytes=VMEM_LIMIT),
        cost_estimate=pl.CostEstimate(
            flops=12 * 10**9, bytes_accessed=16 * 2**20, transcendentals=4 * span * sources
        ),
        name="self_attend" if causal else "cross_attend",
    )(*operands)


def out_norm_kernel(ctx_ref, wo_ref, x_ref, gain_ref, shift_ref, low_ref, n_ref, r_ref):
    total = nn(ctx_ref[...], wo_ref[0]) + x_ref[...].astype(F32)
    normed, scale = norm_rows(total)
    low_ref[...] = (normed * gain_ref[...] + shift_ref[...]).astype(BF16)
    n_ref[...] = normed.astype(BF16)
    r_ref[...] = scale


def out_norm(ctx, weights, residual, gain, shift):
    span, width = ctx.shape
    rows = lambda w: pl.BlockSpec((ROWS, w), lambda i: (i, 0))
    line = pl.BlockSpec((1, width), lambda i: (0, 0))
    return pl.pallas_call(
        out_norm_kernel,
        grid=(span // ROWS,),
        in_specs=[
            rows(width),
            pl.BlockSpec((1, width, width), lambda i: (3, 0, 0), pipeline_mode=pl.Buffered(1)),
            rows(width),
            line,
            line,
        ],
        out_specs=(rows(width), rows(width), rows(1)),
        out_shape=(
            jax.ShapeDtypeStruct((span, width), BF16),
            jax.ShapeDtypeStruct((span, width), BF16),
            jax.ShapeDtypeStruct((span, 1), F32),
        ),
        compiler_params=pltpu.CompilerParams(vmem_limit_bytes=VMEM_LIMIT),
        cost_estimate=pl.CostEstimate(
            flops=2 * span * width * width, bytes_accessed=10 * 2**20, transcendentals=0
        ),
        name="out_norm",
    )(ctx, weights, residual, gain, shift)


def feed_kernel(first, units, extra, *refs):
    refs = list(refs)
    x_ref, bias_ref = refs[:2]
    pieces = refs[2:6]
    refs = refs[6:]
    acc_in = None
    if not first:
        acc_in = refs[0]
        refs = refs[8:]
    acc_ref, gp_ref, gpa_ref, alow_ref, up_ref, down_ref, ain_ref, aout_ref = refs

    @pl.when(pl.program_id(0) == 0)
    def _():
        for t in range(4):
            piece = pieces[t]
            up_ref[t * units : (t + 1) * units, :] = piece[0, :units]
            down_ref[t * units : (t + 1) * units, :] = piece[0, units : 2 * units]
            ain_ref[t * extra : (t + 1) * extra, :] = piece[0, 2 * units : 2 * units + extra]
            aout_ref[t * extra : (t + 1) * extra, :] = piece[0, 2 * units + extra :]

    x = x_ref[...]
    a, slope = gelu_and_slope(nt(x, ain_ref[...]) + bias_ref[...])
    a_low = a.astype(BF16)
    alow_ref[...] = a_low
    gpa_ref[...] = slope.astype(BF16)
    total = 4.0 * nn(a_low, aout_ref[...])
    if not first:
        total = total + acc_in[...]
    for t in range(4):
        part = slice(t * units, (t + 1) * units)
        h, slope = gelu_and_slope(nt(x, up_ref[part, :]))
        gp_ref[:, part] = slope.astype(BF16)
        total = total + nn(h.astype(BF16), down_ref[part, :])
    acc_ref[...] = total


def feed_slot(slot, x, bias, pieces, before, units, extra):
    span, width = x.shape
    first = before is None
    rows = lambda w: pl.BlockSpec((ROWS, w), lambda i: (i, 0))
    operands = [x, bias]
    specs = [rows(width), pl.BlockSpec((1, 4 * extra), lambda i: (0, 0))]
    tall = 2 * units + 2 * extra
    for array, index in pieces:
        operands.append(array)
        specs.append(
            pl.BlockSpec((1, tall, width), lambda i, index=index: (index, 0, 0), pipeline_mode=pl.Buffered(1))
        )
    aliases = {}
    if not first:
        for n, buffer in enumerate(before):
            aliases[len(operands)] = n
            operands.append(buffer)
            specs.append(rows(width) if n == 0 else pl.BlockSpec(memory_space=pl.ANY))
    out_shape = (
        jax.ShapeDtypeStruct((span, width), F32),
        jax.ShapeDtypeStruct((span, 16 * units), BF16),
        jax.ShapeDtypeStruct((span, 16 * extra), BF16),
        jax.ShapeDtypeStruct((span, 16 * extra), BF16),
        jax.ShapeDtypeStruct((16 * units, width), BF16),
        jax.ShapeDtypeStruct((16 * units, width), BF16),
        jax.ShapeDtypeStruct((16 * extra, width), BF16),
        jax.ShapeDtypeStruct((16 * extra, width), BF16),
    )
    out_specs = (
        rows(width),
        pl.BlockSpec((ROWS, 4 * units), lambda i: (i, slot)),
        pl.BlockSpec((ROWS, 4 * extra), lambda i: (i, slot)),
        pl.BlockSpec((ROWS, 4 * extra), lambda i: (i, slot)),
        pl.BlockSpec((4 * units, width), lambda i: (slot, 0)),
        pl.BlockSpec((4 * units, width), lambda i: (slot, 0)),
        pl.BlockSpec((4 * extra, width), lambda i: (slot, 0)),
        pl.BlockSpec((4 * extra, width), lambda i: (slot, 0)),
    )
    return pl.pallas_call(
        functools.partial(feed_kernel, first, units, extra),
        grid=(span // ROWS,),
        in_specs=specs,
        out_specs=out_specs,
        out_shape=out_shape,
        input_output_aliases=aliases,
        compiler_params=pltpu.CompilerParams(vmem_limit_bytes=VMEM_LIMIT),
        cost_estimate=pl.CostEstimate(
            flops=7 * 10**9, bytes_accessed=20 * 2**20, transcendentals=4 * span * units
        ),
        name="feed",
    )(*operands)


def last_norm_kernel(acc_ref, x_ref, extra_ref, gain_ref, shift_ref, grad_ref, out_ref, low_ref, sum_ref):
    total = acc_ref[...] + x_ref[...].astype(F32) + 4.0 * extra_ref[...]
    normed, scale = norm_rows(total)
    out_ref[...] = (normed * gain_ref[...] + shift_ref[...]).astype(BF16)
    grad = grad_ref[...].astype(F32)
    back = norm_back_rows(grad, normed, scale, gain_ref[...])
    low_ref[...] = back.astype(BF16)

    @pl.when(pl.program_id(0) == 0)
    def _():
        sum_ref[...] = jnp.zeros_like(sum_ref)

    sum_ref[0:1, :] += jnp.sum(grad * normed, axis=0, keepdims=True)
    sum_ref[1:2, :] += jnp.sum(grad, axis=0, keepdims=True)
    sum_ref[2:3, :] += 4.0 * jnp.sum(back, axis=0, keepdims=True)


def last_norm(acc, second, extra_shift, gain, shift, grad):
    span, width = acc.shape
    rows = pl.BlockSpec((ROWS, width), lambda i: (i, 0))
    line = pl.BlockSpec((1, width), lambda i: (0, 0))
    return pl.pallas_call(
        last_norm_kernel,
        grid=(span // ROWS,),
        in_specs=[rows, rows, line, line, line, rows],
        out_specs=(rows, rows, pl.BlockSpec((8, width), lambda i: (0, 0))),
        out_shape=(
            jax.ShapeDtypeStruct((span, width), BF16),
            jax.ShapeDtypeStruct((span, width), BF16),
            jax.ShapeDtypeStruct((8, width), F32),
        ),
        compiler_params=pltpu.CompilerParams(vmem_limit_bytes=VMEM_LIMIT),
        cost_estimate=pl.CostEstimate(flops=30 * 2**20, bytes_accessed=12 * 2**20, transcendentals=0),
        name="last_norm",
    )(acc, second, extra_shift, gain, shift, grad)


def feed_back_kernel(
    g_ref, up_ref, down_ref, gp_ref, ain_ref, aout_ref, gpa_ref, alow_ref, x_ref, n_ref, r_ref, gain_ref,
    low_ref, ing_ref, outg_ref, bias_ref, sum_ref, acc,
):
    step = pl.program_id(0)
    span = g_ref.shape[0]

    @pl.when(step == 0)
    def _():
        g = g_ref[...]
        a = 4.0 * nt(g, aout_ref[...]) * gpa_ref[...].astype(F32)
        bias_ref[...] = jnp.sum(a, axis=0, keepdims=True)
        a_low = a.astype(BF16)
        ing_ref[...] = tn(a_low, x_ref[...]).astype(BF16)
        outg_ref[...] = (4.0 * tn(alow_ref[...], g)).astype(BF16)
        acc[...] = nn(a_low, ain_ref[...]) + g.astype(F32)

    for i in range(span // ROWS):
        rows = slice(i * ROWS, (i + 1) * ROWS)
        h = (nt(g_ref[rows, :], down_ref[...]) * gp_ref[rows, :].astype(F32)).astype(BF16)
        acc[rows, :] += nn(h, up_ref[...])

    @pl.when(step == pl.num_programs(0) - 1)
    def _():
        sum_ref[...] = jnp.zeros_like(sum_ref)
        for i in range(span // ROWS):
            rows = slice(i * ROWS, (i + 1) * ROWS)
            grad = acc[rows, :]
            normed = n_ref[rows, :].astype(F32)
            back = norm_back_rows(grad, normed, r_ref[rows, :], gain_ref[...])
            low_ref[rows, :] = back.astype(BF16)
            sum_ref[0:1, :] += jnp.sum(grad * normed, axis=0, keepdims=True)
            sum_ref[1:2, :] += jnp.sum(grad, axis=0, keepdims=True)


def feed_back(g, kept, x, normed, scale, gain):
    _, gp, gpa, alow, up, down, ain, aout = kept
    span, width = g.shape
    units, extra = up.shape[0], ain.shape[0]
    chunk = min(512, units)
    whole = lambda a: pl.BlockSpec(a.shape, lambda j: (0,) * a.ndim, pipeline_mode=pl.Buffered(1))
    out_shape = (
        jax.ShapeDtypeStruct((span, width), BF16),
        jax.ShapeDtypeStruct((extra, width), BF16),
        jax.ShapeDtypeStruct((extra, width), BF16),
        jax.ShapeDtypeStruct((1, extra), F32),
        jax.ShapeDtypeStruct((8, width), F32),
    )
    return pl.pallas_call(
        feed_back_kernel,
        grid=(units // chunk,),
        in_specs=[
            whole(g),
            pl.BlockSpec((chunk, width), lambda j: (j, 0)),
            pl.BlockSpec((chunk, width), lambda j: (j, 0)),
            pl.BlockSpec((span, chunk), lambda j: (0, j)),
            whole(ain),
            whole(aout),
            whole(gpa),
            whole(alow),
            whole(x),
            whole(normed),
            whole(scale),
            whole(gain),
        ],
        out_specs=tuple(pl.BlockSpec(s.shape, lambda j: (0, 0)) for s in out_shape),
        out_shape=out_shape,
        scratch_shapes=[pltpu.VMEM((span, width), F32)],
        compiler_params=pltpu.CompilerParams(vmem_limit_bytes=VMEM_LIMIT),
        cost_estimate=pl.CostEstimate(
            flops=4 * span * width * units + 8 * span * width * extra,
            bytes_accessed=40 * 2**20,
            transcendentals=0,
        ),
        name="feed_back",
    )(g, up, down, gp, ain, aout, gpa, alow, x, normed, scale, gain)


def attention_back_kernel(causal, *refs):
    refs = list(refs)
    g_ref, wf_ref, e_ref, hd_ref, il_ref = refs[:5]
    refs = refs[5:]
    if causal:
        out_ref, ct, dq, dk, dv = refs
    else:
        n_ref, r_ref, gain_ref, low_ref, enc_ref, sum_ref, ct, dq, dk, dv = refs
    step = pl.program_id(0)
    span = g_ref.shape[0]
    sources = e_ref.shape[1]

    @pl.when(step == 0)
    def _():
        ct[...] = nt(wf_ref[3], g_ref[...]).astype(BF16)

    pair = pl.ds(pl.multiple_of(step * 128, 128), 128)
    c2 = ct[pair, :]
    block = min(512, span)
    heads = [slice(h * 64, h * 64 + 64) for h in range(2)]
    scaled, dots = [], []
    for h in range(2):
        c = c2[heads[h], :].astype(F32) * il_ref[h]
        dots.append(jnp.sum(c * hd_ref[3, heads[h], :].astype(F32), axis=0, keepdims=True))
        scaled.append(c.astype(BF16))
    sums_k, sums_v = [None, None], [None, None]
    for i in reversed(range(span // block)):
        n = (i + 1) * block if causal else sources
        cols = slice(i * block, (i + 1) * block)
        grads = [tn(hd_ref[2, heads[h], :n], scaled[h][:, cols]) for h in range(2)]
        queries = []
        for h in range(2):
            e = e_ref[h, :n, cols]
            ds = (e.astype(F32) * (grads[h] - dots[h][:, cols])).astype(BF16)
            queries.append((nn(hd_ref[1, heads[h], :n], ds) * HEAD**-0.5).astype(BF16))
            gk = nn(ds, hd_ref[0, heads[h], cols].T)
            gv = nn(e, scaled[h][:, cols].T)
            if sums_k[h] is None:
                sums_k[h], sums_v[h] = gk, gv
            elif n == sums_k[h].shape[0]:
                sums_k[h], sums_v[h] = sums_k[h] + gk, sums_v[h] + gv
            else:
                sums_k[h] = jnp.concatenate([sums_k[h][:n] + gk, sums_k[h][n:]], axis=0)
                sums_v[h] = jnp.concatenate([sums_v[h][:n] + gv, sums_v[h][n:]], axis=0)
        dq[cols, pair] = jnp.concatenate(queries, axis=0).T
    dk[:, pair] = (jnp.concatenate(sums_k, axis=1) * LN2).astype(BF16)
    dv[:, pair] = jnp.concatenate(sums_v, axis=1).astype(BF16)

    @pl.when(step == pl.num_programs(0) - 1)
    def _():
        if not causal:
            sum_ref[...] = jnp.zeros_like(sum_ref)
        for i in range(span // ROWS):
            rows = slice(i * ROWS, (i + 1) * ROWS)
            from_q = nn(dq[rows, :], wf_ref[0]) + g_ref[rows, :].astype(F32)
            from_kv = nn(dk[rows, :], wf_ref[1]) + nn(dv[rows, :], wf_ref[2])
            if causal:
                out_ref[rows, :] = (from_q + from_kv).astype(BF16)
            else:
                enc_ref[rows, :] = from_kv.astype(BF16)
                normed = n_ref[rows, :].astype(F32)
                back = norm_back_rows(from_q, normed, r_ref[rows, :], gain_ref[...])
                low_ref[rows, :] = back.astype(BF16)
                sum_ref[0:1, :] += jnp.sum(from_q * normed, axis=0, keepdims=True)
                sum_ref[1:2, :] += jnp.sum(from_q, axis=0, keepdims=True)


def attention_back(g, kept, norm):
    e, hd, il, _, wf = kept
    causal = norm is None
    span, width = g.shape
    heads, sources, _ = e.shape
    whole = lambda a: pl.BlockSpec(a.shape, lambda j: (0,) * a.ndim, pipeline_mode=pl.Buffered(1))
    operands = [g, wf, e, hd, il]
    specs = [
        whole(g),
        whole(wf),
        pl.BlockSpec((2, sources, span), lambda j: (j, 0, 0)),
        pl.BlockSpec((4, 128, span), lambda j: (0, j, 0)),
        pl.BlockSpec((2, 1, span), lambda j: (j, 0, 0)),
    ]
    low = jax.ShapeDtypeStruct((span, width), BF16)
    if causal:
        out_shape = (low,)
    else:
        operands += list(norm)
        specs += [whole(a) for a in norm]
        out_shape = (low, jax.ShapeDtypeStruct((sources, width), BF16), jax.ShapeDtypeStruct((8, width), F32))
    return pl.pallas_call(
        functools.partial(attention_back_kernel, causal),
        grid=(heads // 2,),
        in_specs=specs,
        out_specs=tuple(
            pl.BlockSpec(s.shape, lambda j: (0, 0), pipeline_mode=pl.Buffered(1)) for s in out_shape
        ),
        out_shape=out_shape,
        scratch_shapes=[
            pltpu.VMEM((width, span), BF16),
            pltpu.VMEM((span, width), BF16),
            pltpu.VMEM((sources, width), BF16),
            pltpu.VMEM((sources, width), BF16),
        ],
        compiler_params=pltpu.CompilerParams(vmem_limit_bytes=VMEM_LIMIT),
        cost_estimate=pl.CostEstimate(
            flops=40 * 10**9, bytes_accessed=60 * 2**20, transcendentals=0
        ),
        name="self_back" if causal else "cross_back",
    )(*operands)


def over(axis, bit):
    size = lax.axis_size(axis)
    pairs = [(i, i ^ bit) for i in range(size)]
    return lambda values: lax.ppermute(values, axis, pairs)


def swap_positions(values, place):
    received = []
    for k in (1, 2, 3):
        block = lax.dynamic_index_in_dim(values, place ^ k, 0, keepdims=True)
        received.append(over("tensor", k)(block))
    for k in (1, 2, 3):
        values = lax.dynamic_update_index_in_dim(values, received[k - 1], place ^ k, 0)
    return values


def spread_pieces(own):
    slots = []
    for k in (1, 2, 3):
        here = over("tensor", k)(own)
        far = over("dp", 2)(here)
        slots.append([here, over("dp", 1)(here), far, over("dp", 1)(far)])
    return slots


def whole_sequences(
    inputs,
    encoded,
    source_lengths,
    query_weight,
    key_weight,
    value_weight,
    output_weight,
    cross_query,
    cross_key,
    cross_value,
    cross_output,
    up_weight,
    down_weight,
    adapter_in,
    adapter_out,
    adapter_bias,
    adapter_shift,
    norm_gains,
    norm_shifts,
    output_grad,
):
    place = lax.axis_index("tensor")
    turn = lax.axis_index("dp") % 4
    _, share, width = inputs.shape
    span = 4 * share
    units, extra = up_weight.shape[1] // 4, adapter_in.shape[1] // 4

    def cut(weight, transpose):
        return (weight.T if transpose else weight).reshape(4, -1, width)

    x = swap_positions(inputs, place).reshape(span, width)
    self_own = jnp.stack(
        [cut(query_weight, True), cut(key_weight, True), cut(value_weight, True), cut(output_weight, False)],
        axis=1,
    )
    cross_own = jnp.stack(
        [cut(cross_query, True), cut(cross_key, True), cut(cross_value, True), cut(cross_output, False)],
        axis=1,
    )
    feed_own = jnp.concatenate(
        [cut(up_weight, True), cut(down_weight, False), cut(adapter_in, True), cut(adapter_out, False)],
        axis=1,
    )
    pick = lambda packed: lax.dynamic_index_in_dim(packed, turn, 0, keepdims=True)
    self_slots = spread_pieces(pick(self_own))
    source = swap_positions(encoded, place).reshape(span, width)
    cross_slots = spread_pieces(pick(cross_own))
    feed_slots = spread_pieces(pick(feed_own))
    grad = swap_positions(output_grad, place).reshape(span, width)

    def turned(values, axis):
        for bit in (1, 2):
            parts = [lax.index_in_dim(values, t ^ bit, axis) for t in range(4)]
            swapped = lax.concatenate(parts, axis)
            values = jnp.where((turn & bit) != 0, swapped, values)
        return values

    bias_own = adapter_bias.reshape(1, -1)
    biases = [bias_own] + [over("tensor", k)(bias_own) for k in (1, 2, 3)]

    def pieces_of(own, slots, slot):
        if slot == 0:
            return [(own, t) for t in range(4)]
        return [(piece, 0) for piece in slots[slot - 1]]

    gain = lambda j: norm_gains[j : j + 1]
    shift = lambda j: norm_shifts[j : j + 1]
    length = lax.dynamic_slice_in_dim(source_lengths, place, 1, 0)

    self_kept = None
    for slot in range(4):
        self_kept = attend_slot(slot, None, x, None, pieces_of(self_own, self_slots, slot), self_kept)
    first, normed_one, scale_one = out_norm(self_kept[3], self_kept[4], x, gain(0), shift(0))
    cross_kept = None
    for slot in range(4):
        cross_kept = attend_slot(
            slot, length, first, source, pieces_of(cross_own, cross_slots, slot), cross_kept
        )
    second, normed_two, scale_two = out_norm(cross_kept[3], cross_kept[4], first, gain(1), shift(1))
    feed_kept = None
    for slot in range(4):
        bias = biases[slot]
        if slot > 0:
            bias = turned(bias.reshape(4, extra), 0).reshape(1, -1)
        feed_kept = feed_slot(
            slot, second, bias, pieces_of(feed_own, feed_slots, slot), feed_kept, units, extra
        )
    outcome, branch_low, sums_three = last_norm(
        feed_kept[0], second, adapter_shift.reshape(1, -1), gain(2), shift(2), grad
    )
    result = swap_positions(outcome.reshape(4, share, width), place)
    cross_low, in_grad, out_grad, bias_grad, sums_two = feed_back(
        branch_low, feed_kept, second, normed_two, scale_two, gain(1)
    )

    def natural(values):
        slots = values.reshape((4, 4, extra) + values.shape[1:])
        swapped = turned(slots, 1)
        return [slots[0]] + [swapped[k] for k in (1, 2, 3)]

    grads = [jnp.stack(pair) for pair in zip(natural(in_grad), natural(out_grad))]
    sent = [over("tensor", k)(grads[k]) for k in (1, 2, 3)]
    self_low, encoded_back, sums_one = attention_back(
        cross_low, cross_kept, (normed_one, scale_one, gain(0))
    )
    encoded_result = swap_positions(encoded_back.reshape(4, share, width), place)
    adapter_sum = grads[0].astype(F32)
    for part in sent:
        adapter_sum = adapter_sum + part.astype(F32)
    adapter_sum = lax.psum(adapter_sum.astype(BF16), "dp").astype(F32)
    in_total = adapter_sum[0].reshape(4 * extra, width).T
    out_total = adapter_sum[1].reshape(4 * extra, width)

    bias_parts = natural(bias_grad.reshape(-1))
    bias_line = jnp.zeros((4, 4 * extra), F32)
    for k in range(4):
        bias_line = lax.dynamic_update_index_in_dim(bias_line, bias_parts[k].reshape(-1), place ^ k, 0)
    bias_line = jnp.pad(bias_line.reshape(-1), (0, width - 16 * extra))
    small = jnp.stack(
        [
            sums_one[0],
            sums_two[0],
            sums_three[0],
            sums_one[1],
            sums_two[1],
            sums_three[1],
            sums_three[2],
            bias_line,
        ]
    )
    small = lax.psum(small, ("dp", "tensor"))
    bias_total = lax.dynamic_slice_in_dim(small[7], place * (4 * extra), 4 * extra, 0)

    (input_back,) = attention_back(self_low, self_kept, None)
    input_result = swap_positions(input_back.reshape(4, share, width), place)
    return (
        result,
        input_result,
        encoded_result,
        in_total,
        out_total,
        bias_total,
        small[6],
        small[0:3],
        small[3:6],
    )


def gelu_tanh(values):
    return jax.nn.gelu(values, approximate=True)


def multiply(left, right):
    return jnp.dot(left, right, preferred_element_type=jnp.float32)


def multiply_by_transpose(left, right):
    return lax.dot_general(
        left, right, (((1,), (1,)), ((), ())), preferred_element_type=jnp.float32
    )


def multiply_transposed_left(left, right):
    return lax.dot_general(
        left, right, (((0,), (0,)), ((), ())), preferred_element_type=jnp.float32
    )


def layer_norm(values, gain, shift):
    center = values - jnp.mean(values, axis=-1, keepdims=True)
    scale = lax.rsqrt(jnp.mean(center * center, axis=-1, keepdims=True) + 1e-05)
    normed = center * scale
    return (normed * gain + shift, normed, scale)


def norm_back(grad, normed, scale, gain):
    inner = grad * gain
    middle = jnp.mean(inner, axis=-1, keepdims=True)
    along = jnp.mean(inner * normed, axis=-1, keepdims=True)
    return (
        scale * (inner - middle - normed * along),
        jnp.sum(grad * normed, axis=(0, 1)),
        jnp.sum(grad, axis=(0, 1)),
    )


def attend(query_low, key_low, value_low, keep_for):
    count = query_low.shape[1]
    block = min(512, count)
    factor = query_low.shape[-1] ** (-0.5)
    contexts = []
    totals = []
    for first in range(0, count, block):
        scores = (
            jnp.einsum(
                "sqhe,skhe->shqk",
                query_low[:, first : first + block],
                key_low,
                preferred_element_type=jnp.float32,
            )
            * factor
        )
        scores = jnp.where(keep_for(first, block), scores, -1000000000.0)
        top_score = jnp.max(scores, axis=-1, keepdims=True)
        weights = jnp.exp(scores - top_score)
        denom = jnp.sum(weights, axis=-1, keepdims=True)
        probs_low = (weights / denom).astype(jnp.bfloat16)
        contexts.append(
            jnp.einsum("shqk,skhe->sqhe", probs_low, value_low, preferred_element_type=jnp.float32)
        )
        totals.append(top_score + jnp.log(denom))
    return (jnp.concatenate(contexts, axis=1), jnp.concatenate(totals, axis=2))


def attend_back(query_low, key_low, value_low, grad_low, totals, keep_for):
    count = query_low.shape[1]
    block = min(512, count)
    factor = query_low.shape[-1] ** (-0.5)
    key_grad = jnp.zeros(key_low.shape, jnp.float32)
    value_grad = jnp.zeros(value_low.shape, jnp.float32)
    query_grads = []
    for first in range(0, count, block):
        query_part = query_low[:, first : first + block]
        grad_part = grad_low[:, first : first + block]
        scores = (
            jnp.einsum("sqhe,skhe->shqk", query_part, key_low, preferred_element_type=jnp.float32)
            * factor
        )
        scores = jnp.where(keep_for(first, block), scores, -1000000000.0)
        probs = jnp.exp(scores - totals[:, :, first : first + block])
        probs_low = probs.astype(jnp.bfloat16)
        prob_grad = jnp.einsum(
            "sqhe,skhe->shqk", grad_part, value_low, preferred_element_type=jnp.float32
        )
        value_grad = value_grad + jnp.einsum(
            "shqk,sqhe->skhe", probs_low, grad_part, preferred_element_type=jnp.float32
        )
        along = jnp.sum(prob_grad * probs, axis=-1, keepdims=True)
        score_grad = (probs * (prob_grad - along)).astype(jnp.bfloat16)
        query_grads.append(
            jnp.einsum("shqk,skhe->sqhe", score_grad, key_low, preferred_element_type=jnp.float32)
            * factor
        )
        key_grad = (
            key_grad
            + jnp.einsum(
                "shqk,sqhe->skhe", score_grad, query_part, preferred_element_type=jnp.float32
            )
            * factor
        )
    return (jnp.concatenate(query_grads, axis=1), key_grad, value_grad)


def local(
    inputs,
    encoded,
    source_lengths,
    query_weight,
    key_weight,
    value_weight,
    output_weight,
    cross_query,
    cross_key,
    cross_value,
    cross_output,
    up_weight,
    down_weight,
    adapter_in,
    adapter_out,
    adapter_bias,
    adapter_shift,
    norm_gains,
    norm_shifts,
    output_grad,
):
    parts = lax.axis_size("tensor")
    place = lax.axis_index("tensor")
    sequences, share, width = inputs.shape
    length = share * parts
    rows = sequences * length
    heads = query_weight.shape[1] // HEAD
    local_width = heads * HEAD
    whole_inputs, whole_encoded = (
        lax.all_gather(inputs, "tensor", axis=1, tiled=True),
        lax.all_gather(encoded, "tensor", axis=1, tiled=True),
    )
    sources = whole_encoded.shape[1]
    flat_inputs = whole_inputs.reshape(rows, width)
    flat_encoded = whole_encoded.reshape(sequences * sources, width)

    def split_heads(values, count):
        return values.astype(jnp.bfloat16).reshape(sequences, count, heads, HEAD)

    def causal(first, block):
        query_pos = first + lax.broadcasted_iota(jnp.int32, (block, length), 0)
        key_pos = lax.broadcasted_iota(jnp.int32, (block, length), 1)
        return (key_pos <= query_pos)[None, None]

    def padded(first, block):
        key_pos = lax.broadcasted_iota(jnp.int32, (sequences, 1, 1, sources), 3)
        return key_pos < source_lengths[:, None, None, None]

    self_query = split_heads(multiply(flat_inputs, query_weight), length)
    self_key = split_heads(multiply(flat_inputs, key_weight), length)
    self_value = split_heads(multiply(flat_inputs, value_weight), length)
    self_context, self_totals = attend(self_query, self_key, self_value, causal)
    self_context_low = self_context.astype(jnp.bfloat16).reshape(rows, local_width)
    self_partial = multiply(self_context_low, output_weight).reshape(sequences, length, width)
    self_full = lax.psum(self_partial.astype(jnp.bfloat16), "tensor").astype(jnp.float32)
    first_full, normed_full, scale_full = layer_norm(
        whole_inputs.astype(jnp.float32) + self_full, norm_gains[0], norm_shifts[0]
    )
    first_low = first_full.astype(jnp.bfloat16)
    first_share = lax.dynamic_slice_in_dim(first_full, place * share, share, 1)
    normed_one = lax.dynamic_slice_in_dim(normed_full, place * share, share, 1)
    scale_one = lax.dynamic_slice_in_dim(scale_full, place * share, share, 1)
    flat_first = first_low.reshape(rows, width)
    cross_q = split_heads(multiply(flat_first, cross_query), length)
    cross_k = split_heads(multiply(flat_encoded, cross_key), sources)
    cross_v = split_heads(multiply(flat_encoded, cross_value), sources)
    cross_context, cross_totals = attend(cross_q, cross_k, cross_v, padded)
    cross_context_low = cross_context.astype(jnp.bfloat16).reshape(rows, local_width)
    cross_partial = multiply(cross_context_low, cross_output).reshape(sequences, length, width)
    cross_share = lax.psum_scatter(
        cross_partial.astype(jnp.bfloat16), "tensor", scatter_dimension=1, tiled=True
    ).astype(jnp.float32)
    second_share, normed_two, scale_two = layer_norm(
        first_share + cross_share, norm_gains[1], norm_shifts[1]
    )
    second_low = lax.all_gather(second_share.astype(jnp.bfloat16), "tensor", axis=1, tiled=True)
    flat_second = second_low.reshape(rows, width)
    hidden = multiply(flat_second, up_weight)
    hidden_low = gelu_tanh(hidden).astype(jnp.bfloat16)
    adapted = multiply(flat_second, adapter_in) + adapter_bias
    adapted_low = gelu_tanh(adapted).astype(jnp.bfloat16)
    branch_partial = multiply(hidden_low, down_weight) + 4.0 * multiply(adapted_low, adapter_out)
    branch_share = lax.psum_scatter(
        branch_partial.reshape(sequences, length, width).astype(jnp.bfloat16),
        "tensor",
        scatter_dimension=1,
        tiled=True,
    ).astype(jnp.float32)
    third_input = second_share + branch_share + 4.0 * adapter_shift
    outcome, normed_three, scale_three = layer_norm(third_input, norm_gains[2], norm_shifts[2])
    grad_three, gain_grad_three, shift_grad_three = norm_back(
        output_grad.astype(jnp.float32), normed_three, scale_three, norm_gains[2]
    )
    shift_grad_adapter = 4.0 * jnp.sum(grad_three, axis=(0, 1))
    branch_grad = lax.all_gather(
        grad_three.astype(jnp.bfloat16), "tensor", axis=1, tiled=True
    ).reshape(rows, width)
    hidden_grad = multiply_by_transpose(branch_grad, down_weight)
    hidden_unused, hidden_pull = jax.vjp(gelu_tanh, hidden)
    hidden_grad_low = hidden_pull(hidden_grad)[0].astype(jnp.bfloat16)
    adapted_grad = 4.0 * multiply_by_transpose(branch_grad, adapter_out)
    adapted_unused, adapted_pull = jax.vjp(gelu_tanh, adapted)
    adapted_grad = adapted_pull(adapted_grad)[0]
    bias_grad = jnp.sum(adapted_grad, axis=0)
    adapted_grad_low = adapted_grad.astype(jnp.bfloat16)
    in_grad = multiply_transposed_left(flat_second, adapted_grad_low)
    out_grad = 4.0 * multiply_transposed_left(adapted_low, branch_grad)
    second_partial = multiply_by_transpose(hidden_grad_low, up_weight) + multiply_by_transpose(
        adapted_grad_low, adapter_in
    )
    second_grad = grad_three + lax.psum_scatter(
        second_partial.reshape(sequences, length, width).astype(jnp.bfloat16),
        "tensor",
        scatter_dimension=1,
        tiled=True,
    ).astype(jnp.float32)
    grad_two, gain_grad_two, shift_grad_two = norm_back(
        second_grad, normed_two, scale_two, norm_gains[1]
    )
    cross_grad = lax.all_gather(
        grad_two.astype(jnp.bfloat16), "tensor", axis=1, tiled=True
    ).reshape(rows, width)
    cross_context_grad = multiply_by_transpose(cross_grad, cross_output).astype(jnp.bfloat16)
    cross_context_grad = cross_context_grad.reshape(sequences, length, heads, HEAD)
    cq_grad, ck_grad, cv_grad = attend_back(
        cross_q, cross_k, cross_v, cross_context_grad, cross_totals, padded
    )
    first_partial = multiply_by_transpose(
        cq_grad.astype(jnp.bfloat16).reshape(rows, local_width), cross_query
    )
    encoded_partial = multiply_by_transpose(
        ck_grad.astype(jnp.bfloat16).reshape(sequences * sources, local_width), cross_key
    ) + multiply_by_transpose(
        cv_grad.astype(jnp.bfloat16).reshape(sequences * sources, local_width), cross_value
    )
    first_back, encoded_share = (
        lax.psum_scatter(
            first_partial.reshape(sequences, length, width).astype(jnp.bfloat16),
            "tensor",
            scatter_dimension=1,
            tiled=True,
        ).astype(jnp.float32),
        lax.psum_scatter(
            encoded_partial.reshape(sequences, sources, width).astype(jnp.bfloat16),
            "tensor",
            scatter_dimension=1,
            tiled=True,
        ).astype(jnp.float32),
    )
    grad_one, gain_grad_one, shift_grad_one = norm_back(
        grad_two + first_back, normed_one, scale_one, norm_gains[0]
    )
    self_grad = lax.all_gather(grad_one.astype(jnp.bfloat16), "tensor", axis=1, tiled=True).reshape(
        rows, width
    )
    self_context_grad = multiply_by_transpose(self_grad, output_weight).astype(jnp.bfloat16)
    self_context_grad = self_context_grad.reshape(sequences, length, heads, HEAD)
    sq_grad, sk_grad, sv_grad = attend_back(
        self_query, self_key, self_value, self_context_grad, self_totals, causal
    )
    input_partial = (
        multiply_by_transpose(sq_grad.astype(jnp.bfloat16).reshape(rows, local_width), query_weight)
        + multiply_by_transpose(sk_grad.astype(jnp.bfloat16).reshape(rows, local_width), key_weight)
        + multiply_by_transpose(
            sv_grad.astype(jnp.bfloat16).reshape(rows, local_width), value_weight
        )
    )
    small_grads = jnp.stack(
        [
            gain_grad_one,
            gain_grad_two,
            gain_grad_three,
            shift_grad_one,
            shift_grad_two,
            shift_grad_three,
            shift_grad_adapter,
        ]
    )
    spread = jnp.broadcast_to(small_grads[:, None, :], (7, parts, width))
    input_back, small_back = (
        lax.psum_scatter(
            input_partial.reshape(sequences, length, width).astype(jnp.bfloat16),
            "tensor",
            scatter_dimension=1,
            tiled=True,
        ).astype(jnp.float32),
        lax.psum_scatter(
            spread.astype(jnp.bfloat16), "tensor", scatter_dimension=1, tiled=True
        ).astype(jnp.float32),
    )
    input_result = (grad_one + input_back).astype(jnp.bfloat16)
    encoded_result = encoded_share.astype(jnp.bfloat16)
    in_total, out_total, bias_total, small_total = (
        lax.psum(in_grad.astype(jnp.bfloat16), "dp").astype(jnp.float32),
        lax.psum(out_grad.astype(jnp.bfloat16), "dp").astype(jnp.float32),
        lax.psum(bias_grad.astype(jnp.bfloat16), "dp").astype(jnp.float32),
        lax.psum(small_back[:, 0].astype(jnp.bfloat16), "dp").astype(jnp.float32),
    )
    return (
        outcome.astype(jnp.bfloat16),
        input_result,
        encoded_result,
        in_total,
        out_total,
        bias_total,
        small_total[6],
        small_total[0:3],
        small_total[3:6],
    )


def solution(mesh):
    placed = (
        P("dp", "tensor", None),
        P("dp", "tensor", None),
        P("dp"),
        P(None, "tensor"),
        P(None, "tensor"),
        P(None, "tensor"),
        P("tensor", None),
        P(None, "tensor"),
        P(None, "tensor"),
        P(None, "tensor"),
        P("tensor", None),
        P(None, "tensor"),
        P("tensor", None),
        P(None, "tensor"),
        P("tensor", None),
        P("tensor"),
        P(),
        P(),
        P(),
        P("dp", "tensor", None),
    )
    suits = mesh.shape["tensor"] == 4 and mesh.shape["dp"] % 4 == 0

    def layer(*arrays):
        if suits and arrays[0].shape[:2] == (4, ROWS) and arrays[1].shape[:2] == (4, ROWS):
            return whole_sequences(*arrays)
        return local(*arrays)

    return jax.shard_map(
        layer,
        mesh=mesh,
        in_specs=placed,
        out_specs=(
            P("dp", "tensor", None),
            P("dp", "tensor", None),
            P("dp", "tensor", None),
            P(None, "tensor"),
            P("tensor", None),
            P("tensor"),
            P(),
            P(),
            P(),
        ),
        check_vma=False,
    )
```

```python
import functools
import jax
import jax.numpy as jnp
from jax import lax
from jax.experimental import pallas as pl
from jax.experimental.pallas import tpu as pltpu
from jax.sharding import PartitionSpec as P

HEAD = 64
F32 = jnp.float32
BF16 = jnp.bfloat16
LOG2E = 1.4426950408889634
LN2 = 0.6931471805599453
VMEM_LIMIT = 60 * 2**20
ROWS = 256
BLOCK = 256
ANY = pl.BlockSpec(memory_space=pl.ANY)
SMEM = pl.BlockSpec(memory_space=pltpu.SMEM)


def cost(flops, moved):
    return pl.CostEstimate(flops=int(flops * SHARE), bytes_accessed=int(moved * SHARE), transcendentals=0)


SHARE = 1.0


def nn(left, right):
    return lax.dot_general(left, right, (((1,), (0,)), ((), ())), preferred_element_type=F32)


def nt(left, right):
    return lax.dot_general(left, right, (((1,), (1,)), ((), ())), preferred_element_type=F32)


def tn(left, right):
    return lax.dot_general(left, right, (((0,), (0,)), ((), ())), preferred_element_type=F32)


def norm_rows(values):
    center = values - jnp.mean(values, axis=-1, keepdims=True)
    scale = lax.rsqrt(jnp.mean(center * center, axis=-1, keepdims=True) + 1e-05)
    return center * scale, scale


def norm_back_rows(grad, normed, scale, gain):
    inner = grad * gain
    middle = jnp.mean(inner, axis=-1, keepdims=True)
    along = jnp.mean(inner * normed, axis=-1, keepdims=True)
    return scale * (inner - middle - normed * along)


def gelu_and_slope(v):
    root = 0.7978845608028654
    square = v * v
    t = jnp.tanh(v * (root + (root * 0.044715) * square))
    half = 0.5 + 0.5 * t
    slope = half + (v * half) * (1.0 - t) * (root + (3.0 * root * 0.044715) * square)
    return v * half, slope


def head_rows(h):
    return slice(h * HEAD, (h + 1) * HEAD)


def natural(turn, p):
    slot, t = p // 4, p % 4
    return t ^ turn if slot == 3 else t


def sum_rows(values):
    return jnp.sum(values, axis=0, keepdims=True)


def pack_heads_kernel(ids_ref, q_ref, k_ref, v_ref, o_ref, own_ref, piece_ref, *half_refs):
    part = own_ref.shape[2]
    turn = ids_ref[1]
    for m, ref in enumerate((q_ref, k_ref, v_ref, o_ref)):
        values = ref[...] if m == 3 else ref[...].T
        for t in range(4):
            own_ref[t, m] = values[t * part : (t + 1) * part]
    piece_ref[0] = own_ref[turn]
    for half_ref in half_refs:
        for t in range(2):
            half_ref[t] = own_ref[2 * (turn // 2) + t]


def pack_units_kernel(ids_ref, up_ref, down_ref, ain_ref, aout_ref, bias_ref, own_ref, piece_ref):
    units, extra = down_ref.shape[0] // 4, aout_ref.shape[0] // 4
    turn = ids_ref[1]
    turned = ain_ref[...].T
    bias = bias_ref[...]
    begin = 2 * units + 2 * extra
    for t in range(4):
        cols = slice(t * units, (t + 1) * units)
        own_ref[t, :units] = up_ref[:, cols].T
        own_ref[t, units : 2 * units] = down_ref[cols, :]
        own_ref[t, 2 * units : 2 * units + extra] = turned[t * extra : (t + 1) * extra]
        own_ref[t, 2 * units + extra : begin] = aout_ref[t * extra : (t + 1) * extra, :]
        own_ref[t, begin:, : 4 * extra] = split_lines(bias)
    piece_ref[0] = own_ref[turn]


def split_lines(values):
    rows, rest = [], values
    for _ in range(3):
        low = rest.astype(BF16)
        rows.append(low)
        rest = rest - low.astype(F32)
    rows.append(jnp.zeros((13,) + values.shape[1:], BF16))
    return jnp.concatenate(rows, axis=0)


def pack(kernel, name, ids, own_shape, parts, *weights):
    vmem = pl.BlockSpec(memory_space=pltpu.VMEM)
    return pl.pallas_call(
        kernel,
        in_specs=[SMEM] + [vmem] * len(weights),
        out_specs=[vmem] * len(parts),
        out_shape=[jax.ShapeDtypeStruct((n,) + own_shape, BF16) for n in parts],
        compiler_params=pltpu.CompilerParams(vmem_limit_bytes=VMEM_LIMIT),
        cost_estimate=cost(0, 8 * 2**20),
        name=name,
    )(ids, *weights)


def attend_kernel(causal, count, first, homes, ids_ref, *refs):
    refs = list(refs)
    xq_hbm = refs.pop(0)
    xkv_hbm = xq_hbm if causal else refs.pop(0)
    sources_of = [refs.pop(0) for _ in range(len(set(n for n, _ in homes)))]
    if not first:
        refs = refs[4:]
    e_ref, hd_ref, il_ref, ctx_ref, xq, xkv, weights, qkv, x_sems, w_sems = refs
    if causal:
        xkv = xq
    step = pl.program_id(0)
    span, sources = xq.shape[0], xkv.shape[0]
    part = weights.shape[2] // 4

    def weight_copy(s, t):
        n, index = homes[4 * s + t]
        return pltpu.make_async_copy(
            sources_of[n].at[index, pl.ds(0, 3)],
            weights.at[s, :, pl.ds(t * part, part), :],
            w_sems.at[4 * s + t],
        )

    x_copies = [pltpu.make_async_copy(xq_hbm, xq, x_sems.at[0])]
    if not causal:
        x_copies.append(pltpu.make_async_copy(xkv_hbm, xkv, x_sems.at[1]))

    @pl.when(step == 0)
    def _():
        for t in range(4):
            weight_copy(0, t).start()
        for copy in x_copies:
            copy.start()
        for s in range(1, count):
            for t in range(4):
                weight_copy(s, t).start()
        for copy in x_copies:
            copy.wait()

    for s in range(count):

        @pl.when(step == 2 * s)
        def _():
            for t in range(4):
                weight_copy(s, t).wait()
            qkv[0] = (nt(weights[s, 0], xq[...]) * (LOG2E * HEAD**-0.5)).astype(BF16)
            qkv[1] = nt(weights[s, 1], xkv[...]).astype(BF16)
            qkv[2] = nt(weights[s, 2], xkv[...]).astype(BF16)

    pair = pl.ds(pl.multiple_of((step % 2) * 128, 128), 128)
    q2, k2, v2 = qkv[0, pair, :], qkv[1, pair, :], qkv[2, pair, :]
    hd_ref[0], hd_ref[1], hd_ref[2] = q2, k2, v2
    block = min(BLOCK, span)
    work = [(i, h) for i in range(span // block) for h in range(2)]

    def reach(i):
        return (i + 1) * block if causal else sources

    def score(i, h):
        return tn(k2[head_rows(h), : reach(i)], q2[head_rows(h), i * block : (i + 1) * block])

    ahead = 2 if causal else 4
    waiting = [score(i, h) for i, h in work[:ahead]]
    for number, (i, h) in enumerate(work):
        n, cols = reach(i), slice(i * block, (i + 1) * block)
        s = waiting.pop(0)
        if number + ahead < len(work):
            waiting.append(score(*work[number + ahead]))
        if causal:
            key = lax.broadcasted_iota(jnp.int32, (block, block), 0)
            query = lax.broadcasted_iota(jnp.int32, (block, block), 1)
            tail = jnp.where(key <= query, s[n - block :], -1e9)
            s = jnp.concatenate([s[: n - block], tail], axis=0) if n > block else tail
        else:
            key = lax.broadcasted_iota(jnp.int32, (n, block), 0)
            s = jnp.where(key < ids_ref[2], s, -1e9)
        e = jnp.exp2(s - jnp.max(s, axis=0, keepdims=True))
        inverse = 1.0 / jnp.sum(e, axis=0, keepdims=True)
        low = e.astype(BF16)
        e_ref[h, :n, cols] = low
        il_ref[h, :, cols] = inverse
        context = (nn(v2[head_rows(h), :n], low) * inverse).astype(BF16)
        hd_ref[3, head_rows(h), cols] = context
        contexts = [context] if h == 0 else contexts + [context]
        if h == 1:
            ctx_ref[cols, :] = jnp.concatenate(contexts, axis=0).T


def gather_homes(pieces):
    arrays, homes = [], []
    for array, index in pieces:
        where = [n for n, known in enumerate(arrays) if known is array]
        if not where:
            arrays.append(array)
            where = [len(arrays) - 1]
        homes.append((where[0], index))
    return arrays, tuple(homes)


def attend_slots(ids, slots, xq, xkv, pieces, before):
    causal = xkv is None
    span, width = xq.shape
    sources = span if causal else xkv.shape[0]
    heads = width // HEAD
    count, base = len(slots), 2 * slots[0]
    arrays, homes = gather_homes([pieces[4 * s + t] for s in slots for t in range(4)])
    part = arrays[0].shape[2]
    first = before is None
    operands = [ids, xq] + ([] if causal else [xkv]) + arrays
    specs = [SMEM] + [ANY] * (len(operands) - 1)
    aliases = {}
    if not first:
        aliases = {len(operands) + n: n for n in range(4)}
        operands += list(before)
        specs += [ANY] * 4
    return pl.pallas_call(
        functools.partial(attend_kernel, causal, count, first, homes),
        grid=(2 * count,),
        in_specs=specs,
        out_specs=(
            pl.BlockSpec((2, sources, span), lambda j: (base + j, 0, 0)),
            pl.BlockSpec((4, 128, span), lambda j: (0, base + j, 0)),
            pl.BlockSpec((2, 1, span), lambda j: (base + j, 0, 0)),
            pl.BlockSpec((span, 128), lambda j: (0, base + j)),
        ),
        out_shape=(
            jax.ShapeDtypeStruct((heads, sources, span), BF16),
            jax.ShapeDtypeStruct((4, width, span), BF16),
            jax.ShapeDtypeStruct((heads, 1, span), F32),
            jax.ShapeDtypeStruct((span, width), BF16),
        ),
        scratch_shapes=[
            pltpu.VMEM((span, width), BF16),
            pltpu.VMEM((16, 128) if causal else (sources, width), BF16),
            pltpu.VMEM((count, 3, 4 * part, width), BF16),
            pltpu.VMEM((3, 4 * part, max(span, sources)), BF16),
            pltpu.SemaphoreType.DMA((2,)),
            pltpu.SemaphoreType.DMA((4 * count,)),
        ],
        input_output_aliases=aliases,
        compiler_params=pltpu.CompilerParams(vmem_limit_bytes=VMEM_LIMIT),
        cost_estimate=cost(count * 10 * 10**9, count * 12 * 2**20),
        name="self_attend" if causal else "cross_attend",
    )(*operands)


def out_norm_kernel(homes, *refs):
    refs = list(refs)
    ctx_ref, x_ref, gain_ref, shift_ref = refs[:4]
    sources = refs[4:-5]
    low_ref, n_ref, r_ref, wo, sems = refs[-5:]
    part = wo.shape[0] // len(homes)
    copies = [
        pltpu.make_async_copy(sources[n].at[index, 3], wo.at[pl.ds(p * part, part), :], sems.at[p])
        for p, (n, index) in enumerate(homes)
    ]

    @pl.when(pl.program_id(0) == 0)
    def _():
        for copy in copies:
            copy.start()
        for copy in copies:
            copy.wait()

    rows_here = ctx_ref.shape[0]
    for i in range(rows_here // ROWS):
        rows = slice(i * ROWS, (i + 1) * ROWS)
        total = nn(ctx_ref[rows, :], wo[...]) + x_ref[rows, :].astype(F32)
        normed, scale = norm_rows(total)
        low_ref[rows, :] = (normed * gain_ref[...] + shift_ref[...]).astype(BF16)
        n_ref[rows, :] = normed.astype(BF16)
        r_ref[rows, :] = scale


def out_norm(ctx, pieces, residual, gain, shift):
    span, width = ctx.shape
    arrays, homes = gather_homes(pieces)
    block = min(512, span)
    rows = lambda w: pl.BlockSpec((block, w), lambda i: (i, 0))
    line = pl.BlockSpec((1, width), lambda i: (0, 0))
    return pl.pallas_call(
        functools.partial(out_norm_kernel, homes),
        grid=(span // block,),
        in_specs=[rows(width), rows(width), line, line] + [ANY] * len(arrays),
        out_specs=(rows(width), rows(width), rows(1)),
        out_shape=(
            jax.ShapeDtypeStruct((span, width), BF16),
            jax.ShapeDtypeStruct((span, width), BF16),
            jax.ShapeDtypeStruct((span, 1), F32),
        ),
        scratch_shapes=[pltpu.VMEM((width, width), BF16), pltpu.SemaphoreType.DMA((len(homes),))],
        compiler_params=pltpu.CompilerParams(vmem_limit_bytes=VMEM_LIMIT),
        cost_estimate=cost(2 * span * width * width, 10 * 2**20),
        name="out_norm",
    )(ctx, residual, gain, shift, *arrays)


def feed_kernel(slots, first, last, units, extra, homes, ids_ref, *refs):
    count = len(slots)
    refs = list(refs)
    x_ref = refs.pop(0)
    sources = [refs.pop(0) for _ in range(len(set(n for n, _ in homes)))]
    if last:
        shift_a_ref, gain_ref, shift_ref, grad_ref = [refs.pop(0) for _ in range(4)]
    if not first:
        acc_hbm = refs.pop(0)
        refs = refs[3:]
    gp_ref, gpa_ref, alow_ref = [refs.pop(0) for _ in range(3)]
    if last:
        out_ref, low_ref, sum_ref = [refs.pop(0) for _ in range(3)]
    acc, up, down, ain, aout, bias, w_sems, b_sems, acc_sem = refs
    step = pl.program_id(0)
    span = x_ref.shape[0]

    def piece_copies(p):
        n, index = homes[p]
        there = 4 * (p // 4) + natural(ids_ref[1], 4 * slots[0] + p)
        parts = (
            (0, units, up, p),
            (units, units, down, p),
            (2 * units, extra, ain, there),
            (2 * units + extra, extra, aout, there),
        )
        found = [
            pltpu.make_async_copy(
                sources[n].at[index, pl.ds(begin, size), :],
                held.at[pl.ds(to * size, size), :],
                w_sems.at[p, m],
            )
            for m, (begin, size, held, to) in enumerate(parts)
        ]
        if p % 4 == 0:
            found.append(
                pltpu.make_async_copy(
                    sources[n].at[index, pl.ds(2 * units + 2 * extra, 16), pl.ds(0, 4 * extra)],
                    bias.at[p // 4],
                    b_sems.at[p // 4],
                )
            )
        return found

    def acc_copy():
        return pltpu.make_async_copy(acc_hbm, acc, acc_sem)

    @pl.when(step == 0)
    def _():
        for p in range(4 * count):
            for copy in piece_copies(p):
                copy.start()
        if first:
            acc[...] = jnp.zeros_like(acc)
        else:
            acc_copy().start()
            acc_copy().wait()

    for s in range(count):

        @pl.when(step == 2 * s)
        def _():
            for p in range(4 * s, 4 * s + 4):
                for copy in piece_copies(p):
                    copy.wait()
            rows = slice(4 * extra * s, 4 * extra * (s + 1))
            a, slope = gelu_and_slope(nt(x_ref[...], ain[rows, :]) + sum_rows(bias[s].astype(F32)))
            a_low = a.astype(BF16)
            alow_ref[...] = a_low
            gpa_ref[...] = slope.astype(BF16)
            acc[...] += 4.0 * nn(a_low, aout[rows, :])

    chunk = pl.ds(pl.multiple_of(step * (2 * units), 2 * units), 2 * units)
    half = min(512, span)
    for i in range(span // half):
        rows = slice(i * half, (i + 1) * half)
        h, slope = gelu_and_slope(nt(x_ref[rows, :], up[chunk, :]))
        gp_ref[rows, :] = slope.astype(BF16)
        acc[rows, :] += nn(h.astype(BF16), down[chunk, :])

    if last:

        @pl.when(step == pl.num_programs(0) - 1)
        def _():
            sum_ref[...] = jnp.zeros_like(sum_ref)
            for i in range(span // ROWS):
                rows = slice(i * ROWS, (i + 1) * ROWS)
                total = acc[rows, :] + x_ref[rows, :].astype(F32) + 4.0 * shift_a_ref[...]
                normed, scale = norm_rows(total)
                out_ref[rows, :] = (normed * gain_ref[...] + shift_ref[...]).astype(BF16)
                grad = grad_ref[rows, :].astype(F32)
                back = norm_back_rows(grad, normed, scale, gain_ref[...])
                low_ref[rows, :] = back.astype(BF16)
                sum_ref[0:1, :] += sum_rows(grad * normed)
                sum_ref[1:2, :] += sum_rows(grad)
                sum_ref[2:3, :] += 4.0 * sum_rows(back)


def feed_slots(ids, slots, x, pieces, before, norm, units, extra):
    span, width = x.shape
    first, last = before is None, norm is not None
    count = len(slots)
    whole = lambda a: pl.BlockSpec(a.shape, lambda j: (0,) * a.ndim, pipeline_mode=pl.Buffered(1))
    arrays, homes = gather_homes([pieces[4 * s + t] for s in slots for t in range(4)])
    operands = [ids, x] + arrays
    specs = [SMEM, whole(x)] + [ANY] * len(arrays)
    if last:
        operands += list(norm)
        specs += [whole(a) for a in norm]
    kept_shape = [
        jax.ShapeDtypeStruct((span, 16 * units), BF16),
        jax.ShapeDtypeStruct((span, 16 * extra), BF16),
        jax.ShapeDtypeStruct((span, 16 * extra), BF16),
    ]
    kept_specs = [
        pl.BlockSpec((span, 2 * units), lambda j: (0, 2 * slots[0] + j)),
        pl.BlockSpec((span, 4 * extra), lambda j: (0, slots[0] + j // 2)),
        pl.BlockSpec((span, 4 * extra), lambda j: (0, slots[0] + j // 2)),
    ]
    aliases = {}
    if not first:
        aliases = {len(operands) + 1 + n: n for n in range(3)}
        operands += list(before)
        specs += [ANY] * 4
    total = jax.ShapeDtypeStruct((span, width), F32)
    once = lambda s: pl.BlockSpec(s.shape, lambda j: (0,) * len(s.shape), pipeline_mode=pl.Buffered(1))
    if last:
        low = jax.ShapeDtypeStruct((span, width), BF16)
        more = [low, low, jax.ShapeDtypeStruct((8, width), F32)]
        scratch = [pltpu.VMEM((span, width), F32)]
    else:
        more, scratch = [total], []
    outs = pl.pallas_call(
        functools.partial(feed_kernel, slots, first, last, units, extra, homes),
        grid=(2 * count,),
        in_specs=specs,
        out_specs=kept_specs + [once(s) for s in more],
        out_shape=kept_shape + more,
        scratch_shapes=scratch
        + [
            pltpu.VMEM((count * 4 * units, width), BF16),
            pltpu.VMEM((count * 4 * units, width), BF16),
            pltpu.VMEM((count * 4 * extra, width), BF16),
            pltpu.VMEM((count * 4 * extra, width), BF16),
            pltpu.VMEM((count, 16, 4 * extra), BF16),
            pltpu.SemaphoreType.DMA((4 * count, 4)),
            pltpu.SemaphoreType.DMA((count,)),
            pltpu.SemaphoreType.DMA,
        ],
        input_output_aliases=aliases,
        compiler_params=pltpu.CompilerParams(vmem_limit_bytes=VMEM_LIMIT),
        cost_estimate=cost(count * 6 * 10**9, count * 14 * 2**20),
        name="feed",
    )(*operands)
    kept, rest = list(outs[:3]), list(outs[3:])
    return kept, rest


def adapter_back_kernel(extra, units, homes, ids_ref, *refs):
    refs = list(refs)
    g_ref, x_ref, gpa_ref, alow_ref = refs[:4]
    low_ref, *slot_refs, aout, sems = refs[-7:]
    sources = refs[4:-7]
    begin = 2 * units + extra
    copies = []
    for p, (n, index) in enumerate(homes):
        there = 4 * (p // 4) + natural(ids_ref[1], p)
        copies.append(
            pltpu.make_async_copy(
                sources[n].at[index, pl.ds(begin, extra), :],
                aout.at[pl.ds(there * extra, extra), :],
                sems.at[p],
            )
        )
    for copy in copies:
        copy.start()
    for copy in copies:
        copy.wait()
    g = g_ref[...]
    a = 4.0 * nt(g, aout[...]) * gpa_ref[...].astype(F32)
    bias = sum_rows(a)
    a_low = a.astype(BF16)
    low_ref[...] = a_low
    in_grad = tn(a_low, x_ref[...]).astype(BF16)
    out_grad = (4.0 * tn(alow_ref[...], g)).astype(BF16)
    size = 4 * extra
    for k in range(4):
        rows = slice(k * size, (k + 1) * size)
        slot_refs[k][:size] = in_grad[rows]
        slot_refs[k][size : 2 * size] = out_grad[rows]
        slot_refs[k][2 * size :] = jnp.zeros((16, g.shape[1]), BF16)
        slot_refs[k][2 * size :, :size] = split_lines(bias[:, rows])


def adapter_back(ids, g, x, gpa, alow, pieces, units, extra):
    span, width = g.shape
    arrays, homes = gather_homes(pieces)
    vmem = pl.BlockSpec(memory_space=pltpu.VMEM)
    outs = pl.pallas_call(
        functools.partial(adapter_back_kernel, extra, units, homes),
        in_specs=[SMEM] + [vmem] * 4 + [ANY] * len(arrays),
        out_specs=[vmem] * 5,
        out_shape=[jax.ShapeDtypeStruct((span, 16 * extra), BF16)]
        + [jax.ShapeDtypeStruct((8 * extra + 16, width), BF16)] * 4,
        scratch_shapes=[pltpu.VMEM((16 * extra, width), BF16), pltpu.SemaphoreType.DMA((16,))],
        compiler_params=pltpu.CompilerParams(vmem_limit_bytes=VMEM_LIMIT),
        cost_estimate=cost(6 * span * width * 16 * extra, 12 * 2**20),
        name="adapter_back",
    )(ids, g, x, gpa, alow, *arrays)
    return outs[0], list(outs[1:])


def feed_back_kernel(units, extra, homes, ids_ref, *refs):
    refs = list(refs)
    g_ref, gp_ref, alow_ref, n_ref, r_ref, gain_ref = refs[:6]
    low_ref, sum_ref, acc, up, down, ain, w_sems, a_sems = refs[-8:]
    sources = refs[6:-8]
    step = pl.program_id(0)
    steps = len(homes) // 2
    span = g_ref.shape[0]

    def chunk_copies(j, home):
        copies = []
        for t in range(2):
            n, index = homes[2 * home + t]
            for m, held in enumerate((up, down)):
                copies.append(
                    pltpu.make_async_copy(
                        sources[n].at[index, pl.ds(m * units, units), :],
                        held.at[j % 2, pl.ds(t * units, units), :],
                        w_sems.at[j % 2, t, m],
                    )
                )
        return copies

    def ain_copies():
        return [
            pltpu.make_async_copy(
                sources[n].at[index, pl.ds(2 * units, extra), :],
                ain.at[pl.ds((4 * (p // 4) + natural(ids_ref[1], p)) * extra, extra), :],
                a_sems.at[p],
            )
            for p, (n, index) in enumerate(homes)
        ]

    @pl.when(step == 0)
    def _():
        for copy in ain_copies():
            copy.start()
        for copy in chunk_copies(0, 0):
            copy.start()
        for copy in ain_copies():
            copy.wait()
        acc[...] = nn(alow_ref[...], ain[...]) + g_ref[...].astype(F32)

    for j in range(1, steps):

        @pl.when(step == j - 1)
        def _():
            for copy in chunk_copies(j, j):
                copy.start()

    for copy in chunk_copies(step, 0):
        copy.wait()
    half = min(512, span)
    side = step % 2
    for i in range(span // half):
        rows = slice(i * half, (i + 1) * half)
        h = (nt(g_ref[rows, :], down[side]) * gp_ref[rows, :].astype(F32)).astype(BF16)
        acc[rows, :] += nn(h, up[side])

    @pl.when(step == pl.num_programs(0) - 1)
    def _():
        sum_ref[...] = jnp.zeros_like(sum_ref)
        for i in range(span // ROWS):
            rows = slice(i * ROWS, (i + 1) * ROWS)
            grad = acc[rows, :]
            normed = n_ref[rows, :].astype(F32)
            back = norm_back_rows(grad, normed, r_ref[rows, :], gain_ref[...])
            low_ref[rows, :] = back.astype(BF16)
            sum_ref[0:1, :] += sum_rows(grad * normed)
            sum_ref[1:2, :] += sum_rows(grad)


def feed_back(ids, g, slopes, a_low, pieces, normed, scale, gain, units, extra):
    span, width = g.shape
    arrays, homes = gather_homes(pieces)
    whole = lambda a: pl.BlockSpec(a.shape, lambda j: (0,) * a.ndim, pipeline_mode=pl.Buffered(1))
    out_shape = (jax.ShapeDtypeStruct((span, width), BF16), jax.ShapeDtypeStruct((8, width), F32))
    return pl.pallas_call(
        functools.partial(feed_back_kernel, units, extra, homes),
        grid=(8,),
        in_specs=[
            SMEM,
            whole(g),
            pl.BlockSpec((span, 2 * units), lambda j: (0, j)),
            whole(a_low),
            whole(normed),
            whole(scale),
            whole(gain),
        ]
        + [ANY] * len(arrays),
        out_specs=tuple(
            pl.BlockSpec(s.shape, lambda j: (0, 0), pipeline_mode=pl.Buffered(1)) for s in out_shape
        ),
        out_shape=out_shape,
        scratch_shapes=[
            pltpu.VMEM((span, width), F32),
            pltpu.VMEM((2, 2 * units, width), BF16),
            pltpu.VMEM((2, 2 * units, width), BF16),
            pltpu.VMEM((16 * extra, width), BF16),
            pltpu.SemaphoreType.DMA((2, 2, 2)),
            pltpu.SemaphoreType.DMA((16,)),
        ],
        compiler_params=pltpu.CompilerParams(vmem_limit_bytes=VMEM_LIMIT),
        cost_estimate=cost(20 * 10**9, 40 * 2**20),
        name="feed_back",
    )(ids, g, slopes, a_low, normed, scale, gain, *arrays)


def attention_back_kernel(causal, homes, *refs):
    refs = list(refs)
    g_ref, e_ref, hd_ref, il_ref = refs[:4]
    refs = refs[4:]
    if not causal:
        n_ref, r_ref, gain_ref = [refs.pop(0) for _ in range(3)]
    sources_of = [refs.pop(0) for _ in range(len(set(n for n, _ in homes)))]
    if causal:
        passed_hbm = refs.pop(0)
    out_ref = refs.pop(0)
    if causal:
        put_hbm = refs.pop(0)
    else:
        low_ref, sum_ref = [refs.pop(0) for _ in range(2)]
    wf, ct, dq, dk, dv, sems = refs[:6]
    step = pl.program_id(0)
    if causal:
        passing, pass_sems = refs[6:]
        bring = pltpu.make_async_copy(passed_hbm, passing, pass_sems.at[0])
        put = pltpu.make_async_copy(passing, put_hbm, pass_sems.at[1])

        @pl.when(step == 1)
        def _():
            bring.start()

        @pl.when(step == 3)
        def _():
            bring.wait()
            put.start()

        @pl.when(step == pl.num_programs(0) - 1)
        def _():
            put.wait()

    span = g_ref.shape[0]
    sources = e_ref.shape[1]
    part = wf.shape[1] // len(homes)

    def copies(wanted):
        found = []
        for p, (n, index) in enumerate(homes):
            begin, size = (3, 1) if wanted else (0, 3)
            found.append(
                pltpu.make_async_copy(
                    sources_of[n].at[index, pl.ds(begin, size)],
                    wf.at[pl.ds(begin, size), pl.ds(p * part, part), :],
                    sems.at[wanted, p],
                )
            )
        return found

    @pl.when(step == 0)
    def _():
        for copy in copies(1) + copies(0):
            copy.start()
        for copy in copies(1):
            copy.wait()
        ct[...] = nt(wf[3], g_ref[...]).astype(BF16)

    pair = pl.ds(pl.multiple_of(step * 128, 128), 128)
    c2 = ct[pair, :]
    block = min(BLOCK if causal else 512, span)
    scaled, dots = [], []
    for h in range(2):
        c = c2[head_rows(h), :].astype(F32) * il_ref[h]
        dots.append(jnp.sum(c * hd_ref[3, head_rows(h), :].astype(F32), axis=0, keepdims=True))
        scaled.append(c.astype(BF16))
    sums_k, sums_v = [None, None], [None, None]
    for i in reversed(range(span // block)):
        n = (i + 1) * block if causal else sources
        cols = slice(i * block, (i + 1) * block)
        grads = [tn(hd_ref[2, head_rows(h), :n], scaled[h][:, cols]) for h in range(2)]
        queries = []
        for h in range(2):
            e = e_ref[h, :n, cols]
            ds = (e.astype(F32) * (grads[h] - dots[h][:, cols])).astype(BF16)
            queries.append((nn(hd_ref[1, head_rows(h), :n], ds) * HEAD**-0.5).astype(BF16))
            gk = nn(ds, hd_ref[0, head_rows(h), cols].T)
            gv = nn(e, scaled[h][:, cols].T)
            if sums_k[h] is None:
                sums_k[h], sums_v[h] = gk, gv
            elif n == sums_k[h].shape[0]:
                sums_k[h], sums_v[h] = sums_k[h] + gk, sums_v[h] + gv
            else:
                sums_k[h] = jnp.concatenate([sums_k[h][:n] + gk, sums_k[h][n:]], axis=0)
                sums_v[h] = jnp.concatenate([sums_v[h][:n] + gv, sums_v[h][n:]], axis=0)
        dq[cols, pair] = jnp.concatenate(queries, axis=0).T
    dk[:, pair] = (jnp.concatenate(sums_k, axis=1) * LN2).astype(BF16)
    dv[:, pair] = jnp.concatenate(sums_v, axis=1).astype(BF16)

    @pl.when(step == pl.num_programs(0) - 1)
    def _():
        for copy in copies(0):
            copy.wait()
        for i in range(sources // ROWS):
            rows = slice(i * ROWS, (i + 1) * ROWS)
            total = nn(dk[rows, :], wf[1]) + nn(dv[rows, :], wf[2])
            if causal:
                total = total + nn(dq[rows, :], wf[0]) + g_ref[rows, :].astype(F32)
            out_ref[rows, :] = total.astype(BF16)
        if not causal:
            sum_ref[...] = jnp.zeros_like(sum_ref)
            for i in range(span // ROWS):
                rows = slice(i * ROWS, (i + 1) * ROWS)
                grad = nn(dq[rows, :], wf[0]) + g_ref[rows, :].astype(F32)
                normed = n_ref[rows, :].astype(F32)
                back = norm_back_rows(grad, normed, r_ref[rows, :], gain_ref[...])
                low_ref[rows, :] = back.astype(BF16)
                sum_ref[0:1, :] += sum_rows(grad * normed)
                sum_ref[1:2, :] += sum_rows(grad)


def attention_back(g, kept, pieces, norm, passed=None):
    e, hd, il, _ = kept
    causal = norm is None
    span, width = g.shape
    heads, sources, _ = e.shape
    arrays, homes = gather_homes(pieces)
    whole = lambda a: pl.BlockSpec(a.shape, lambda j: (0,) * a.ndim, pipeline_mode=pl.Buffered(1))
    operands = [g, e, hd, il]
    specs = [
        whole(g),
        pl.BlockSpec((2, sources, span), lambda j: (j, 0, 0)),
        pl.BlockSpec((4, 128, span), lambda j: (0, j, 0)),
        pl.BlockSpec((2, 1, span), lambda j: (j, 0, 0)),
    ]
    out_shape = [jax.ShapeDtypeStruct((sources, width), BF16)]
    if not causal:
        operands += list(norm)
        specs += [whole(a) for a in norm]
        out_shape += [jax.ShapeDtypeStruct((span, width), BF16), jax.ShapeDtypeStruct((8, width), F32)]
    out_specs = [pl.BlockSpec(s.shape, lambda j: (0, 0), pipeline_mode=pl.Buffered(1)) for s in out_shape]
    scratch = []
    if causal:
        arrays = arrays + [passed]
        out_shape.append(jax.ShapeDtypeStruct(passed.shape, passed.dtype))
        out_specs.append(ANY)
        scratch = [pltpu.VMEM(passed.shape, passed.dtype), pltpu.SemaphoreType.DMA((2,))]
    return pl.pallas_call(
        functools.partial(attention_back_kernel, causal, homes),
        grid=(heads // 2,),
        in_specs=specs + [ANY] * len(arrays),
        out_specs=out_specs,
        out_shape=out_shape,
        scratch_shapes=[
            pltpu.VMEM((4, width, width), BF16),
            pltpu.VMEM((width, span), BF16),
            pltpu.VMEM((span, width), BF16),
            pltpu.VMEM((sources, width), BF16),
            pltpu.VMEM((sources, width), BF16),
            pltpu.SemaphoreType.DMA((2, len(homes))),
        ]
        + scratch,
        compiler_params=pltpu.CompilerParams(vmem_limit_bytes=VMEM_LIMIT),
        cost_estimate=cost(40 * 10**9, 60 * 2**20),
        name="self_back" if causal else "cross_back",
    )(*operands, *arrays)


def copy_kernel(from_ref, to_ref):
    to_ref[...] = from_ref[...]


def copied(values):
    spec = pl.BlockSpec((1,) + values.shape[1:], lambda i: (i, 0, 0))
    return pl.pallas_call(
        copy_kernel,
        grid=(values.shape[0],),
        in_specs=[spec],
        out_specs=spec,
        out_shape=jax.ShapeDtypeStruct(values.shape, values.dtype),
        cost_estimate=cost(0, 4 * 2**20),
        name="copied",
    )(values)


def swap(values, name, bit):
    size = lax.axis_size(name)
    return lax.ppermute(values, name, [(i, i ^ bit) for i in range(size)])


def cross_swap(values, even, odd):
    size = lax.axis_size("tensor")
    pairs = []
    for d in range(lax.axis_size("dp")):
        for i in range(size):
            pairs.append((d * size + i, d * size + (i ^ (odd if d % 2 else even))))
    return lax.ppermute(values, ("dp", "tensor"), pairs)


def turn_over(values):
    return lax.all_to_all(values, "tensor", 0, 0, tiled=True)


def add_low(left, right):
    return (left.astype(F32) + right.astype(F32)).astype(BF16)


def after(values, *earlier):
    return lax.optimization_barrier((values, earlier))[0]


def send_near(what, half, piece):
    with jax.named_scope(what + "_near"):
        return cross_swap(half, 1, 2), swap(piece, "tensor", 3)


def all_pieces(*arrays):
    return [(array, t) for array in arrays for t in range(array.shape[0])]


def whole_sequences(
    inputs,
    encoded,
    source_lengths,
    query_weight,
    key_weight,
    value_weight,
    output_weight,
    cross_query,
    cross_key,
    cross_value,
    cross_output,
    up_weight,
    down_weight,
    adapter_in,
    adapter_out,
    adapter_bias,
    adapter_shift,
    norm_gains,
    norm_shifts,
    output_grad,
):
    place = lax.axis_index("tensor")
    turn = lax.axis_index("dp") % 4
    _, share, width = inputs.shape
    span = 4 * share
    units, extra = up_weight.shape[1] // 4, adapter_in.shape[1] // 4
    length = lax.dynamic_index_in_dim(source_lengths, place, 0, keepdims=False)
    ids = jnp.stack([place, turn, length]).astype(jnp.int32)
    gain = lambda j: norm_gains[j : j + 1]
    shift = lambda j: norm_shifts[j : j + 1]
    heads_shape = (4, output_weight.shape[0] // 4, width)
    units_shape = (2 * units + 2 * extra + 16, width)

    x = turn_over(inputs).reshape(span, width)
    self_own, self_piece, self_half = pack(
        pack_heads_kernel, "pack_self", ids, heads_shape, (4, 1, 2), query_weight, key_weight, value_weight, output_weight
    )
    self_near = send_near("self", self_half, self_piece)
    cross_own, cross_piece = pack(
        pack_heads_kernel,
        "pack_cross",
        after(ids, self_half),
        heads_shape,
        (4, 1),
        cross_query,
        cross_key,
        cross_value,
        cross_output,
    )
    feed_own, feed_piece = pack(
        pack_units_kernel,
        "pack_feed",
        after(ids, cross_piece),
        units_shape,
        (4, 1),
        up_weight,
        down_weight,
        adapter_in,
        adapter_out,
        adapter_bias.reshape(1, -1),
    )
    x = after(x, feed_piece)
    source = turn_over(after(encoded, x)).reshape(span, width)
    cross_near = send_near("cross", cross_own, cross_piece)
    self_kept = attend_slots(ids, (0,), x, None, all_pieces(self_own), None)

    half, piece = after(self_near, self_kept[0])
    with jax.named_scope("self_far"):
        far_half, far_piece = swap(half, "dp", 2), swap(piece, "dp", 2)
    with jax.named_scope("self_core"):
        core_half, core_piece = swap(half, "dp", 1), swap(piece, "dp", 1)
        core_far_half = swap(far_half, "dp", 1)
    shard = after(cross_near[0], far_half)
    self_pieces = all_pieces(self_own, half, far_half, core_half, core_far_half)
    self_kept = attend_slots(ids, (1, 2), after(x, piece, shard), None, self_pieces, self_kept)
    with jax.named_scope("self_core"):
        core_far_piece = swap(after(far_piece, self_kept[0]), "dp", 1)
    self_pieces += all_pieces(piece, core_piece, far_piece, core_far_piece)
    feed_near = send_near("feed", after(feed_own, self_kept[0]), after(feed_piece, self_kept[0]))
    shard, piece = after(shard, self_kept[0]), after(cross_near[1], self_kept[0])
    with jax.named_scope("cross_far"):
        far_piece = swap(piece, "dp", 2)
    with jax.named_scope("cross_core"):
        core_shard, core_piece = swap(shard, "dp", 1), swap(piece, "dp", 1)
    self_kept = attend_slots(ids, (3,), after(x, piece), None, self_pieces, self_kept)
    first, normed_one, scale_one = out_norm(self_kept[3], self_pieces, x, gain(0), shift(0))

    with jax.named_scope("cross_core"):
        core_far_piece = swap(after(far_piece, first), "dp", 1)
    cross_pieces = all_pieces(cross_own, shard)
    cross_kept = attend_slots(
        ids, (0, 1), after(first, core_shard, core_piece, core_far_piece), source, cross_pieces, None
    )
    cross_pieces += all_pieces(core_shard, piece, core_piece, far_piece, core_far_piece)
    cross_kept = attend_slots(ids, (2, 3), first, source, cross_pieces, cross_kept)
    shard = after(feed_near[0], cross_kept[0])
    grad = turn_over(after(output_grad, cross_kept[0])).reshape(span, width)
    second, normed_two, scale_two = out_norm(
        cross_kept[3], cross_pieces, after(first, shard), gain(1), shift(1)
    )

    with jax.named_scope("feed_core"):
        core_shard = swap(after(shard, cross_kept[0]), "dp", 1)
    kept, rest = feed_slots(
        ids, (0,), after(second, core_shard), all_pieces(feed_own), None, None, units, extra
    )
    piece = after(feed_near[1], rest[0])
    with jax.named_scope("feed_far"):
        far_piece = swap(piece, "dp", 2)
    with jax.named_scope("feed_core"):
        core_piece = swap(piece, "dp", 1)
    feed_pieces = all_pieces(feed_own, shard, core_shard)
    kept, rest = feed_slots(
        ids, (1, 2), after(second, piece), feed_pieces, rest + kept, None, units, extra
    )
    with jax.named_scope("feed_core"):
        core_far_piece = swap(after(far_piece, rest[0]), "dp", 1)
    feed_pieces += all_pieces(piece, core_piece, far_piece, core_far_piece)
    norm = (adapter_shift.reshape(1, -1), gain(2), shift(2), grad)
    kept, rest = feed_slots(
        ids, (3,), after(second, core_piece), feed_pieces, rest + kept, norm, units, extra
    )
    outcome, branch_low, sums_three = rest
    slopes, adapter_slopes, adapted_low = kept
    result = turn_over(outcome.reshape(4, share, width))
    a_low, grads = adapter_back(
        ids, branch_low, second, adapter_slopes, adapted_low, feed_pieces, units, extra
    )
    with jax.named_scope("adapter"):
        grads_there = [
            cross_swap(grads[1], 1, 2),
            cross_swap(grads[2], 2, 1),
            swap(grads[3], "tensor", 3),
        ]
    cross_low, sums_two = feed_back(
        ids,
        after(branch_low, a_low),
        slopes,
        a_low,
        feed_pieces,
        normed_two,
        scale_two,
        gain(1),
        units,
        extra,
    )
    adapter_sum = grads[0].astype(F32)
    for part in grads_there:
        adapter_sum = adapter_sum + part.astype(F32)
    adapter_sum = adapter_sum.astype(BF16)
    with jax.named_scope("adapter"):
        adapter_there = swap(adapter_sum, "dp", 1)
    encoded_back, self_low, sums_one = attention_back(
        after(cross_low, adapter_sum), cross_kept, cross_pieces, (normed_one, scale_one, gain(0))
    )
    adapter_sum = add_low(adapter_sum, after(adapter_there, self_low))
    encoded_result = turn_over(encoded_back.reshape(4, share, width))
    small = jnp.concatenate(
        [
            sums_one[0:1],
            sums_two[0:1],
            sums_three[0:1],
            sums_one[1:2],
            sums_two[1:2],
            sums_three[1:2],
            sums_three[2:3],
            jnp.zeros((1, width), F32),
        ],
        axis=0,
    )
    with jax.named_scope("small"):
        small_there = [swap(small, "tensor", k) for k in (1, 2, 3)]
    with jax.named_scope("adapter"):
        adapter_there = swap(adapter_sum, "dp", 2)
    input_back, result = attention_back(
        after(self_low, small, adapter_sum), self_kept, self_pieces, None, result
    )
    input_back, small_there, adapter_there, encoded_result = lax.optimization_barrier(
        (input_back, small_there, adapter_there, encoded_result)
    )
    input_result = turn_over(input_back.reshape(4, share, width))
    for part in small_there:
        small = small + part
    adapter_sum = add_low(adapter_sum, adapter_there)
    bit = 4
    while bit < lax.axis_size("dp"):
        with jax.named_scope("adapter"):
            adapter_sum = add_low(adapter_sum, swap(adapter_sum, "dp", bit))
        bit *= 2
    bit = 1
    while bit < lax.axis_size("dp"):
        with jax.named_scope("small"):
            small = small + swap(small, "dp", bit)
        bit *= 2
    encoded_result = copied(encoded_result)
    adapter_sum = adapter_sum.astype(F32)
    size = 4 * extra
    return (
        result,
        input_result,
        encoded_result,
        adapter_sum[:size].T,
        adapter_sum[size : 2 * size],
        jnp.sum(adapter_sum[2 * size :, :size], axis=0),
        small[6],
        small[0:3],
        small[3:6],
    )


def gelu_tanh(values):
    return jax.nn.gelu(values, approximate=True)


def multiply(left, right):
    return jnp.dot(left, right, preferred_element_type=jnp.float32)


def multiply_by_transpose(left, right):
    return lax.dot_general(
        left, right, (((1,), (1,)), ((), ())), preferred_element_type=jnp.float32
    )


def multiply_transposed_left(left, right):
    return lax.dot_general(
        left, right, (((0,), (0,)), ((), ())), preferred_element_type=jnp.float32
    )


def layer_norm(values, gain, shift):
    center = values - jnp.mean(values, axis=-1, keepdims=True)
    scale = lax.rsqrt(jnp.mean(center * center, axis=-1, keepdims=True) + 1e-05)
    normed = center * scale
    return (normed * gain + shift, normed, scale)


def norm_back(grad, normed, scale, gain):
    inner = grad * gain
    middle = jnp.mean(inner, axis=-1, keepdims=True)
    along = jnp.mean(inner * normed, axis=-1, keepdims=True)
    return (
        scale * (inner - middle - normed * along),
        jnp.sum(grad * normed, axis=(0, 1)),
        jnp.sum(grad, axis=(0, 1)),
    )


def attend(query_low, key_low, value_low, keep_for):
    count = query_low.shape[1]
    block = min(512, count)
    factor = query_low.shape[-1] ** (-0.5)
    contexts = []
    totals = []
    for first in range(0, count, block):
        scores = (
            jnp.einsum(
                "sqhe,skhe->shqk",
                query_low[:, first : first + block],
                key_low,
                preferred_element_type=jnp.float32,
            )
            * factor
        )
        scores = jnp.where(keep_for(first, block), scores, -1000000000.0)
        top_score = jnp.max(scores, axis=-1, keepdims=True)
        weights = jnp.exp(scores - top_score)
        denom = jnp.sum(weights, axis=-1, keepdims=True)
        probs_low = (weights / denom).astype(jnp.bfloat16)
        contexts.append(
            jnp.einsum("shqk,skhe->sqhe", probs_low, value_low, preferred_element_type=jnp.float32)
        )
        totals.append(top_score + jnp.log(denom))
    return (jnp.concatenate(contexts, axis=1), jnp.concatenate(totals, axis=2))


def attend_back(query_low, key_low, value_low, grad_low, totals, keep_for):
    count = query_low.shape[1]
    block = min(512, count)
    factor = query_low.shape[-1] ** (-0.5)
    key_grad = jnp.zeros(key_low.shape, jnp.float32)
    value_grad = jnp.zeros(value_low.shape, jnp.float32)
    query_grads = []
    for first in range(0, count, block):
        query_part = query_low[:, first : first + block]
        grad_part = grad_low[:, first : first + block]
        scores = (
            jnp.einsum("sqhe,skhe->shqk", query_part, key_low, preferred_element_type=jnp.float32)
            * factor
        )
        scores = jnp.where(keep_for(first, block), scores, -1000000000.0)
        probs = jnp.exp(scores - totals[:, :, first : first + block])
        probs_low = probs.astype(jnp.bfloat16)
        prob_grad = jnp.einsum(
            "sqhe,skhe->shqk", grad_part, value_low, preferred_element_type=jnp.float32
        )
        value_grad = value_grad + jnp.einsum(
            "shqk,sqhe->skhe", probs_low, grad_part, preferred_element_type=jnp.float32
        )
        along = jnp.sum(prob_grad * probs, axis=-1, keepdims=True)
        score_grad = (probs * (prob_grad - along)).astype(jnp.bfloat16)
        query_grads.append(
            jnp.einsum("shqk,skhe->sqhe", score_grad, key_low, preferred_element_type=jnp.float32)
            * factor
        )
        key_grad = (
            key_grad
            + jnp.einsum(
                "shqk,sqhe->skhe", score_grad, query_part, preferred_element_type=jnp.float32
            )
            * factor
        )
    return (jnp.concatenate(query_grads, axis=1), key_grad, value_grad)


def local(
    inputs,
    encoded,
    source_lengths,
    query_weight,
    key_weight,
    value_weight,
    output_weight,
    cross_query,
    cross_key,
    cross_value,
    cross_output,
    up_weight,
    down_weight,
    adapter_in,
    adapter_out,
    adapter_bias,
    adapter_shift,
    norm_gains,
    norm_shifts,
    output_grad,
):
    parts = lax.axis_size("tensor")
    place = lax.axis_index("tensor")
    sequences, share, width = inputs.shape
    length = share * parts
    rows = sequences * length
    heads = query_weight.shape[1] // HEAD
    local_width = heads * HEAD
    whole_inputs, whole_encoded = (
        lax.all_gather(inputs, "tensor", axis=1, tiled=True),
        lax.all_gather(encoded, "tensor", axis=1, tiled=True),
    )
    sources = whole_encoded.shape[1]
    flat_inputs = whole_inputs.reshape(rows, width)
    flat_encoded = whole_encoded.reshape(sequences * sources, width)

    def split_heads(values, count):
        return values.astype(jnp.bfloat16).reshape(sequences, count, heads, HEAD)

    def causal(first, block):
        query_pos = first + lax.broadcasted_iota(jnp.int32, (block, length), 0)
        key_pos = lax.broadcasted_iota(jnp.int32, (block, length), 1)
        return (key_pos <= query_pos)[None, None]

    def padded(first, block):
        key_pos = lax.broadcasted_iota(jnp.int32, (sequences, 1, 1, sources), 3)
        return key_pos < source_lengths[:, None, None, None]

    self_query = split_heads(multiply(flat_inputs, query_weight), length)
    self_key = split_heads(multiply(flat_inputs, key_weight), length)
    self_value = split_heads(multiply(flat_inputs, value_weight), length)
    self_context, self_totals = attend(self_query, self_key, self_value, causal)
    self_context_low = self_context.astype(jnp.bfloat16).reshape(rows, local_width)
    self_partial = multiply(self_context_low, output_weight).reshape(sequences, length, width)
    self_full = lax.psum(self_partial.astype(jnp.bfloat16), "tensor").astype(jnp.float32)
    first_full, normed_full, scale_full = layer_norm(
        whole_inputs.astype(jnp.float32) + self_full, norm_gains[0], norm_shifts[0]
    )
    first_low = first_full.astype(jnp.bfloat16)
    first_share = lax.dynamic_slice_in_dim(first_full, place * share, share, 1)
    normed_one = lax.dynamic_slice_in_dim(normed_full, place * share, share, 1)
    scale_one = lax.dynamic_slice_in_dim(scale_full, place * share, share, 1)
    flat_first = first_low.reshape(rows, width)
    cross_q = split_heads(multiply(flat_first, cross_query), length)
    cross_k = split_heads(multiply(flat_encoded, cross_key), sources)
    cross_v = split_heads(multiply(flat_encoded, cross_value), sources)
    cross_context, cross_totals = attend(cross_q, cross_k, cross_v, padded)
    cross_context_low = cross_context.astype(jnp.bfloat16).reshape(rows, local_width)
    cross_partial = multiply(cross_context_low, cross_output).reshape(sequences, length, width)
    cross_share = lax.psum_scatter(
        cross_partial.astype(jnp.bfloat16), "tensor", scatter_dimension=1, tiled=True
    ).astype(jnp.float32)
    second_share, normed_two, scale_two = layer_norm(
        first_share + cross_share, norm_gains[1], norm_shifts[1]
    )
    second_low = lax.all_gather(second_share.astype(jnp.bfloat16), "tensor", axis=1, tiled=True)
    flat_second = second_low.reshape(rows, width)
    hidden = multiply(flat_second, up_weight)
    hidden_low = gelu_tanh(hidden).astype(jnp.bfloat16)
    adapted = multiply(flat_second, adapter_in) + adapter_bias
    adapted_low = gelu_tanh(adapted).astype(jnp.bfloat16)
    branch_partial = multiply(hidden_low, down_weight) + 4.0 * multiply(adapted_low, adapter_out)
    branch_share = lax.psum_scatter(
        branch_partial.reshape(sequences, length, width).astype(jnp.bfloat16),
        "tensor",
        scatter_dimension=1,
        tiled=True,
    ).astype(jnp.float32)
    third_input = second_share + branch_share + 4.0 * adapter_shift
    outcome, normed_three, scale_three = layer_norm(third_input, norm_gains[2], norm_shifts[2])
    grad_three, gain_grad_three, shift_grad_three = norm_back(
        output_grad.astype(jnp.float32), normed_three, scale_three, norm_gains[2]
    )
    shift_grad_adapter = 4.0 * jnp.sum(grad_three, axis=(0, 1))
    branch_grad = lax.all_gather(
        grad_three.astype(jnp.bfloat16), "tensor", axis=1, tiled=True
    ).reshape(rows, width)
    hidden_grad = multiply_by_transpose(branch_grad, down_weight)
    hidden_unused, hidden_pull = jax.vjp(gelu_tanh, hidden)
    hidden_grad_low = hidden_pull(hidden_grad)[0].astype(jnp.bfloat16)
    adapted_grad = 4.0 * multiply_by_transpose(branch_grad, adapter_out)
    adapted_unused, adapted_pull = jax.vjp(gelu_tanh, adapted)
    adapted_grad = adapted_pull(adapted_grad)[0]
    bias_grad = jnp.sum(adapted_grad, axis=0)
    adapted_grad_low = adapted_grad.astype(jnp.bfloat16)
    in_grad = multiply_transposed_left(flat_second, adapted_grad_low)
    out_grad = 4.0 * multiply_transposed_left(adapted_low, branch_grad)
    second_partial = multiply_by_transpose(hidden_grad_low, up_weight) + multiply_by_transpose(
        adapted_grad_low, adapter_in
    )
    second_grad = grad_three + lax.psum_scatter(
        second_partial.reshape(sequences, length, width).astype(jnp.bfloat16),
        "tensor",
        scatter_dimension=1,
        tiled=True,
    ).astype(jnp.float32)
    grad_two, gain_grad_two, shift_grad_two = norm_back(
        second_grad, normed_two, scale_two, norm_gains[1]
    )
    cross_grad = lax.all_gather(
        grad_two.astype(jnp.bfloat16), "tensor", axis=1, tiled=True
    ).reshape(rows, width)
    cross_context_grad = multiply_by_transpose(cross_grad, cross_output).astype(jnp.bfloat16)
    cross_context_grad = cross_context_grad.reshape(sequences, length, heads, HEAD)
    cq_grad, ck_grad, cv_grad = attend_back(
        cross_q, cross_k, cross_v, cross_context_grad, cross_totals, padded
    )
    first_partial = multiply_by_transpose(
        cq_grad.astype(jnp.bfloat16).reshape(rows, local_width), cross_query
    )
    encoded_partial = multiply_by_transpose(
        ck_grad.astype(jnp.bfloat16).reshape(sequences * sources, local_width), cross_key
    ) + multiply_by_transpose(
        cv_grad.astype(jnp.bfloat16).reshape(sequences * sources, local_width), cross_value
    )
    first_back, encoded_share = (
        lax.psum_scatter(
            first_partial.reshape(sequences, length, width).astype(jnp.bfloat16),
            "tensor",
            scatter_dimension=1,
            tiled=True,
        ).astype(jnp.float32),
        lax.psum_scatter(
            encoded_partial.reshape(sequences, sources, width).astype(jnp.bfloat16),
            "tensor",
            scatter_dimension=1,
            tiled=True,
        ).astype(jnp.float32),
    )
    grad_one, gain_grad_one, shift_grad_one = norm_back(
        grad_two + first_back, normed_one, scale_one, norm_gains[0]
    )
    self_grad = lax.all_gather(grad_one.astype(jnp.bfloat16), "tensor", axis=1, tiled=True).reshape(
        rows, width
    )
    self_context_grad = multiply_by_transpose(self_grad, output_weight).astype(jnp.bfloat16)
    self_context_grad = self_context_grad.reshape(sequences, length, heads, HEAD)
    sq_grad, sk_grad, sv_grad = attend_back(
        self_query, self_key, self_value, self_context_grad, self_totals, causal
    )
    input_partial = (
        multiply_by_transpose(sq_grad.astype(jnp.bfloat16).reshape(rows, local_width), query_weight)
        + multiply_by_transpose(sk_grad.astype(jnp.bfloat16).reshape(rows, local_width), key_weight)
        + multiply_by_transpose(
            sv_grad.astype(jnp.bfloat16).reshape(rows, local_width), value_weight
        )
    )
    small_grads = jnp.stack(
        [
            gain_grad_one,
            gain_grad_two,
            gain_grad_three,
            shift_grad_one,
            shift_grad_two,
            shift_grad_three,
            shift_grad_adapter,
        ]
    )
    spread = jnp.broadcast_to(small_grads[:, None, :], (7, parts, width))
    input_back, small_back = (
        lax.psum_scatter(
            input_partial.reshape(sequences, length, width).astype(jnp.bfloat16),
            "tensor",
            scatter_dimension=1,
            tiled=True,
        ).astype(jnp.float32),
        lax.psum_scatter(
            spread.astype(jnp.bfloat16), "tensor", scatter_dimension=1, tiled=True
        ).astype(jnp.float32),
    )
    input_result = (grad_one + input_back).astype(jnp.bfloat16)
    encoded_result = encoded_share.astype(jnp.bfloat16)
    in_total, out_total, bias_total, small_total = (
        lax.psum(in_grad.astype(jnp.bfloat16), "dp").astype(jnp.float32),
        lax.psum(out_grad.astype(jnp.bfloat16), "dp").astype(jnp.float32),
        lax.psum(bias_grad.astype(jnp.bfloat16), "dp").astype(jnp.float32),
        lax.psum(small_back[:, 0].astype(jnp.bfloat16), "dp").astype(jnp.float32),
    )
    return (
        outcome.astype(jnp.bfloat16),
        input_result,
        encoded_result,
        in_total,
        out_total,
        bias_total,
        small_total[6],
        small_total[0:3],
        small_total[3:6],
    )


def solution(mesh):
    placed = (
        P("dp", "tensor", None),
        P("dp", "tensor", None),
        P("dp"),
        P(None, "tensor"),
        P(None, "tensor"),
        P(None, "tensor"),
        P("tensor", None),
        P(None, "tensor"),
        P(None, "tensor"),
        P(None, "tensor"),
        P("tensor", None),
        P(None, "tensor"),
        P("tensor", None),
        P(None, "tensor"),
        P("tensor", None),
        P("tensor"),
        P(),
        P(),
        P(),
        P("dp", "tensor", None),
    )
    suits = mesh.shape["tensor"] == 4 and mesh.shape["dp"] in (4, 8, 16, 32)

    def layer(*arrays):
        if suits and arrays[0].shape[:2] == (4, ROWS) and arrays[1].shape[:2] == (4, ROWS):
            return whole_sequences(*arrays)
        return local(*arrays)

    return jax.shard_map(
        layer,
        mesh=mesh,
        in_specs=placed,
        out_specs=(
            P("dp", "tensor", None),
            P("dp", "tensor", None),
            P("dp", "tensor", None),
            P(None, "tensor"),
            P("tensor", None),
            P("tensor"),
            P(),
            P(),
            P(),
        ),
        check_vma=False,
    )
```

```python
import functools
import jax
import jax.numpy as jnp
from jax import lax
from jax.experimental import pallas as pl
from jax.experimental.pallas import tpu as pltpu
from jax.sharding import PartitionSpec as P

HEAD = 64
F32 = jnp.float32
BF16 = jnp.bfloat16
LOG2E = 1.4426950408889634
LN2 = 0.6931471805599453
VMEM_LIMIT = 60 * 2**20
ROWS = 256
BLOCK = 256
ANY = pl.BlockSpec(memory_space=pl.ANY)
SMEM = pl.BlockSpec(memory_space=pltpu.SMEM)


def cost(flops, moved):
    return pl.CostEstimate(flops=int(flops * SHARE), bytes_accessed=int(moved * SHARE), transcendentals=0)


SHARE = 1.0


def nn(left, right):
    return lax.dot_general(left, right, (((1,), (0,)), ((), ())), preferred_element_type=F32)


def nt(left, right):
    return lax.dot_general(left, right, (((1,), (1,)), ((), ())), preferred_element_type=F32)


def tn(left, right):
    return lax.dot_general(left, right, (((0,), (0,)), ((), ())), preferred_element_type=F32)


def norm_rows(values):
    center = values - jnp.mean(values, axis=-1, keepdims=True)
    scale = lax.rsqrt(jnp.mean(center * center, axis=-1, keepdims=True) + 1e-05)
    return center * scale, scale


def norm_back_rows(grad, normed, scale, gain):
    inner = grad * gain
    middle = jnp.mean(inner, axis=-1, keepdims=True)
    along = jnp.mean(inner * normed, axis=-1, keepdims=True)
    return scale * (inner - middle - normed * along)


def gelu_and_slope(v):
    root = 0.7978845608028654
    square = v * v
    t = jnp.tanh(v * (root + (root * 0.044715) * square))
    half = 0.5 + 0.5 * t
    slope = half + (v * half) * (1.0 - t) * (root + (3.0 * root * 0.044715) * square)
    return v * half, slope


def head_rows(h):
    return slice(h * HEAD, (h + 1) * HEAD)


def natural(turn, p):
    slot, t = p // 4, p % 4
    return t ^ turn if slot == 3 else t


def sum_rows(values):
    return jnp.sum(values, axis=0, keepdims=True)


def pack_heads_kernel(ids_ref, q_ref, k_ref, v_ref, o_ref, own_ref):
    part = own_ref.shape[2]
    for m, ref in enumerate((q_ref, k_ref, v_ref, o_ref)):
        values = ref[...] if m == 3 else ref[...].T
        for t in range(4):
            own_ref[t, m] = values[t * part : (t + 1) * part]


def pack_units_kernel(ids_ref, up_ref, down_ref, ain_ref, aout_ref, bias_ref, own_ref):
    units, extra = down_ref.shape[0] // 4, aout_ref.shape[0] // 4
    turned = ain_ref[...].T
    bias = bias_ref[...]
    begin = 2 * units + 2 * extra
    for t in range(4):
        cols = slice(t * units, (t + 1) * units)
        own_ref[t, :units] = up_ref[:, cols].T
        own_ref[t, units : 2 * units] = down_ref[cols, :]
        own_ref[t, 2 * units : 2 * units + extra] = turned[t * extra : (t + 1) * extra]
        own_ref[t, 2 * units + extra : begin] = aout_ref[t * extra : (t + 1) * extra, :]
        own_ref[t, begin:, : 4 * extra] = split_lines(bias)


def split_lines(values):
    rows, rest = [], values
    for _ in range(3):
        low = rest.astype(BF16)
        rows.append(low)
        rest = rest - low.astype(F32)
    rows.append(jnp.zeros((13,) + values.shape[1:], BF16))
    return jnp.concatenate(rows, axis=0)


def pack(kernel, name, ids, own_shape, *weights):
    vmem = pl.BlockSpec(memory_space=pltpu.VMEM)
    return pl.pallas_call(
        kernel,
        in_specs=[SMEM] + [vmem] * len(weights),
        out_specs=vmem,
        out_shape=jax.ShapeDtypeStruct((4,) + own_shape, BF16),
        compiler_params=pltpu.CompilerParams(vmem_limit_bytes=VMEM_LIMIT),
        cost_estimate=cost(0, 8 * 2**20),
        name=name,
    )(ids, *weights)


def attend_kernel(causal, count, first, homes, ids_ref, *refs):
    refs = list(refs)
    xq_hbm = refs.pop(0)
    xkv_hbm = xq_hbm if causal else refs.pop(0)
    sources_of = [refs.pop(0) for _ in range(len(set(n for n, _ in homes)))]
    if not first:
        refs = refs[4:]
    e_ref, hd_ref, il_ref, ctx_ref, xq, xkv, weights, qkv, x_sems, w_sems = refs
    if causal:
        xkv = xq
    step = pl.program_id(0)
    span, sources = xq.shape[0], xkv.shape[0]
    part = weights.shape[2] // 4

    def weight_copy(s, t):
        n, index = homes[4 * s + t]
        return pltpu.make_async_copy(
            sources_of[n].at[index, pl.ds(0, 3)],
            weights.at[s, :, pl.ds(t * part, part), :],
            w_sems.at[4 * s + t],
        )

    x_copies = [pltpu.make_async_copy(xq_hbm, xq, x_sems.at[0])]
    if not causal:
        x_copies.append(pltpu.make_async_copy(xkv_hbm, xkv, x_sems.at[1]))

    @pl.when(step == 0)
    def _():
        for t in range(4):
            weight_copy(0, t).start()
        for copy in x_copies:
            copy.start()
        for s in range(1, count):
            for t in range(4):
                weight_copy(s, t).start()
        for copy in x_copies:
            copy.wait()

    for s in range(count):

        @pl.when(step == 2 * s)
        def _():
            for t in range(4):
                weight_copy(s, t).wait()
            qkv[0] = (nt(weights[s, 0], xq[...]) * (LOG2E * HEAD**-0.5)).astype(BF16)
            qkv[1] = nt(weights[s, 1], xkv[...]).astype(BF16)
            qkv[2] = nt(weights[s, 2], xkv[...]).astype(BF16)

    pair = pl.ds(pl.multiple_of((step % 2) * 128, 128), 128)
    q2, k2, v2 = qkv[0, pair, :], qkv[1, pair, :], qkv[2, pair, :]
    hd_ref[0], hd_ref[1], hd_ref[2] = q2, k2, v2
    block = min(BLOCK, span)
    work = [(i, h) for i in range(span // block) for h in range(2)]

    def reach(i):
        return (i + 1) * block if causal else sources

    def score(i, h):
        return tn(k2[head_rows(h), : reach(i)], q2[head_rows(h), i * block : (i + 1) * block])

    ahead = 2 if causal else 4
    waiting = [score(i, h) for i, h in work[:ahead]]
    for number, (i, h) in enumerate(work):
        n, cols = reach(i), slice(i * block, (i + 1) * block)
        s = waiting.pop(0)
        if number + ahead < len(work):
            waiting.append(score(*work[number + ahead]))
        if causal:
            key = lax.broadcasted_iota(jnp.int32, (block, block), 0)
            query = lax.broadcasted_iota(jnp.int32, (block, block), 1)
            tail = jnp.where(key <= query, s[n - block :], -1e9)
            s = jnp.concatenate([s[: n - block], tail], axis=0) if n > block else tail
        else:
            key = lax.broadcasted_iota(jnp.int32, (n, block), 0)
            s = jnp.where(key < ids_ref[2], s, -1e9)
        e = jnp.exp2(s - jnp.max(s, axis=0, keepdims=True))
        inverse = 1.0 / jnp.sum(e, axis=0, keepdims=True)
        low = e.astype(BF16)
        e_ref[h, :n, cols] = low
        il_ref[h, :, cols] = inverse
        context = (nn(v2[head_rows(h), :n], low) * inverse).astype(BF16)
        hd_ref[3, head_rows(h), cols] = context
        contexts = [context] if h == 0 else contexts + [context]
        if h == 1:
            ctx_ref[cols, :] = jnp.concatenate(contexts, axis=0).T


def gather_homes(pieces):
    arrays, homes = [], []
    for array, index in pieces:
        where = [n for n, known in enumerate(arrays) if known is array]
        if not where:
            arrays.append(array)
            where = [len(arrays) - 1]
        homes.append((where[0], index))
    return arrays, tuple(homes)


def attend_slots(ids, slots, xq, xkv, pieces, before):
    causal = xkv is None
    span, width = xq.shape
    sources = span if causal else xkv.shape[0]
    heads = width // HEAD
    count, base = len(slots), 2 * slots[0]
    arrays, homes = gather_homes([pieces[4 * s + t] for s in slots for t in range(4)])
    part = arrays[0].shape[2]
    first = before is None
    operands = [ids, xq] + ([] if causal else [xkv]) + arrays
    specs = [SMEM] + [ANY] * (len(operands) - 1)
    aliases = {}
    if not first:
        aliases = {len(operands) + n: n for n in range(4)}
        operands += list(before)
        specs += [ANY] * 4
    return pl.pallas_call(
        functools.partial(attend_kernel, causal, count, first, homes),
        grid=(2 * count,),
        in_specs=specs,
        out_specs=(
            pl.BlockSpec((2, sources, span), lambda j: (base + j, 0, 0)),
            pl.BlockSpec((4, 128, span), lambda j: (0, base + j, 0)),
            pl.BlockSpec((2, 1, span), lambda j: (base + j, 0, 0)),
            pl.BlockSpec((span, 128), lambda j: (0, base + j)),
        ),
        out_shape=(
            jax.ShapeDtypeStruct((heads, sources, span), BF16),
            jax.ShapeDtypeStruct((4, width, span), BF16),
            jax.ShapeDtypeStruct((heads, 1, span), F32),
            jax.ShapeDtypeStruct((span, width), BF16),
        ),
        scratch_shapes=[
            pltpu.VMEM((span, width), BF16),
            pltpu.VMEM((16, 128) if causal else (sources, width), BF16),
            pltpu.VMEM((count, 3, 4 * part, width), BF16),
            pltpu.VMEM((3, 4 * part, max(span, sources)), BF16),
            pltpu.SemaphoreType.DMA((2,)),
            pltpu.SemaphoreType.DMA((4 * count,)),
        ],
        input_output_aliases=aliases,
        compiler_params=pltpu.CompilerParams(vmem_limit_bytes=VMEM_LIMIT),
        cost_estimate=cost(count * 10 * 10**9, count * 12 * 2**20),
        name="self_attend" if causal else "cross_attend",
    )(*operands)


def out_norm_kernel(homes, *refs):
    refs = list(refs)
    ctx_ref, x_ref, gain_ref, shift_ref = refs[:4]
    sources = refs[4:-5]
    low_ref, n_ref, r_ref, wo, sems = refs[-5:]
    part = wo.shape[0] // len(homes)
    copies = [
        pltpu.make_async_copy(sources[n].at[index, 3], wo.at[pl.ds(p * part, part), :], sems.at[p])
        for p, (n, index) in enumerate(homes)
    ]

    @pl.when(pl.program_id(0) == 0)
    def _():
        for copy in copies:
            copy.start()
        for copy in copies:
            copy.wait()

    rows_here = ctx_ref.shape[0]
    for i in range(rows_here // ROWS):
        rows = slice(i * ROWS, (i + 1) * ROWS)
        total = nn(ctx_ref[rows, :], wo[...]) + x_ref[rows, :].astype(F32)
        normed, scale = norm_rows(total)
        low_ref[rows, :] = (normed * gain_ref[...] + shift_ref[...]).astype(BF16)
        n_ref[rows, :] = normed.astype(BF16)
        r_ref[rows, :] = scale


def out_norm(ctx, pieces, residual, gain, shift):
    span, width = ctx.shape
    arrays, homes = gather_homes(pieces)
    block = min(512, span)
    rows = lambda w: pl.BlockSpec((block, w), lambda i: (i, 0))
    line = pl.BlockSpec((1, width), lambda i: (0, 0))
    return pl.pallas_call(
        functools.partial(out_norm_kernel, homes),
        grid=(span // block,),
        in_specs=[rows(width), rows(width), line, line] + [ANY] * len(arrays),
        out_specs=(rows(width), rows(width), rows(1)),
        out_shape=(
            jax.ShapeDtypeStruct((span, width), BF16),
            jax.ShapeDtypeStruct((span, width), BF16),
            jax.ShapeDtypeStruct((span, 1), F32),
        ),
        scratch_shapes=[pltpu.VMEM((width, width), BF16), pltpu.SemaphoreType.DMA((len(homes),))],
        compiler_params=pltpu.CompilerParams(vmem_limit_bytes=VMEM_LIMIT),
        cost_estimate=cost(2 * span * width * width, 10 * 2**20),
        name="out_norm",
    )(ctx, residual, gain, shift, *arrays)


def feed_kernel(slots, first, last, units, extra, homes, ids_ref, *refs):
    count = len(slots)
    refs = list(refs)
    x_ref = refs.pop(0)
    sources = [refs.pop(0) for _ in range(len(set(n for n, _ in homes)))]
    if last:
        shift_a_ref, gain_ref, shift_ref, grad_ref = [refs.pop(0) for _ in range(4)]
    if not first:
        acc_hbm = refs.pop(0)
        refs = refs[3:]
    gp_ref, gpa_ref, alow_ref = [refs.pop(0) for _ in range(3)]
    if last:
        out_ref, low_ref, sum_ref = [refs.pop(0) for _ in range(3)]
    acc, up, down, ain, aout, bias, w_sems, b_sems, acc_sem = refs
    step = pl.program_id(0)
    span = x_ref.shape[0]

    def piece_copies(p):
        n, index = homes[p]
        there = 4 * (p // 4) + natural(ids_ref[1], 4 * slots[0] + p)
        parts = (
            (0, units, up, p),
            (units, units, down, p),
            (2 * units, extra, ain, there),
            (2 * units + extra, extra, aout, there),
        )
        found = [
            pltpu.make_async_copy(
                sources[n].at[index, pl.ds(begin, size), :],
                held.at[pl.ds(to * size, size), :],
                w_sems.at[p, m],
            )
            for m, (begin, size, held, to) in enumerate(parts)
        ]
        if p % 4 == 0:
            found.append(
                pltpu.make_async_copy(
                    sources[n].at[index, pl.ds(2 * units + 2 * extra, 16), pl.ds(0, 4 * extra)],
                    bias.at[p // 4],
                    b_sems.at[p // 4],
                )
            )
        return found

    def acc_copy():
        return pltpu.make_async_copy(acc_hbm, acc, acc_sem)

    @pl.when(step == 0)
    def _():
        for p in range(4 * count):
            for copy in piece_copies(p):
                copy.start()
            if p == 3 and not first:
                acc_copy().start()

    half = min(512, span)
    for s in range(count):

        @pl.when(step == s)
        def _():
            for p in range(4 * s, 4 * s + 4):
                for copy in piece_copies(p):
                    copy.wait()
            wide = slice(4 * units * s, 4 * units * (s + 1))
            small = slice(4 * extra * s, 4 * extra * (s + 1))
            shift_a = sum_rows(bias[s].astype(F32))
            for i in range(span // half):
                rows = slice(i * half, (i + 1) * half)
                x = x_ref[rows, :]
                a, slope = gelu_and_slope(nt(x, ain[small, :]) + shift_a)
                a_low = a.astype(BF16)
                alow_ref[rows, :] = a_low
                gpa_ref[rows, :] = slope.astype(BF16)
                h, slope = gelu_and_slope(nt(x, up[wide, :]))
                gp_ref[rows, :] = slope.astype(BF16)
                total = nn(h.astype(BF16), down[wide, :]) + 4.0 * nn(a_low, aout[small, :])
                if s == 0 and i == 0 and not first:
                    acc_copy().wait()
                acc[rows, :] = total if first and s == 0 else acc[rows, :] + total

    if last:

        @pl.when(step == pl.num_programs(0) - 1)
        def _():
            sum_ref[...] = jnp.zeros_like(sum_ref)
            for i in range(span // ROWS):
                rows = slice(i * ROWS, (i + 1) * ROWS)
                total = acc[rows, :] + x_ref[rows, :].astype(F32) + 4.0 * shift_a_ref[...]
                normed, scale = norm_rows(total)
                out_ref[rows, :] = (normed * gain_ref[...] + shift_ref[...]).astype(BF16)
                grad = grad_ref[rows, :].astype(F32)
                back = norm_back_rows(grad, normed, scale, gain_ref[...])
                low_ref[rows, :] = back.astype(BF16)
                sum_ref[0:1, :] += sum_rows(grad * normed)
                sum_ref[1:2, :] += sum_rows(grad)
                sum_ref[2:3, :] += 4.0 * sum_rows(back)


def feed_slots(ids, slots, x, pieces, before, norm, units, extra):
    span, width = x.shape
    first, last = before is None, norm is not None
    count = len(slots)
    whole = lambda a: pl.BlockSpec(a.shape, lambda j: (0,) * a.ndim, pipeline_mode=pl.Buffered(1))
    arrays, homes = gather_homes([pieces[4 * s + t] for s in slots for t in range(4)])
    operands = [ids, x] + arrays
    specs = [SMEM, whole(x)] + [ANY] * len(arrays)
    if last:
        operands += list(norm)
        specs += [whole(a) for a in norm]
    kept_shape = [
        jax.ShapeDtypeStruct((span, 16 * units), BF16),
        jax.ShapeDtypeStruct((span, 16 * extra), BF16),
        jax.ShapeDtypeStruct((span, 16 * extra), BF16),
    ]
    kept_specs = [
        pl.BlockSpec((span, 4 * units), lambda j: (0, slots[0] + j)),
        pl.BlockSpec((span, 4 * extra), lambda j: (0, slots[0] + j)),
        pl.BlockSpec((span, 4 * extra), lambda j: (0, slots[0] + j)),
    ]
    aliases = {}
    if not first:
        aliases = {len(operands) + 1 + n: n for n in range(3)}
        operands += list(before)
        specs += [ANY] * 4
    total = jax.ShapeDtypeStruct((span, width), F32)
    once = lambda s: pl.BlockSpec(s.shape, lambda j: (0,) * len(s.shape), pipeline_mode=pl.Buffered(1))
    if last:
        low = jax.ShapeDtypeStruct((span, width), BF16)
        more = [low, low, jax.ShapeDtypeStruct((8, width), F32)]
        scratch = [pltpu.VMEM((span, width), F32)]
    else:
        more, scratch = [total], []
    outs = pl.pallas_call(
        functools.partial(feed_kernel, slots, first, last, units, extra, homes),
        grid=(count,),
        in_specs=specs,
        out_specs=kept_specs + [once(s) for s in more],
        out_shape=kept_shape + more,
        scratch_shapes=scratch
        + [
            pltpu.VMEM((count * 4 * units, width), BF16),
            pltpu.VMEM((count * 4 * units, width), BF16),
            pltpu.VMEM((count * 4 * extra, width), BF16),
            pltpu.VMEM((count * 4 * extra, width), BF16),
            pltpu.VMEM((count, 16, 4 * extra), BF16),
            pltpu.SemaphoreType.DMA((4 * count, 4)),
            pltpu.SemaphoreType.DMA((count,)),
            pltpu.SemaphoreType.DMA,
        ],
        input_output_aliases=aliases,
        compiler_params=pltpu.CompilerParams(vmem_limit_bytes=VMEM_LIMIT),
        cost_estimate=cost(count * 6 * 10**9, count * 14 * 2**20),
        name="feed",
    )(*operands)
    kept, rest = list(outs[:3]), list(outs[3:])
    return kept, rest


def adapter_back_kernel(extra, units, homes, ids_ref, *refs):
    refs = list(refs)
    g_ref, x_ref, gpa_ref, alow_ref = refs[:4]
    low_ref, *slot_refs, aout, sems = refs[-7:]
    sources = refs[4:-7]
    begin = 2 * units + extra
    copies = []
    for p, (n, index) in enumerate(homes):
        there = 4 * (p // 4) + natural(ids_ref[1], p)
        copies.append(
            pltpu.make_async_copy(
                sources[n].at[index, pl.ds(begin, extra), :],
                aout.at[pl.ds(there * extra, extra), :],
                sems.at[p],
            )
        )
    for copy in copies:
        copy.start()
    for copy in copies:
        copy.wait()
    g = g_ref[...]
    a = 4.0 * nt(g, aout[...]) * gpa_ref[...].astype(F32)
    bias = sum_rows(a)
    a_low = a.astype(BF16)
    low_ref[...] = a_low
    in_grad = tn(a_low, x_ref[...]).astype(BF16)
    out_grad = (4.0 * tn(alow_ref[...], g)).astype(BF16)
    size = 4 * extra
    for k in range(4):
        rows = slice(k * size, (k + 1) * size)
        slot_refs[k][:size] = in_grad[rows]
        slot_refs[k][size : 2 * size] = out_grad[rows]
        slot_refs[k][2 * size :] = jnp.zeros((16, g.shape[1]), BF16)
        slot_refs[k][2 * size :, :size] = split_lines(bias[:, rows])


def adapter_back(ids, g, x, gpa, alow, pieces, units, extra):
    span, width = g.shape
    arrays, homes = gather_homes(pieces)
    vmem = pl.BlockSpec(memory_space=pltpu.VMEM)
    outs = pl.pallas_call(
        functools.partial(adapter_back_kernel, extra, units, homes),
        in_specs=[SMEM] + [vmem] * 4 + [ANY] * len(arrays),
        out_specs=[vmem] * 5,
        out_shape=[jax.ShapeDtypeStruct((span, 16 * extra), BF16)]
        + [jax.ShapeDtypeStruct((8 * extra + 16, width), BF16)] * 4,
        scratch_shapes=[pltpu.VMEM((16 * extra, width), BF16), pltpu.SemaphoreType.DMA((16,))],
        compiler_params=pltpu.CompilerParams(vmem_limit_bytes=VMEM_LIMIT),
        cost_estimate=cost(6 * span * width * 16 * extra, 12 * 2**20),
        name="adapter_back",
    )(ids, g, x, gpa, alow, *arrays)
    return outs[0], list(outs[1:])


def feed_back_kernel(units, extra, homes, ids_ref, *refs):
    refs = list(refs)
    g_ref, gp_ref, alow_ref, n_ref, r_ref, gain_ref = refs[:6]
    low_ref, sum_ref, acc, up, down, ain, w_sems, a_sems = refs[-8:]
    sources = refs[6:-8]
    step = pl.program_id(0)
    steps = len(homes) // 2
    span = g_ref.shape[0]

    def chunk_copies(j, home):
        copies = []
        for t in range(2):
            n, index = homes[2 * home + t]
            for m, held in enumerate((up, down)):
                copies.append(
                    pltpu.make_async_copy(
                        sources[n].at[index, pl.ds(m * units, units), :],
                        held.at[j % 2, pl.ds(t * units, units), :],
                        w_sems.at[j % 2, t, m],
                    )
                )
        return copies

    def ain_copies():
        return [
            pltpu.make_async_copy(
                sources[n].at[index, pl.ds(2 * units, extra), :],
                ain.at[pl.ds((4 * (p // 4) + natural(ids_ref[1], p)) * extra, extra), :],
                a_sems.at[p],
            )
            for p, (n, index) in enumerate(homes)
        ]

    @pl.when(step == 0)
    def _():
        for copy in ain_copies():
            copy.start()
        for copy in chunk_copies(0, 0):
            copy.start()
        for copy in ain_copies():
            copy.wait()
        acc[...] = nn(alow_ref[...], ain[...]) + g_ref[...].astype(F32)

    for j in range(1, steps):

        @pl.when(step == j - 1)
        def _():
            for copy in chunk_copies(j, j):
                copy.start()

    for copy in chunk_copies(step, 0):
        copy.wait()
    half = min(512, span)
    side = step % 2
    for i in range(span // half):
        rows = slice(i * half, (i + 1) * half)
        h = (nt(g_ref[rows, :], down[side]) * gp_ref[rows, :].astype(F32)).astype(BF16)
        acc[rows, :] += nn(h, up[side])

    @pl.when(step == pl.num_programs(0) - 1)
    def _():
        sum_ref[...] = jnp.zeros_like(sum_ref)
        for i in range(span // ROWS):
            rows = slice(i * ROWS, (i + 1) * ROWS)
            grad = acc[rows, :]
            normed = n_ref[rows, :].astype(F32)
            back = norm_back_rows(grad, normed, r_ref[rows, :], gain_ref[...])
            low_ref[rows, :] = back.astype(BF16)
            sum_ref[0:1, :] += sum_rows(grad * normed)
            sum_ref[1:2, :] += sum_rows(grad)


def feed_back(ids, g, slopes, a_low, pieces, normed, scale, gain, units, extra):
    span, width = g.shape
    arrays, homes = gather_homes(pieces)
    whole = lambda a: pl.BlockSpec(a.shape, lambda j: (0,) * a.ndim, pipeline_mode=pl.Buffered(1))
    out_shape = (jax.ShapeDtypeStruct((span, width), BF16), jax.ShapeDtypeStruct((8, width), F32))
    return pl.pallas_call(
        functools.partial(feed_back_kernel, units, extra, homes),
        grid=(8,),
        in_specs=[
            SMEM,
            whole(g),
            pl.BlockSpec((span, 2 * units), lambda j: (0, j)),
            whole(a_low),
            whole(normed),
            whole(scale),
            whole(gain),
        ]
        + [ANY] * len(arrays),
        out_specs=tuple(
            pl.BlockSpec(s.shape, lambda j: (0, 0), pipeline_mode=pl.Buffered(1)) for s in out_shape
        ),
        out_shape=out_shape,
        scratch_shapes=[
            pltpu.VMEM((span, width), F32),
            pltpu.VMEM((2, 2 * units, width), BF16),
            pltpu.VMEM((2, 2 * units, width), BF16),
            pltpu.VMEM((16 * extra, width), BF16),
            pltpu.SemaphoreType.DMA((2, 2, 2)),
            pltpu.SemaphoreType.DMA((16,)),
        ],
        compiler_params=pltpu.CompilerParams(vmem_limit_bytes=VMEM_LIMIT),
        cost_estimate=cost(20 * 10**9, 40 * 2**20),
        name="feed_back",
    )(ids, g, slopes, a_low, normed, scale, gain, *arrays)


def attention_back_kernel(causal, homes, *refs):
    refs = list(refs)
    g_ref, e_ref, hd_ref, il_ref = refs[:4]
    refs = refs[4:]
    if not causal:
        n_ref, r_ref, gain_ref = [refs.pop(0) for _ in range(3)]
    sources_of = [refs.pop(0) for _ in range(len(set(n for n, _ in homes)))]
    if causal:
        passed_hbm = refs.pop(0)
    out_ref = refs.pop(0)
    if causal:
        put_hbm = refs.pop(0)
    else:
        low_ref, sum_ref = [refs.pop(0) for _ in range(2)]
    wf, ct, dq, dk, dv, sems = refs[:6]
    step = pl.program_id(0)
    if causal:
        passing, pass_sems = refs[6:]
        bring = pltpu.make_async_copy(passed_hbm, passing, pass_sems.at[0])
        put = pltpu.make_async_copy(passing, put_hbm, pass_sems.at[1])

        @pl.when(step == 1)
        def _():
            bring.start()

        @pl.when(step == 3)
        def _():
            bring.wait()
            put.start()

        @pl.when(step == pl.num_programs(0) - 1)
        def _():
            put.wait()

    span = g_ref.shape[0]
    sources = e_ref.shape[1]
    part = wf.shape[1] // len(homes)

    def copies(wanted):
        found = []
        for p, (n, index) in enumerate(homes):
            begin, size = (3, 1) if wanted else (0, 3)
            found.append(
                pltpu.make_async_copy(
                    sources_of[n].at[index, pl.ds(begin, size)],
                    wf.at[pl.ds(begin, size), pl.ds(p * part, part), :],
                    sems.at[wanted, p],
                )
            )
        return found

    @pl.when(step == 0)
    def _():
        for copy in copies(1) + copies(0):
            copy.start()
        for copy in copies(1):
            copy.wait()
        ct[...] = nt(wf[3], g_ref[...]).astype(BF16)

    pair = pl.ds(pl.multiple_of(step * 128, 128), 128)
    c2 = ct[pair, :]
    block = min(BLOCK if causal else 512, span)
    scaled, dots = [], []
    for h in range(2):
        c = c2[head_rows(h), :].astype(F32) * il_ref[h]
        dots.append(jnp.sum(c * hd_ref[3, head_rows(h), :].astype(F32), axis=0, keepdims=True))
        scaled.append(c.astype(BF16))
    sums_k, sums_v = [None, None], [None, None]
    for i in reversed(range(span // block)):
        n = (i + 1) * block if causal else sources
        cols = slice(i * block, (i + 1) * block)
        grads = [tn(hd_ref[2, head_rows(h), :n], scaled[h][:, cols]) for h in range(2)]
        queries = []
        for h in range(2):
            e = e_ref[h, :n, cols]
            ds = (e.astype(F32) * (grads[h] - dots[h][:, cols])).astype(BF16)
            queries.append((nn(hd_ref[1, head_rows(h), :n], ds) * HEAD**-0.5).astype(BF16))
            gk = nn(ds, hd_ref[0, head_rows(h), cols].T)
            gv = nn(e, scaled[h][:, cols].T)
            if sums_k[h] is None:
                sums_k[h], sums_v[h] = gk, gv
            elif n == sums_k[h].shape[0]:
                sums_k[h], sums_v[h] = sums_k[h] + gk, sums_v[h] + gv
            else:
                sums_k[h] = jnp.concatenate([sums_k[h][:n] + gk, sums_k[h][n:]], axis=0)
                sums_v[h] = jnp.concatenate([sums_v[h][:n] + gv, sums_v[h][n:]], axis=0)
        dq[cols, pair] = jnp.concatenate(queries, axis=0).T
    dk[:, pair] = (jnp.concatenate(sums_k, axis=1) * LN2).astype(BF16)
    dv[:, pair] = jnp.concatenate(sums_v, axis=1).astype(BF16)

    @pl.when(step == pl.num_programs(0) - 1)
    def _():
        for copy in copies(0):
            copy.wait()
        for i in range(sources // ROWS):
            rows = slice(i * ROWS, (i + 1) * ROWS)
            total = nn(dk[rows, :], wf[1]) + nn(dv[rows, :], wf[2])
            if causal:
                total = total + nn(dq[rows, :], wf[0]) + g_ref[rows, :].astype(F32)
            out_ref[rows, :] = total.astype(BF16)
        if not causal:
            sum_ref[...] = jnp.zeros_like(sum_ref)
            for i in range(span // ROWS):
                rows = slice(i * ROWS, (i + 1) * ROWS)
                grad = nn(dq[rows, :], wf[0]) + g_ref[rows, :].astype(F32)
                normed = n_ref[rows, :].astype(F32)
                back = norm_back_rows(grad, normed, r_ref[rows, :], gain_ref[...])
                low_ref[rows, :] = back.astype(BF16)
                sum_ref[0:1, :] += sum_rows(grad * normed)
                sum_ref[1:2, :] += sum_rows(grad)


def attention_back(g, kept, pieces, norm, passed=None):
    e, hd, il, _ = kept
    causal = norm is None
    span, width = g.shape
    heads, sources, _ = e.shape
    arrays, homes = gather_homes(pieces)
    whole = lambda a: pl.BlockSpec(a.shape, lambda j: (0,) * a.ndim, pipeline_mode=pl.Buffered(1))
    operands = [g, e, hd, il]
    specs = [
        whole(g),
        pl.BlockSpec((2, sources, span), lambda j: (j, 0, 0)),
        pl.BlockSpec((4, 128, span), lambda j: (0, j, 0)),
        pl.BlockSpec((2, 1, span), lambda j: (j, 0, 0)),
    ]
    out_shape = [jax.ShapeDtypeStruct((sources, width), BF16)]
    if not causal:
        operands += list(norm)
        specs += [whole(a) for a in norm]
        out_shape += [jax.ShapeDtypeStruct((span, width), BF16), jax.ShapeDtypeStruct((8, width), F32)]
    out_specs = [pl.BlockSpec(s.shape, lambda j: (0, 0), pipeline_mode=pl.Buffered(1)) for s in out_shape]
    scratch = []
    if causal:
        arrays = arrays + [passed]
        out_shape.append(jax.ShapeDtypeStruct(passed.shape, passed.dtype))
        out_specs.append(ANY)
        scratch = [pltpu.VMEM(passed.shape, passed.dtype), pltpu.SemaphoreType.DMA((2,))]
    return pl.pallas_call(
        functools.partial(attention_back_kernel, causal, homes),
        grid=(heads // 2,),
        in_specs=specs + [ANY] * len(arrays),
        out_specs=out_specs,
        out_shape=out_shape,
        scratch_shapes=[
            pltpu.VMEM((4, width, width), BF16),
            pltpu.VMEM((width, span), BF16),
            pltpu.VMEM((span, width), BF16),
            pltpu.VMEM((sources, width), BF16),
            pltpu.VMEM((sources, width), BF16),
            pltpu.SemaphoreType.DMA((2, len(homes))),
        ]
        + scratch,
        compiler_params=pltpu.CompilerParams(vmem_limit_bytes=VMEM_LIMIT),
        cost_estimate=cost(40 * 10**9, 60 * 2**20),
        name="self_back" if causal else "cross_back",
    )(*operands, *arrays)


def copy_kernel(from_ref, to_ref):
    to_ref[...] = from_ref[...]


def copied(values):
    spec = pl.BlockSpec((1,) + values.shape[1:], lambda i: (i, 0, 0))
    return pl.pallas_call(
        copy_kernel,
        grid=(values.shape[0],),
        in_specs=[spec],
        out_specs=spec,
        out_shape=jax.ShapeDtypeStruct(values.shape, values.dtype),
        cost_estimate=cost(0, 4 * 2**20),
        name="copied",
    )(values)


def swap(values, name, bit):
    size = lax.axis_size(name)
    return lax.ppermute(values, name, [(i, i ^ bit) for i in range(size)])


def cross_swap(values, even, odd):
    size = lax.axis_size("tensor")
    pairs = []
    for d in range(lax.axis_size("dp")):
        for i in range(size):
            pairs.append((d * size + i, d * size + (i ^ (odd if d % 2 else even))))
    return lax.ppermute(values, ("dp", "tensor"), pairs)


def turn_over(values):
    return lax.all_to_all(values, "tensor", 0, 0, tiled=True)


def add_low(left, right):
    return (left.astype(F32) + right.astype(F32)).astype(BF16)


def after(values, *earlier):
    return lax.optimization_barrier((values, earlier))[0]


def near(what, own):
    with jax.named_scope(what + "_near"):
        return cross_swap(own, 1, 2)


def onward(what, shard, parts=2):
    where = lax.axis_index("dp")
    begin = 2 * (where % 2) + (where // 2 % 2 if parts == 1 else 0)
    half = lax.dynamic_slice_in_dim(shard, begin, parts, 0)
    with jax.named_scope(what + "_onward"):
        return cross_swap(half, 2, 1)


def core(what, values):
    with jax.named_scope(what + "_core"):
        return swap(values, "dp", 1)


def all_pieces(*arrays):
    return [(array, t) for array in arrays for t in range(array.shape[0])]


def whole_sequences(
    inputs,
    encoded,
    source_lengths,
    query_weight,
    key_weight,
    value_weight,
    output_weight,
    cross_query,
    cross_key,
    cross_value,
    cross_output,
    up_weight,
    down_weight,
    adapter_in,
    adapter_out,
    adapter_bias,
    adapter_shift,
    norm_gains,
    norm_shifts,
    output_grad,
):
    place = lax.axis_index("tensor")
    turn = 2 * (lax.axis_index("dp") % 2) + lax.axis_index("dp") // 2 % 2
    _, share, width = inputs.shape
    span = 4 * share
    units, extra = up_weight.shape[1] // 4, adapter_in.shape[1] // 4
    length = lax.dynamic_index_in_dim(source_lengths, place, 0, keepdims=False)
    ids = jnp.stack([place, turn, length]).astype(jnp.int32)
    gain = lambda j: norm_gains[j : j + 1]
    shift = lambda j: norm_shifts[j : j + 1]
    heads_shape = (4, output_weight.shape[0] // 4, width)
    units_shape = (2 * units + 2 * extra + 16, width)

    x = turn_over(inputs).reshape(span, width)
    self_own = pack(
        pack_heads_kernel, "pack_self", ids, heads_shape, query_weight, key_weight, value_weight, output_weight
    )
    shard = near("self", self_own)
    cross_own = pack(
        pack_heads_kernel,
        "pack_cross",
        after(ids, self_own),
        heads_shape,
        cross_query,
        cross_key,
        cross_value,
        cross_output,
    )
    feed_own = pack(
        pack_units_kernel,
        "pack_feed",
        after(ids, cross_own),
        units_shape,
        up_weight,
        down_weight,
        adapter_in,
        adapter_out,
        adapter_bias.reshape(1, -1),
    )
    x = after(x, feed_own)
    self_kept = attend_slots(ids, (0,), x, None, all_pieces(self_own), None)

    shard = after(shard, self_kept[0])
    half, core_shard = onward("self", shard), core("self", shard)
    source = turn_over(after(encoded, core_shard)).reshape(span, width)
    self_pieces = all_pieces(self_own, shard, core_shard)
    self_kept = attend_slots(ids, (1, 2), after(x, core_shard), None, self_pieces, self_kept)
    half = after(half, self_kept[0])
    self_pieces += all_pieces(half, core("self", half))
    cross_shard = near("cross", after(cross_own, source, half))
    self_kept = attend_slots(ids, (3,), x, None, self_pieces, self_kept)
    first, normed_one, scale_one = out_norm(self_kept[3], self_pieces, x, gain(0), shift(0))

    shard = after(cross_shard, first)
    half, core_shard = onward("cross", shard), core("cross", shard)
    feed_shard = near("feed", after(feed_own, shard))
    cross_pieces = all_pieces(cross_own, shard)
    cross_kept = attend_slots(ids, (0, 1), after(first, shard), source, cross_pieces, None)
    half = after(half, cross_kept[0])
    cross_pieces += all_pieces(core_shard, half, core("cross", half))
    cross_kept = attend_slots(ids, (2, 3), first, source, cross_pieces, cross_kept)
    second, normed_two, scale_two = out_norm(cross_kept[3], cross_pieces, first, gain(1), shift(1))

    shard = after(feed_shard, second)
    piece, core_shard = onward("feed", shard, 1), core("feed", shard)
    kept, rest = feed_slots(
        ids, (0,), after(second, shard), all_pieces(feed_own), None, None, units, extra
    )
    piece = after(piece, rest[0])
    with jax.named_scope("feed_far"):
        far_piece = swap(piece, "dp", 2)
    core_piece = core("feed", piece)
    feed_pieces = all_pieces(feed_own, shard, core_shard)
    grad = turn_over(after(output_grad, rest[0])).reshape(span, width)
    kept, rest = feed_slots(ids, (1, 2), second, feed_pieces, rest + kept, None, units, extra)
    far_piece = after(far_piece, rest[0], grad)
    feed_pieces += all_pieces(piece, far_piece, core_piece, core("feed", far_piece))
    norm = (adapter_shift.reshape(1, -1), gain(2), shift(2), grad)
    kept, rest = feed_slots(ids, (3,), second, feed_pieces, rest + kept, norm, units, extra)
    outcome, branch_low, sums_three = rest
    slopes, adapter_slopes, adapted_low = kept
    result = turn_over(outcome.reshape(4, share, width))
    a_low, grads = adapter_back(
        ids, branch_low, second, adapter_slopes, adapted_low, feed_pieces, units, extra
    )
    with jax.named_scope("adapter"):
        grads_there = [
            cross_swap(grads[1], 1, 2),
            cross_swap(grads[2], 2, 1),
            swap(grads[3], "tensor", 3),
        ]
    cross_low, sums_two = feed_back(
        ids,
        after(branch_low, a_low),
        slopes,
        a_low,
        feed_pieces,
        normed_two,
        scale_two,
        gain(1),
        units,
        extra,
    )
    adapter_sum = grads[0].astype(F32)
    for part in grads_there:
        adapter_sum = adapter_sum + part.astype(F32)
    adapter_sum = adapter_sum.astype(BF16)
    with jax.named_scope("adapter"):
        adapter_there = swap(adapter_sum, "dp", 1)
    encoded_back, self_low, sums_one = attention_back(
        after(cross_low, adapter_sum), cross_kept, cross_pieces, (normed_one, scale_one, gain(0))
    )
    adapter_sum = add_low(adapter_sum, after(adapter_there, self_low))
    encoded_result = turn_over(encoded_back.reshape(4, share, width))
    small = jnp.concatenate(
        [
            sums_one[0:1],
            sums_two[0:1],
            sums_three[0:1],
            sums_one[1:2],
            sums_two[1:2],
            sums_three[1:2],
            sums_three[2:3],
            jnp.zeros((1, width), F32),
        ],
        axis=0,
    )
    with jax.named_scope("small"):
        small_there = [swap(small, "tensor", k) for k in (1, 2, 3)]
    with jax.named_scope("adapter"):
        adapter_there = swap(adapter_sum, "dp", 2)
    input_back, result = attention_back(
        after(self_low, small, adapter_sum), self_kept, self_pieces, None, result
    )
    input_back, small_there, adapter_there, encoded_result = lax.optimization_barrier(
        (input_back, small_there, adapter_there, encoded_result)
    )
    input_result = turn_over(input_back.reshape(4, share, width))
    for part in small_there:
        small = small + part
    adapter_sum = add_low(adapter_sum, adapter_there)
    bit = 4
    while bit < lax.axis_size("dp"):
        with jax.named_scope("adapter"):
            adapter_sum = add_low(adapter_sum, swap(adapter_sum, "dp", bit))
        bit *= 2
    bit = 1
    while bit < lax.axis_size("dp"):
        with jax.named_scope("small"):
            small = small + swap(small, "dp", bit)
        bit *= 2
    encoded_result = copied(encoded_result)
    adapter_sum = adapter_sum.astype(F32)
    size = 4 * extra
    return (
        result,
        input_result,
        encoded_result,
        adapter_sum[:size].T,
        adapter_sum[size : 2 * size],
        jnp.sum(adapter_sum[2 * size :, :size], axis=0),
        small[6],
        small[0:3],
        small[3:6],
    )


def gelu_tanh(values):
    return jax.nn.gelu(values, approximate=True)


def multiply(left, right):
    return jnp.dot(left, right, preferred_element_type=jnp.float32)


def multiply_by_transpose(left, right):
    return lax.dot_general(
        left, right, (((1,), (1,)), ((), ())), preferred_element_type=jnp.float32
    )


def multiply_transposed_left(left, right):
    return lax.dot_general(
        left, right, (((0,), (0,)), ((), ())), preferred_element_type=jnp.float32
    )


def layer_norm(values, gain, shift):
    center = values - jnp.mean(values, axis=-1, keepdims=True)
    scale = lax.rsqrt(jnp.mean(center * center, axis=-1, keepdims=True) + 1e-05)
    normed = center * scale
    return (normed * gain + shift, normed, scale)


def norm_back(grad, normed, scale, gain):
    inner = grad * gain
    middle = jnp.mean(inner, axis=-1, keepdims=True)
    along = jnp.mean(inner * normed, axis=-1, keepdims=True)
    return (
        scale * (inner - middle - normed * along),
        jnp.sum(grad * normed, axis=(0, 1)),
        jnp.sum(grad, axis=(0, 1)),
    )


def attend(query_low, key_low, value_low, keep_for):
    count = query_low.shape[1]
    block = min(512, count)
    factor = query_low.shape[-1] ** (-0.5)
    contexts = []
    totals = []
    for first in range(0, count, block):
        scores = (
            jnp.einsum(
                "sqhe,skhe->shqk",
                query_low[:, first : first + block],
                key_low,
                preferred_element_type=jnp.float32,
            )
            * factor
        )
        scores = jnp.where(keep_for(first, block), scores, -1000000000.0)
        top_score = jnp.max(scores, axis=-1, keepdims=True)
        weights = jnp.exp(scores - top_score)
        denom = jnp.sum(weights, axis=-1, keepdims=True)
        probs_low = (weights / denom).astype(jnp.bfloat16)
        contexts.append(
            jnp.einsum("shqk,skhe->sqhe", probs_low, value_low, preferred_element_type=jnp.float32)
        )
        totals.append(top_score + jnp.log(denom))
    return (jnp.concatenate(contexts, axis=1), jnp.concatenate(totals, axis=2))


def attend_back(query_low, key_low, value_low, grad_low, totals, keep_for):
    count = query_low.shape[1]
    block = min(512, count)
    factor = query_low.shape[-1] ** (-0.5)
    key_grad = jnp.zeros(key_low.shape, jnp.float32)
    value_grad = jnp.zeros(value_low.shape, jnp.float32)
    query_grads = []
    for first in range(0, count, block):
        query_part = query_low[:, first : first + block]
        grad_part = grad_low[:, first : first + block]
        scores = (
            jnp.einsum("sqhe,skhe->shqk", query_part, key_low, preferred_element_type=jnp.float32)
            * factor
        )
        scores = jnp.where(keep_for(first, block), scores, -1000000000.0)
        probs = jnp.exp(scores - totals[:, :, first : first + block])
        probs_low = probs.astype(jnp.bfloat16)
        prob_grad = jnp.einsum(
            "sqhe,skhe->shqk", grad_part, value_low, preferred_element_type=jnp.float32
        )
        value_grad = value_grad + jnp.einsum(
            "shqk,sqhe->skhe", probs_low, grad_part, preferred_element_type=jnp.float32
        )
        along = jnp.sum(prob_grad * probs, axis=-1, keepdims=True)
        score_grad = (probs * (prob_grad - along)).astype(jnp.bfloat16)
        query_grads.append(
            jnp.einsum("shqk,skhe->sqhe", score_grad, key_low, preferred_element_type=jnp.float32)
            * factor
        )
        key_grad = (
            key_grad
            + jnp.einsum(
                "shqk,sqhe->skhe", score_grad, query_part, preferred_element_type=jnp.float32
            )
            * factor
        )
    return (jnp.concatenate(query_grads, axis=1), key_grad, value_grad)


def local(
    inputs,
    encoded,
    source_lengths,
    query_weight,
    key_weight,
    value_weight,
    output_weight,
    cross_query,
    cross_key,
    cross_value,
    cross_output,
    up_weight,
    down_weight,
    adapter_in,
    adapter_out,
    adapter_bias,
    adapter_shift,
    norm_gains,
    norm_shifts,
    output_grad,
):
    parts = lax.axis_size("tensor")
    place = lax.axis_index("tensor")
    sequences, share, width = inputs.shape
    length = share * parts
    rows = sequences * length
    heads = query_weight.shape[1] // HEAD
    local_width = heads * HEAD
    whole_inputs, whole_encoded = (
        lax.all_gather(inputs, "tensor", axis=1, tiled=True),
        lax.all_gather(encoded, "tensor", axis=1, tiled=True),
    )
    sources = whole_encoded.shape[1]
    flat_inputs = whole_inputs.reshape(rows, width)
    flat_encoded = whole_encoded.reshape(sequences * sources, width)

    def split_heads(values, count):
        return values.astype(jnp.bfloat16).reshape(sequences, count, heads, HEAD)

    def causal(first, block):
        query_pos = first + lax.broadcasted_iota(jnp.int32, (block, length), 0)
        key_pos = lax.broadcasted_iota(jnp.int32, (block, length), 1)
        return (key_pos <= query_pos)[None, None]

    def padded(first, block):
        key_pos = lax.broadcasted_iota(jnp.int32, (sequences, 1, 1, sources), 3)
        return key_pos < source_lengths[:, None, None, None]

    self_query = split_heads(multiply(flat_inputs, query_weight), length)
    self_key = split_heads(multiply(flat_inputs, key_weight), length)
    self_value = split_heads(multiply(flat_inputs, value_weight), length)
    self_context, self_totals = attend(self_query, self_key, self_value, causal)
    self_context_low = self_context.astype(jnp.bfloat16).reshape(rows, local_width)
    self_partial = multiply(self_context_low, output_weight).reshape(sequences, length, width)
    self_full = lax.psum(self_partial.astype(jnp.bfloat16), "tensor").astype(jnp.float32)
    first_full, normed_full, scale_full = layer_norm(
        whole_inputs.astype(jnp.float32) + self_full, norm_gains[0], norm_shifts[0]
    )
    first_low = first_full.astype(jnp.bfloat16)
    first_share = lax.dynamic_slice_in_dim(first_full, place * share, share, 1)
    normed_one = lax.dynamic_slice_in_dim(normed_full, place * share, share, 1)
    scale_one = lax.dynamic_slice_in_dim(scale_full, place * share, share, 1)
    flat_first = first_low.reshape(rows, width)
    cross_q = split_heads(multiply(flat_first, cross_query), length)
    cross_k = split_heads(multiply(flat_encoded, cross_key), sources)
    cross_v = split_heads(multiply(flat_encoded, cross_value), sources)
    cross_context, cross_totals = attend(cross_q, cross_k, cross_v, padded)
    cross_context_low = cross_context.astype(jnp.bfloat16).reshape(rows, local_width)
    cross_partial = multiply(cross_context_low, cross_output).reshape(sequences, length, width)
    cross_share = lax.psum_scatter(
        cross_partial.astype(jnp.bfloat16), "tensor", scatter_dimension=1, tiled=True
    ).astype(jnp.float32)
    second_share, normed_two, scale_two = layer_norm(
        first_share + cross_share, norm_gains[1], norm_shifts[1]
    )
    second_low = lax.all_gather(second_share.astype(jnp.bfloat16), "tensor", axis=1, tiled=True)
    flat_second = second_low.reshape(rows, width)
    hidden = multiply(flat_second, up_weight)
    hidden_low = gelu_tanh(hidden).astype(jnp.bfloat16)
    adapted = multiply(flat_second, adapter_in) + adapter_bias
    adapted_low = gelu_tanh(adapted).astype(jnp.bfloat16)
    branch_partial = multiply(hidden_low, down_weight) + 4.0 * multiply(adapted_low, adapter_out)
    branch_share = lax.psum_scatter(
        branch_partial.reshape(sequences, length, width).astype(jnp.bfloat16),
        "tensor",
        scatter_dimension=1,
        tiled=True,
    ).astype(jnp.float32)
    third_input = second_share + branch_share + 4.0 * adapter_shift
    outcome, normed_three, scale_three = layer_norm(third_input, norm_gains[2], norm_shifts[2])
    grad_three, gain_grad_three, shift_grad_three = norm_back(
        output_grad.astype(jnp.float32), normed_three, scale_three, norm_gains[2]
    )
    shift_grad_adapter = 4.0 * jnp.sum(grad_three, axis=(0, 1))
    branch_grad = lax.all_gather(
        grad_three.astype(jnp.bfloat16), "tensor", axis=1, tiled=True
    ).reshape(rows, width)
    hidden_grad = multiply_by_transpose(branch_grad, down_weight)
    hidden_unused, hidden_pull = jax.vjp(gelu_tanh, hidden)
    hidden_grad_low = hidden_pull(hidden_grad)[0].astype(jnp.bfloat16)
    adapted_grad = 4.0 * multiply_by_transpose(branch_grad, adapter_out)
    adapted_unused, adapted_pull = jax.vjp(gelu_tanh, adapted)
    adapted_grad = adapted_pull(adapted_grad)[0]
    bias_grad = jnp.sum(adapted_grad, axis=0)
    adapted_grad_low = adapted_grad.astype(jnp.bfloat16)
    in_grad = multiply_transposed_left(flat_second, adapted_grad_low)
    out_grad = 4.0 * multiply_transposed_left(adapted_low, branch_grad)
    second_partial = multiply_by_transpose(hidden_grad_low, up_weight) + multiply_by_transpose(
        adapted_grad_low, adapter_in
    )
    second_grad = grad_three + lax.psum_scatter(
        second_partial.reshape(sequences, length, width).astype(jnp.bfloat16),
        "tensor",
        scatter_dimension=1,
        tiled=True,
    ).astype(jnp.float32)
    grad_two, gain_grad_two, shift_grad_two = norm_back(
        second_grad, normed_two, scale_two, norm_gains[1]
    )
    cross_grad = lax.all_gather(
        grad_two.astype(jnp.bfloat16), "tensor", axis=1, tiled=True
    ).reshape(rows, width)
    cross_context_grad = multiply_by_transpose(cross_grad, cross_output).astype(jnp.bfloat16)
    cross_context_grad = cross_context_grad.reshape(sequences, length, heads, HEAD)
    cq_grad, ck_grad, cv_grad = attend_back(
        cross_q, cross_k, cross_v, cross_context_grad, cross_totals, padded
    )
    first_partial = multiply_by_transpose(
        cq_grad.astype(jnp.bfloat16).reshape(rows, local_width), cross_query
    )
    encoded_partial = multiply_by_transpose(
        ck_grad.astype(jnp.bfloat16).reshape(sequences * sources, local_width), cross_key
    ) + multiply_by_transpose(
        cv_grad.astype(jnp.bfloat16).reshape(sequences * sources, local_width), cross_value
    )
    first_back, encoded_share = (
        lax.psum_scatter(
            first_partial.reshape(sequences, length, width).astype(jnp.bfloat16),
            "tensor",
            scatter_dimension=1,
            tiled=True,
        ).astype(jnp.float32),
        lax.psum_scatter(
            encoded_partial.reshape(sequences, sources, width).astype(jnp.bfloat16),
            "tensor",
            scatter_dimension=1,
            tiled=True,
        ).astype(jnp.float32),
    )
    grad_one, gain_grad_one, shift_grad_one = norm_back(
        grad_two + first_back, normed_one, scale_one, norm_gains[0]
    )
    self_grad = lax.all_gather(grad_one.astype(jnp.bfloat16), "tensor", axis=1, tiled=True).reshape(
        rows, width
    )
    self_context_grad = multiply_by_transpose(self_grad, output_weight).astype(jnp.bfloat16)
    self_context_grad = self_context_grad.reshape(sequences, length, heads, HEAD)
    sq_grad, sk_grad, sv_grad = attend_back(
        self_query, self_key, self_value, self_context_grad, self_totals, causal
    )
    input_partial = (
        multiply_by_transpose(sq_grad.astype(jnp.bfloat16).reshape(rows, local_width), query_weight)
        + multiply_by_transpose(sk_grad.astype(jnp.bfloat16).reshape(rows, local_width), key_weight)
        + multiply_by_transpose(
            sv_grad.astype(jnp.bfloat16).reshape(rows, local_width), value_weight
        )
    )
    small_grads = jnp.stack(
        [
            gain_grad_one,
            gain_grad_two,
            gain_grad_three,
            shift_grad_one,
            shift_grad_two,
            shift_grad_three,
            shift_grad_adapter,
        ]
    )
    spread = jnp.broadcast_to(small_grads[:, None, :], (7, parts, width))
    input_back, small_back = (
        lax.psum_scatter(
            input_partial.reshape(sequences, length, width).astype(jnp.bfloat16),
            "tensor",
            scatter_dimension=1,
            tiled=True,
        ).astype(jnp.float32),
        lax.psum_scatter(
            spread.astype(jnp.bfloat16), "tensor", scatter_dimension=1, tiled=True
        ).astype(jnp.float32),
    )
    input_result = (grad_one + input_back).astype(jnp.bfloat16)
    encoded_result = encoded_share.astype(jnp.bfloat16)
    in_total, out_total, bias_total, small_total = (
        lax.psum(in_grad.astype(jnp.bfloat16), "dp").astype(jnp.float32),
        lax.psum(out_grad.astype(jnp.bfloat16), "dp").astype(jnp.float32),
        lax.psum(bias_grad.astype(jnp.bfloat16), "dp").astype(jnp.float32),
        lax.psum(small_back[:, 0].astype(jnp.bfloat16), "dp").astype(jnp.float32),
    )
    return (
        outcome.astype(jnp.bfloat16),
        input_result,
        encoded_result,
        in_total,
        out_total,
        bias_total,
        small_total[6],
        small_total[0:3],
        small_total[3:6],
    )


def solution(mesh):
    placed = (
        P("dp", "tensor", None),
        P("dp", "tensor", None),
        P("dp"),
        P(None, "tensor"),
        P(None, "tensor"),
        P(None, "tensor"),
        P("tensor", None),
        P(None, "tensor"),
        P(None, "tensor"),
        P(None, "tensor"),
        P("tensor", None),
        P(None, "tensor"),
        P("tensor", None),
        P(None, "tensor"),
        P("tensor", None),
        P("tensor"),
        P(),
        P(),
        P(),
        P("dp", "tensor", None),
    )
    suits = mesh.shape["tensor"] == 4 and mesh.shape["dp"] in (4, 8, 16, 32)

    def layer(*arrays):
        if suits and arrays[0].shape[:2] == (4, ROWS) and arrays[1].shape[:2] == (4, ROWS):
            return whole_sequences(*arrays)
        return local(*arrays)

    return jax.shard_map(
        layer,
        mesh=mesh,
        in_specs=placed,
        out_specs=(
            P("dp", "tensor", None),
            P("dp", "tensor", None),
            P("dp", "tensor", None),
            P(None, "tensor"),
            P("tensor", None),
            P("tensor"),
            P(),
            P(),
            P(),
        ),
        check_vma=False,
    )
```

```python
import functools
import jax
import jax.numpy as jnp
from jax import lax
from jax.experimental import pallas as pl
from jax.experimental.pallas import tpu as pltpu
from jax.sharding import PartitionSpec as P

HEAD = 64
F32 = jnp.float32
BF16 = jnp.bfloat16
LOG2E = 1.4426950408889634
LN2 = 0.6931471805599453
VMEM_LIMIT = 60 * 2**20
ROWS = 256
BLOCK = 256
ANY = pl.BlockSpec(memory_space=pl.ANY)
SMEM = pl.BlockSpec(memory_space=pltpu.SMEM)


def cost(flops, moved):
    return pl.CostEstimate(flops=int(flops * SHARE), bytes_accessed=int(moved * SHARE), transcendentals=0)


SHARE = 1.0


def nn(left, right):
    return lax.dot_general(left, right, (((1,), (0,)), ((), ())), preferred_element_type=F32)


def nt(left, right):
    return lax.dot_general(left, right, (((1,), (1,)), ((), ())), preferred_element_type=F32)


def tn(left, right):
    return lax.dot_general(left, right, (((0,), (0,)), ((), ())), preferred_element_type=F32)


def norm_rows(values):
    center = values - jnp.mean(values, axis=-1, keepdims=True)
    scale = lax.rsqrt(jnp.mean(center * center, axis=-1, keepdims=True) + 1e-05)
    return center * scale, scale


def norm_back_rows(grad, normed, scale, gain):
    inner = grad * gain
    middle = jnp.mean(inner, axis=-1, keepdims=True)
    along = jnp.mean(inner * normed, axis=-1, keepdims=True)
    return scale * (inner - middle - normed * along)


def gelu_and_slope(v):
    root = 0.7978845608028654
    square = v * v
    t = jnp.tanh(v * (root + (root * 0.044715) * square))
    half = 0.5 + 0.5 * t
    slope = half + (v * half) * (1.0 - t) * (root + (3.0 * root * 0.044715) * square)
    return v * half, slope


def head_rows(h):
    return slice(h * HEAD, (h + 1) * HEAD)


def natural(turn, p):
    slot, t = p // 4, p % 4
    return t ^ turn if slot == 3 else t


def sum_rows(values):
    return jnp.sum(values, axis=0, keepdims=True)


def pack_heads_kernel(ids_ref, q_ref, k_ref, v_ref, o_ref, own_ref):
    part = own_ref.shape[2]
    for m, ref in enumerate((q_ref, k_ref, v_ref, o_ref)):
        values = ref[...] if m == 3 else ref[...].T
        for t in range(4):
            own_ref[t, m] = values[t * part : (t + 1) * part]


def pack_units_kernel(ids_ref, up_ref, down_ref, ain_ref, aout_ref, bias_ref, own_ref):
    units, extra = down_ref.shape[0] // 4, aout_ref.shape[0] // 4
    turned = ain_ref[...].T
    bias = bias_ref[...]
    begin = 2 * units + 2 * extra
    for t in range(4):
        cols = slice(t * units, (t + 1) * units)
        own_ref[t, :units] = up_ref[:, cols].T
        own_ref[t, units : 2 * units] = down_ref[cols, :]
        own_ref[t, 2 * units : 2 * units + extra] = turned[t * extra : (t + 1) * extra]
        own_ref[t, 2 * units + extra : begin] = aout_ref[t * extra : (t + 1) * extra, :]
        own_ref[t, begin:, : 4 * extra] = split_lines(bias)


def split_lines(values):
    rows, rest = [], values
    for _ in range(3):
        low = rest.astype(BF16)
        rows.append(low)
        rest = rest - low.astype(F32)
    rows.append(jnp.zeros((13,) + values.shape[1:], BF16))
    return jnp.concatenate(rows, axis=0)


def pack(kernel, name, ids, own_shape, *weights):
    vmem = pl.BlockSpec(memory_space=pltpu.VMEM)
    return pl.pallas_call(
        kernel,
        in_specs=[SMEM] + [vmem] * len(weights),
        out_specs=vmem,
        out_shape=jax.ShapeDtypeStruct((4,) + own_shape, BF16),
        compiler_params=pltpu.CompilerParams(vmem_limit_bytes=VMEM_LIMIT),
        cost_estimate=cost(0, 8 * 2**20),
        name=name,
    )(ids, *weights)


def attend_kernel(causal, count, first, homes, ids_ref, *refs):
    refs = list(refs)
    xq_hbm = refs.pop(0)
    xkv_hbm = xq_hbm if causal else refs.pop(0)
    sources_of = [refs.pop(0) for _ in range(len(set(n for n, _ in homes)))]
    if not first:
        refs = refs[4:]
    e_ref, hd_ref, il_ref, ctx_ref, xq, xkv, weights, qkv, x_sems, w_sems = refs
    if causal:
        xkv = xq
    step = pl.program_id(0)
    span, sources = xq.shape[0], xkv.shape[0]
    part = weights.shape[2] // 4

    def weight_copy(s, t):
        n, index = homes[4 * s + t]
        return pltpu.make_async_copy(
            sources_of[n].at[index, pl.ds(0, 3)],
            weights.at[s, :, pl.ds(t * part, part), :],
            w_sems.at[4 * s + t],
        )

    x_copies = [pltpu.make_async_copy(xq_hbm, xq, x_sems.at[0])]
    if not causal:
        x_copies.append(pltpu.make_async_copy(xkv_hbm, xkv, x_sems.at[1]))

    @pl.when(step == 0)
    def _():
        for t in range(4):
            weight_copy(0, t).start()
        for copy in x_copies:
            copy.start()
        for s in range(1, count):
            for t in range(4):
                weight_copy(s, t).start()
        for copy in x_copies:
            copy.wait()

    for s in range(count):

        @pl.when(step == 2 * s)
        def _():
            for t in range(4):
                weight_copy(s, t).wait()
            qkv[0] = (nt(weights[s, 0], xq[...]) * (LOG2E * HEAD**-0.5)).astype(BF16)
            qkv[1] = nt(weights[s, 1], xkv[...]).astype(BF16)
            qkv[2] = nt(weights[s, 2], xkv[...]).astype(BF16)

    pair = pl.ds(pl.multiple_of((step % 2) * 128, 128), 128)
    q2, k2, v2 = qkv[0, pair, :], qkv[1, pair, :], qkv[2, pair, :]
    hd_ref[0], hd_ref[1], hd_ref[2] = q2, k2, v2
    block = min(BLOCK, span)
    work = [(i, h) for i in range(span // block) for h in range(2)]

    def reach(i):
        return (i + 1) * block if causal else sources

    def score(i, h):
        return tn(k2[head_rows(h), : reach(i)], q2[head_rows(h), i * block : (i + 1) * block])

    ahead = 2 if causal else 4
    waiting = [score(i, h) for i, h in work[:ahead]]
    for number, (i, h) in enumerate(work):
        n, cols = reach(i), slice(i * block, (i + 1) * block)
        s = waiting.pop(0)
        if number + ahead < len(work):
            waiting.append(score(*work[number + ahead]))
        if causal:
            key = lax.broadcasted_iota(jnp.int32, (block, block), 0)
            query = lax.broadcasted_iota(jnp.int32, (block, block), 1)
            tail = jnp.where(key <= query, s[n - block :], -1e9)
            s = jnp.concatenate([s[: n - block], tail], axis=0) if n > block else tail
        else:
            key = lax.broadcasted_iota(jnp.int32, (n, block), 0)
            s = jnp.where(key < ids_ref[2], s, -1e9)
        e = jnp.exp2(s - jnp.max(s, axis=0, keepdims=True))
        inverse = 1.0 / jnp.sum(e, axis=0, keepdims=True)
        low = e.astype(BF16)
        e_ref[h, :n, cols] = low
        il_ref[h, :, cols] = inverse
        context = (nn(v2[head_rows(h), :n], low) * inverse).astype(BF16)
        hd_ref[3, head_rows(h), cols] = context
        contexts = [context] if h == 0 else contexts + [context]
        if h == 1:
            ctx_ref[cols, :] = jnp.concatenate(contexts, axis=0).T


def gather_homes(pieces):
    arrays, homes = [], []
    for array, index in pieces:
        where = [n for n, known in enumerate(arrays) if known is array]
        if not where:
            arrays.append(array)
            where = [len(arrays) - 1]
        homes.append((where[0], index))
    return arrays, tuple(homes)


def attend_slots(ids, slots, xq, xkv, pieces, before):
    causal = xkv is None
    span, width = xq.shape
    sources = span if causal else xkv.shape[0]
    heads = width // HEAD
    count, base = len(slots), 2 * slots[0]
    arrays, homes = gather_homes([pieces[4 * s + t] for s in slots for t in range(4)])
    part = arrays[0].shape[2]
    first = before is None
    operands = [ids, xq] + ([] if causal else [xkv]) + arrays
    specs = [SMEM] + [ANY] * (len(operands) - 1)
    aliases = {}
    if not first:
        aliases = {len(operands) + n: n for n in range(4)}
        operands += list(before)
        specs += [ANY] * 4
    return pl.pallas_call(
        functools.partial(attend_kernel, causal, count, first, homes),
        grid=(2 * count,),
        in_specs=specs,
        out_specs=(
            pl.BlockSpec((2, sources, span), lambda j: (base + j, 0, 0)),
            pl.BlockSpec((4, 128, span), lambda j: (0, base + j, 0)),
            pl.BlockSpec((2, 1, span), lambda j: (base + j, 0, 0)),
            pl.BlockSpec((span, 128), lambda j: (0, base + j)),
        ),
        out_shape=(
            jax.ShapeDtypeStruct((heads, sources, span), BF16),
            jax.ShapeDtypeStruct((4, width, span), BF16),
            jax.ShapeDtypeStruct((heads, 1, span), F32),
            jax.ShapeDtypeStruct((span, width), BF16),
        ),
        scratch_shapes=[
            pltpu.VMEM((span, width), BF16),
            pltpu.VMEM((16, 128) if causal else (sources, width), BF16),
            pltpu.VMEM((count, 3, 4 * part, width), BF16),
            pltpu.VMEM((3, 4 * part, max(span, sources)), BF16),
            pltpu.SemaphoreType.DMA((2,)),
            pltpu.SemaphoreType.DMA((4 * count,)),
        ],
        input_output_aliases=aliases,
        compiler_params=pltpu.CompilerParams(vmem_limit_bytes=VMEM_LIMIT),
        cost_estimate=cost(count * 10 * 10**9, count * 12 * 2**20),
        name="self_attend" if causal else "cross_attend",
    )(*operands)


def out_norm_kernel(homes, *refs):
    refs = list(refs)
    ctx_ref, x_ref, gain_ref, shift_ref = refs[:4]
    sources = refs[4:-5]
    low_ref, n_ref, r_ref, wo, sems = refs[-5:]
    part = wo.shape[0] // len(homes)
    copies = [
        pltpu.make_async_copy(sources[n].at[index, 3], wo.at[pl.ds(p * part, part), :], sems.at[p])
        for p, (n, index) in enumerate(homes)
    ]

    @pl.when(pl.program_id(0) == 0)
    def _():
        for copy in copies:
            copy.start()
        for copy in copies:
            copy.wait()

    rows_here = ctx_ref.shape[0]
    for i in range(rows_here // ROWS):
        rows = slice(i * ROWS, (i + 1) * ROWS)
        total = nn(ctx_ref[rows, :], wo[...]) + x_ref[rows, :].astype(F32)
        normed, scale = norm_rows(total)
        low_ref[rows, :] = (normed * gain_ref[...] + shift_ref[...]).astype(BF16)
        n_ref[rows, :] = normed.astype(BF16)
        r_ref[rows, :] = scale


def out_norm(ctx, pieces, residual, gain, shift):
    span, width = ctx.shape
    arrays, homes = gather_homes(pieces)
    block = min(512, span)
    rows = lambda w: pl.BlockSpec((block, w), lambda i: (i, 0))
    line = pl.BlockSpec((1, width), lambda i: (0, 0))
    return pl.pallas_call(
        functools.partial(out_norm_kernel, homes),
        grid=(span // block,),
        in_specs=[rows(width), rows(width), line, line] + [ANY] * len(arrays),
        out_specs=(rows(width), rows(width), rows(1)),
        out_shape=(
            jax.ShapeDtypeStruct((span, width), BF16),
            jax.ShapeDtypeStruct((span, width), BF16),
            jax.ShapeDtypeStruct((span, 1), F32),
        ),
        scratch_shapes=[pltpu.VMEM((width, width), BF16), pltpu.SemaphoreType.DMA((len(homes),))],
        compiler_params=pltpu.CompilerParams(vmem_limit_bytes=VMEM_LIMIT),
        cost_estimate=cost(2 * span * width * width, 10 * 2**20),
        name="out_norm",
    )(ctx, residual, gain, shift, *arrays)


def feed_kernel(slots, first, last, units, extra, homes, ids_ref, *refs):
    count = len(slots)
    refs = list(refs)
    x_ref = refs.pop(0)
    sources = [refs.pop(0) for _ in range(len(set(n for n, _ in homes)))]
    if last:
        shift_a_ref, gain_ref, shift_ref, grad_ref = [refs.pop(0) for _ in range(4)]
    if not first:
        acc_hbm = refs.pop(0)
        refs = refs[3:]
    gp_ref, gpa_ref, alow_ref = [refs.pop(0) for _ in range(3)]
    if last:
        out_ref, low_ref, sum_ref = [refs.pop(0) for _ in range(3)]
    acc, up, down, ain, aout, bias, w_sems, b_sems, acc_sem = refs
    step = pl.program_id(0)
    span = x_ref.shape[0]

    def piece_copies(p):
        n, index = homes[p]
        there = 4 * (p // 4) + natural(ids_ref[1], 4 * slots[0] + p)
        parts = (
            (0, units, up, p),
            (units, units, down, p),
            (2 * units, extra, ain, there),
            (2 * units + extra, extra, aout, there),
        )
        found = [
            pltpu.make_async_copy(
                sources[n].at[index, pl.ds(begin, size), :],
                held.at[pl.ds(to * size, size), :],
                w_sems.at[p, m],
            )
            for m, (begin, size, held, to) in enumerate(parts)
        ]
        if p % 4 == 0:
            found.append(
                pltpu.make_async_copy(
                    sources[n].at[index, pl.ds(2 * units + 2 * extra, 16), pl.ds(0, 4 * extra)],
                    bias.at[p // 4],
                    b_sems.at[p // 4],
                )
            )
        return found

    def acc_copy():
        return pltpu.make_async_copy(acc_hbm, acc, acc_sem)

    @pl.when(step == 0)
    def _():
        for p in range(4 * count):
            for copy in piece_copies(p):
                copy.start()
            if p == 3 and not first:
                acc_copy().start()

    half = min(512, span)
    for s in range(count):

        @pl.when(step == s)
        def _():
            for p in range(4 * s, 4 * s + 4):
                for copy in piece_copies(p):
                    copy.wait()
            wide = slice(4 * units * s, 4 * units * (s + 1))
            small = slice(4 * extra * s, 4 * extra * (s + 1))
            shift_a = sum_rows(bias[s].astype(F32))
            for i in range(span // half):
                rows = slice(i * half, (i + 1) * half)
                x = x_ref[rows, :]
                a, slope = gelu_and_slope(nt(x, ain[small, :]) + shift_a)
                a_low = a.astype(BF16)
                alow_ref[rows, :] = a_low
                gpa_ref[rows, :] = slope.astype(BF16)
                h, slope = gelu_and_slope(nt(x, up[wide, :]))
                gp_ref[rows, :] = slope.astype(BF16)
                total = nn(h.astype(BF16), down[wide, :]) + 4.0 * nn(a_low, aout[small, :])
                if s == 0 and i == 0 and not first:
                    acc_copy().wait()
                acc[rows, :] = total if first and s == 0 else acc[rows, :] + total

    if last:

        @pl.when(step == pl.num_programs(0) - 1)
        def _():
            sum_ref[...] = jnp.zeros_like(sum_ref)
            for i in range(span // ROWS):
                rows = slice(i * ROWS, (i + 1) * ROWS)
                total = acc[rows, :] + x_ref[rows, :].astype(F32) + 4.0 * shift_a_ref[...]
                normed, scale = norm_rows(total)
                out_ref[rows, :] = (normed * gain_ref[...] + shift_ref[...]).astype(BF16)
                grad = grad_ref[rows, :].astype(F32)
                back = norm_back_rows(grad, normed, scale, gain_ref[...])
                low_ref[rows, :] = back.astype(BF16)
                sum_ref[0:1, :] += sum_rows(grad * normed)
                sum_ref[1:2, :] += sum_rows(grad)
                sum_ref[2:3, :] += 4.0 * sum_rows(back)


def feed_slots(ids, slots, x, pieces, before, norm, units, extra):
    span, width = x.shape
    first, last = before is None, norm is not None
    count = len(slots)
    whole = lambda a: pl.BlockSpec(a.shape, lambda j: (0,) * a.ndim, pipeline_mode=pl.Buffered(1))
    arrays, homes = gather_homes([pieces[4 * s + t] for s in slots for t in range(4)])
    operands = [ids, x] + arrays
    specs = [SMEM, whole(x)] + [ANY] * len(arrays)
    if last:
        operands += list(norm)
        specs += [whole(a) for a in norm]
    kept_shape = [
        jax.ShapeDtypeStruct((span, 16 * units), BF16),
        jax.ShapeDtypeStruct((span, 16 * extra), BF16),
        jax.ShapeDtypeStruct((span, 16 * extra), BF16),
    ]
    kept_specs = [
        pl.BlockSpec((span, 4 * units), lambda j: (0, slots[0] + j)),
        pl.BlockSpec((span, 4 * extra), lambda j: (0, slots[0] + j)),
        pl.BlockSpec((span, 4 * extra), lambda j: (0, slots[0] + j)),
    ]
    aliases = {}
    if not first:
        aliases = {len(operands) + 1 + n: n for n in range(3)}
        operands += list(before)
        specs += [ANY] * 4
    total = jax.ShapeDtypeStruct((span, width), F32)
    once = lambda s: pl.BlockSpec(s.shape, lambda j: (0,) * len(s.shape), pipeline_mode=pl.Buffered(1))
    if last:
        low = jax.ShapeDtypeStruct((span, width), BF16)
        more = [low, low, jax.ShapeDtypeStruct((8, width), F32)]
        scratch = [pltpu.VMEM((span, width), F32)]
    else:
        more, scratch = [total], []
    outs = pl.pallas_call(
        functools.partial(feed_kernel, slots, first, last, units, extra, homes),
        grid=(count,),
        in_specs=specs,
        out_specs=kept_specs + [once(s) for s in more],
        out_shape=kept_shape + more,
        scratch_shapes=scratch
        + [
            pltpu.VMEM((count * 4 * units, width), BF16),
            pltpu.VMEM((count * 4 * units, width), BF16),
            pltpu.VMEM((count * 4 * extra, width), BF16),
            pltpu.VMEM((count * 4 * extra, width), BF16),
            pltpu.VMEM((count, 16, 4 * extra), BF16),
            pltpu.SemaphoreType.DMA((4 * count, 4)),
            pltpu.SemaphoreType.DMA((count,)),
            pltpu.SemaphoreType.DMA,
        ],
        input_output_aliases=aliases,
        compiler_params=pltpu.CompilerParams(vmem_limit_bytes=VMEM_LIMIT),
        cost_estimate=cost(count * 6 * 10**9, count * 14 * 2**20),
        name="feed",
    )(*operands)
    kept, rest = list(outs[:3]), list(outs[3:])
    return kept, rest


def adapter_back_kernel(extra, units, homes, ids_ref, *refs):
    refs = list(refs)
    g_ref, x_ref, gpa_ref, alow_ref = refs[:4]
    low_ref, *slot_refs, aout, sems = refs[-7:]
    sources = refs[4:-7]
    begin = 2 * units + extra
    copies = []
    for p, (n, index) in enumerate(homes):
        there = 4 * (p // 4) + natural(ids_ref[1], p)
        copies.append(
            pltpu.make_async_copy(
                sources[n].at[index, pl.ds(begin, extra), :],
                aout.at[pl.ds(there * extra, extra), :],
                sems.at[p],
            )
        )
    for copy in copies:
        copy.start()
    for copy in copies:
        copy.wait()
    g = g_ref[...]
    a = 4.0 * nt(g, aout[...]) * gpa_ref[...].astype(F32)
    bias = sum_rows(a)
    a_low = a.astype(BF16)
    low_ref[...] = a_low
    in_grad = tn(a_low, x_ref[...]).astype(BF16)
    out_grad = (4.0 * tn(alow_ref[...], g)).astype(BF16)
    size = 4 * extra
    for k in range(4):
        rows = slice(k * size, (k + 1) * size)
        slot_refs[k][:size] = in_grad[rows]
        slot_refs[k][size : 2 * size] = out_grad[rows]
        slot_refs[k][2 * size :] = jnp.zeros((16, g.shape[1]), BF16)
        slot_refs[k][2 * size :, :size] = split_lines(bias[:, rows])


def adapter_back(ids, g, x, gpa, alow, pieces, units, extra):
    span, width = g.shape
    arrays, homes = gather_homes(pieces)
    vmem = pl.BlockSpec(memory_space=pltpu.VMEM)
    outs = pl.pallas_call(
        functools.partial(adapter_back_kernel, extra, units, homes),
        in_specs=[SMEM] + [vmem] * 4 + [ANY] * len(arrays),
        out_specs=[vmem] * 5,
        out_shape=[jax.ShapeDtypeStruct((span, 16 * extra), BF16)]
        + [jax.ShapeDtypeStruct((8 * extra + 16, width), BF16)] * 4,
        scratch_shapes=[pltpu.VMEM((16 * extra, width), BF16), pltpu.SemaphoreType.DMA((16,))],
        compiler_params=pltpu.CompilerParams(vmem_limit_bytes=VMEM_LIMIT),
        cost_estimate=cost(6 * span * width * 16 * extra, 12 * 2**20),
        name="adapter_back",
    )(ids, g, x, gpa, alow, *arrays)
    return outs[0], list(outs[1:])


def feed_back_kernel(units, extra, homes, ids_ref, *refs):
    refs = list(refs)
    g_ref, gp_ref, alow_ref, n_ref, r_ref, gain_ref = refs[:6]
    low_ref, sum_ref, acc, up, down, ain, w_sems, a_sems = refs[-8:]
    sources = refs[6:-8]
    step = pl.program_id(0)
    steps = len(homes) // 2
    span = g_ref.shape[0]

    def chunk_copies(j, home):
        copies = []
        for t in range(2):
            n, index = homes[2 * home + t]
            for m, held in enumerate((up, down)):
                copies.append(
                    pltpu.make_async_copy(
                        sources[n].at[index, pl.ds(m * units, units), :],
                        held.at[j % 2, pl.ds(t * units, units), :],
                        w_sems.at[j % 2, t, m],
                    )
                )
        return copies

    def ain_copies():
        return [
            pltpu.make_async_copy(
                sources[n].at[index, pl.ds(2 * units, extra), :],
                ain.at[pl.ds((4 * (p // 4) + natural(ids_ref[1], p)) * extra, extra), :],
                a_sems.at[p],
            )
            for p, (n, index) in enumerate(homes)
        ]

    @pl.when(step == 0)
    def _():
        for copy in ain_copies():
            copy.start()
        for copy in chunk_copies(0, 0):
            copy.start()
        for copy in ain_copies():
            copy.wait()
        acc[...] = nn(alow_ref[...], ain[...]) + g_ref[...].astype(F32)

    for j in range(1, steps):

        @pl.when(step == j - 1)
        def _():
            for copy in chunk_copies(j, j):
                copy.start()

    for copy in chunk_copies(step, 0):
        copy.wait()
    half = min(512, span)
    side = step % 2
    for i in range(span // half):
        rows = slice(i * half, (i + 1) * half)
        h = (nt(g_ref[rows, :], down[side]) * gp_ref[rows, :].astype(F32)).astype(BF16)
        acc[rows, :] += nn(h, up[side])

    @pl.when(step == pl.num_programs(0) - 1)
    def _():
        sum_ref[...] = jnp.zeros_like(sum_ref)
        for i in range(span // ROWS):
            rows = slice(i * ROWS, (i + 1) * ROWS)
            grad = acc[rows, :]
            normed = n_ref[rows, :].astype(F32)
            back = norm_back_rows(grad, normed, r_ref[rows, :], gain_ref[...])
            low_ref[rows, :] = back.astype(BF16)
            sum_ref[0:1, :] += sum_rows(grad * normed)
            sum_ref[1:2, :] += sum_rows(grad)


def feed_back(ids, g, slopes, a_low, pieces, normed, scale, gain, units, extra):
    span, width = g.shape
    arrays, homes = gather_homes(pieces)
    whole = lambda a: pl.BlockSpec(a.shape, lambda j: (0,) * a.ndim, pipeline_mode=pl.Buffered(1))
    out_shape = (jax.ShapeDtypeStruct((span, width), BF16), jax.ShapeDtypeStruct((8, width), F32))
    return pl.pallas_call(
        functools.partial(feed_back_kernel, units, extra, homes),
        grid=(8,),
        in_specs=[
            SMEM,
            whole(g),
            pl.BlockSpec((span, 2 * units), lambda j: (0, j)),
            whole(a_low),
            whole(normed),
            whole(scale),
            whole(gain),
        ]
        + [ANY] * len(arrays),
        out_specs=tuple(
            pl.BlockSpec(s.shape, lambda j: (0, 0), pipeline_mode=pl.Buffered(1)) for s in out_shape
        ),
        out_shape=out_shape,
        scratch_shapes=[
            pltpu.VMEM((span, width), F32),
            pltpu.VMEM((2, 2 * units, width), BF16),
            pltpu.VMEM((2, 2 * units, width), BF16),
            pltpu.VMEM((16 * extra, width), BF16),
            pltpu.SemaphoreType.DMA((2, 2, 2)),
            pltpu.SemaphoreType.DMA((16,)),
        ],
        compiler_params=pltpu.CompilerParams(vmem_limit_bytes=VMEM_LIMIT),
        cost_estimate=cost(20 * 10**9, 40 * 2**20),
        name="feed_back",
    )(ids, g, slopes, a_low, normed, scale, gain, *arrays)


def attention_back_kernel(causal, homes, *refs):
    refs = list(refs)
    g_ref, e_ref, hd_ref, il_ref = refs[:4]
    refs = refs[4:]
    if not causal:
        n_ref, r_ref, gain_ref = [refs.pop(0) for _ in range(3)]
    sources_of = [refs.pop(0) for _ in range(len(set(n for n, _ in homes)))]
    if causal:
        passed_hbm = refs.pop(0)
    out_ref = refs.pop(0)
    if causal:
        put_hbm = refs.pop(0)
    else:
        low_ref, sum_ref = [refs.pop(0) for _ in range(2)]
    wf, ct, dq, dk, dv, sems = refs[:6]
    step = pl.program_id(0)
    if causal:
        passing, pass_sems = refs[6:]
        bring = pltpu.make_async_copy(passed_hbm, passing, pass_sems.at[0])
        put = pltpu.make_async_copy(passing, put_hbm, pass_sems.at[1])

        @pl.when(step == 1)
        def _():
            bring.start()

        @pl.when(step == 3)
        def _():
            bring.wait()
            put.start()

        @pl.when(step == pl.num_programs(0) - 1)
        def _():
            put.wait()

    span = g_ref.shape[0]
    sources = e_ref.shape[1]
    part = wf.shape[1] // len(homes)

    def copies(wanted):
        found = []
        for p, (n, index) in enumerate(homes):
            begin, size = (3, 1) if wanted else (0, 3)
            found.append(
                pltpu.make_async_copy(
                    sources_of[n].at[index, pl.ds(begin, size)],
                    wf.at[pl.ds(begin, size), pl.ds(p * part, part), :],
                    sems.at[wanted, p],
                )
            )
        return found

    @pl.when(step == 0)
    def _():
        for copy in copies(1) + copies(0):
            copy.start()
        for copy in copies(1):
            copy.wait()
        ct[...] = nt(wf[3], g_ref[...]).astype(BF16)

    pair = pl.ds(pl.multiple_of(step * 128, 128), 128)
    c2 = ct[pair, :]
    block = min(BLOCK if causal else 512, span)
    scaled, dots = [], []
    for h in range(2):
        c = c2[head_rows(h), :].astype(F32) * il_ref[h]
        dots.append(jnp.sum(c * hd_ref[3, head_rows(h), :].astype(F32), axis=0, keepdims=True))
        scaled.append(c.astype(BF16))
    sums_k, sums_v = [None, None], [None, None]
    for i in reversed(range(span // block)):
        n = (i + 1) * block if causal else sources
        cols = slice(i * block, (i + 1) * block)
        grads = [tn(hd_ref[2, head_rows(h), :n], scaled[h][:, cols]) for h in range(2)]
        queries = []
        for h in range(2):
            e = e_ref[h, :n, cols]
            ds = (e.astype(F32) * (grads[h] - dots[h][:, cols])).astype(BF16)
            queries.append((nn(hd_ref[1, head_rows(h), :n], ds) * HEAD**-0.5).astype(BF16))
            gk = nn(ds, hd_ref[0, head_rows(h), cols].T)
            gv = nn(e, scaled[h][:, cols].T)
            if sums_k[h] is None:
                sums_k[h], sums_v[h] = gk, gv
            elif n == sums_k[h].shape[0]:
                sums_k[h], sums_v[h] = sums_k[h] + gk, sums_v[h] + gv
            else:
                sums_k[h] = jnp.concatenate([sums_k[h][:n] + gk, sums_k[h][n:]], axis=0)
                sums_v[h] = jnp.concatenate([sums_v[h][:n] + gv, sums_v[h][n:]], axis=0)
        dq[cols, pair] = jnp.concatenate(queries, axis=0).T
    dk[:, pair] = (jnp.concatenate(sums_k, axis=1) * LN2).astype(BF16)
    dv[:, pair] = jnp.concatenate(sums_v, axis=1).astype(BF16)

    @pl.when(step == pl.num_programs(0) - 1)
    def _():
        for copy in copies(0):
            copy.wait()
        for i in range(sources // ROWS):
            rows = slice(i * ROWS, (i + 1) * ROWS)
            total = nn(dk[rows, :], wf[1]) + nn(dv[rows, :], wf[2])
            if causal:
                total = total + nn(dq[rows, :], wf[0]) + g_ref[rows, :].astype(F32)
            out_ref[rows, :] = total.astype(BF16)
        if not causal:
            sum_ref[...] = jnp.zeros_like(sum_ref)
            for i in range(span // ROWS):
                rows = slice(i * ROWS, (i + 1) * ROWS)
                grad = nn(dq[rows, :], wf[0]) + g_ref[rows, :].astype(F32)
                normed = n_ref[rows, :].astype(F32)
                back = norm_back_rows(grad, normed, r_ref[rows, :], gain_ref[...])
                low_ref[rows, :] = back.astype(BF16)
                sum_ref[0:1, :] += sum_rows(grad * normed)
                sum_ref[1:2, :] += sum_rows(grad)


def attention_back(g, kept, pieces, norm, passed=None):
    e, hd, il, _ = kept
    causal = norm is None
    span, width = g.shape
    heads, sources, _ = e.shape
    arrays, homes = gather_homes(pieces)
    whole = lambda a: pl.BlockSpec(a.shape, lambda j: (0,) * a.ndim, pipeline_mode=pl.Buffered(1))
    operands = [g, e, hd, il]
    specs = [
        whole(g),
        pl.BlockSpec((2, sources, span), lambda j: (j, 0, 0)),
        pl.BlockSpec((4, 128, span), lambda j: (0, j, 0)),
        pl.BlockSpec((2, 1, span), lambda j: (j, 0, 0)),
    ]
    out_shape = [jax.ShapeDtypeStruct((sources, width), BF16)]
    if not causal:
        operands += list(norm)
        specs += [whole(a) for a in norm]
        out_shape += [jax.ShapeDtypeStruct((span, width), BF16), jax.ShapeDtypeStruct((8, width), F32)]
    out_specs = [pl.BlockSpec(s.shape, lambda j: (0, 0), pipeline_mode=pl.Buffered(1)) for s in out_shape]
    scratch = []
    if causal:
        arrays = arrays + [passed]
        out_shape.append(jax.ShapeDtypeStruct(passed.shape, passed.dtype))
        out_specs.append(ANY)
        scratch = [pltpu.VMEM(passed.shape, passed.dtype), pltpu.SemaphoreType.DMA((2,))]
    return pl.pallas_call(
        functools.partial(attention_back_kernel, causal, homes),
        grid=(heads // 2,),
        in_specs=specs + [ANY] * len(arrays),
        out_specs=out_specs,
        out_shape=out_shape,
        scratch_shapes=[
            pltpu.VMEM((4, width, width), BF16),
            pltpu.VMEM((width, span), BF16),
            pltpu.VMEM((span, width), BF16),
            pltpu.VMEM((sources, width), BF16),
            pltpu.VMEM((sources, width), BF16),
            pltpu.SemaphoreType.DMA((2, len(homes))),
        ]
        + scratch,
        compiler_params=pltpu.CompilerParams(vmem_limit_bytes=VMEM_LIMIT),
        cost_estimate=cost(40 * 10**9, 60 * 2**20),
        name="self_back" if causal else "cross_back",
    )(*operands, *arrays)


def copy_kernel(from_ref, to_ref):
    to_ref[...] = from_ref[...]


def copied(values):
    spec = pl.BlockSpec((1,) + values.shape[1:], lambda i: (i, 0, 0))
    return pl.pallas_call(
        copy_kernel,
        grid=(values.shape[0],),
        in_specs=[spec],
        out_specs=spec,
        out_shape=jax.ShapeDtypeStruct(values.shape, values.dtype),
        cost_estimate=cost(0, 4 * 2**20),
        name="copied",
    )(values)


def swap(values, name, bit):
    size = lax.axis_size(name)
    return lax.ppermute(values, name, [(i, i ^ bit) for i in range(size)])


def cross_swap(values, even, odd):
    size = lax.axis_size("tensor")
    pairs = []
    for d in range(lax.axis_size("dp")):
        for i in range(size):
            pairs.append((d * size + i, d * size + (i ^ (odd if d % 2 else even))))
    return lax.ppermute(values, ("dp", "tensor"), pairs)


def turn_over(values):
    return lax.all_to_all(values, "tensor", 0, 0, tiled=True)


def add_low(left, right):
    return (left.astype(F32) + right.astype(F32)).astype(BF16)


def after(values, *earlier):
    return lax.optimization_barrier((values, earlier))[0]


def near(what, own):
    with jax.named_scope(what + "_near"):
        return cross_swap(own, 1, 2)


def onward(what, shard, parts=2):
    where = lax.axis_index("dp")
    begin = 2 * (where % 2) + (where // 2 % 2 if parts == 1 else 0)
    half = lax.dynamic_slice_in_dim(shard, begin, parts, 0)
    with jax.named_scope(what + "_onward"):
        return cross_swap(half, 2, 1)


def core(what, values):
    with jax.named_scope(what + "_core"):
        return swap(values, "dp", 1)


def all_pieces(*arrays):
    return [(array, t) for array in arrays for t in range(array.shape[0])]


def whole_sequences(
    inputs,
    encoded,
    source_lengths,
    query_weight,
    key_weight,
    value_weight,
    output_weight,
    cross_query,
    cross_key,
    cross_value,
    cross_output,
    up_weight,
    down_weight,
    adapter_in,
    adapter_out,
    adapter_bias,
    adapter_shift,
    norm_gains,
    norm_shifts,
    output_grad,
):
    place = lax.axis_index("tensor")
    turn = 2 * (lax.axis_index("dp") % 2) + lax.axis_index("dp") // 2 % 2
    _, share, width = inputs.shape
    span = 4 * share
    units, extra = up_weight.shape[1] // 4, adapter_in.shape[1] // 4
    length = lax.dynamic_index_in_dim(source_lengths, place, 0, keepdims=False)
    ids = jnp.stack([place, turn, length]).astype(jnp.int32)
    gain = lambda j: norm_gains[j : j + 1]
    shift = lambda j: norm_shifts[j : j + 1]
    heads_shape = (4, output_weight.shape[0] // 4, width)
    units_shape = (2 * units + 2 * extra + 16, width)

    x = turn_over(inputs).reshape(span, width)
    self_own = pack(
        pack_heads_kernel, "pack_self", ids, heads_shape, query_weight, key_weight, value_weight, output_weight
    )
    shard = near("self", self_own)
    cross_own = pack(
        pack_heads_kernel,
        "pack_cross",
        after(ids, self_own),
        heads_shape,
        cross_query,
        cross_key,
        cross_value,
        cross_output,
    )
    feed_own = pack(
        pack_units_kernel,
        "pack_feed",
        after(ids, cross_own),
        units_shape,
        up_weight,
        down_weight,
        adapter_in,
        adapter_out,
        adapter_bias.reshape(1, -1),
    )
    x = after(x, feed_own)
    self_kept = attend_slots(ids, (0,), x, None, all_pieces(self_own), None)

    shard = after(shard, self_kept[0])
    half, core_shard = onward("self", shard), core("self", shard)
    source = turn_over(after(encoded, core_shard)).reshape(span, width)
    self_pieces = all_pieces(self_own, shard, core_shard)
    self_kept = attend_slots(ids, (1, 2), after(x, core_shard), None, self_pieces, self_kept)
    half = after(half, self_kept[0])
    self_pieces += all_pieces(half, core("self", half))
    cross_shard = near("cross", after(cross_own, source, half))
    self_kept = attend_slots(ids, (3,), x, None, self_pieces, self_kept)
    first, normed_one, scale_one = out_norm(self_kept[3], self_pieces, x, gain(0), shift(0))

    shard = after(cross_shard, first)
    half, core_shard = onward("cross", shard), core("cross", shard)
    feed_shard = near("feed", after(feed_own, shard))
    cross_pieces = all_pieces(cross_own, shard)
    cross_kept = attend_slots(ids, (0, 1), after(first, shard), source, cross_pieces, None)
    half = after(half, cross_kept[0])
    cross_pieces += all_pieces(core_shard, half, core("cross", half))
    cross_kept = attend_slots(ids, (2, 3), first, source, cross_pieces, cross_kept)
    second, normed_two, scale_two = out_norm(cross_kept[3], cross_pieces, first, gain(1), shift(1))

    shard = after(feed_shard, second)
    piece, core_shard = onward("feed", shard, 1), core("feed", shard)
    kept, rest = feed_slots(
        ids, (0,), after(second, shard), all_pieces(feed_own), None, None, units, extra
    )
    piece = after(piece, rest[0])
    with jax.named_scope("feed_far"):
        far_piece = swap(piece, "dp", 2)
    core_piece = core("feed", piece)
    feed_pieces = all_pieces(feed_own, shard, core_shard)
    grad = turn_over(after(output_grad, core_piece)).reshape(span, width)
    kept, rest = feed_slots(ids, (1, 2), second, feed_pieces, rest + kept, None, units, extra)
    far_piece = after(far_piece, rest[0], grad)
    feed_pieces += all_pieces(piece, far_piece, core_piece, core("feed", far_piece))
    norm = (adapter_shift.reshape(1, -1), gain(2), shift(2), grad)
    kept, rest = feed_slots(ids, (3,), second, feed_pieces, rest + kept, norm, units, extra)
    outcome, branch_low, sums_three = rest
    slopes, adapter_slopes, adapted_low = kept
    result = turn_over(outcome.reshape(4, share, width))
    a_low, grads = adapter_back(
        ids, branch_low, second, adapter_slopes, adapted_low, feed_pieces, units, extra
    )
    with jax.named_scope("adapter"):
        grads_there = [
            cross_swap(grads[1], 1, 2),
            cross_swap(grads[2], 2, 1),
            swap(grads[3], "tensor", 3),
        ]
    cross_low, sums_two = feed_back(
        ids,
        after(branch_low, a_low),
        slopes,
        a_low,
        feed_pieces,
        normed_two,
        scale_two,
        gain(1),
        units,
        extra,
    )
    adapter_sum = grads[0].astype(F32)
    for part in grads_there:
        adapter_sum = adapter_sum + part.astype(F32)
    adapter_sum = adapter_sum.astype(BF16)
    with jax.named_scope("adapter"):
        adapter_there = swap(adapter_sum, "dp", 1)
    encoded_back, self_low, sums_one = attention_back(
        after(cross_low, adapter_sum), cross_kept, cross_pieces, (normed_one, scale_one, gain(0))
    )
    adapter_sum = add_low(adapter_sum, after(adapter_there, self_low))
    encoded_result = turn_over(encoded_back.reshape(4, share, width))
    small = jnp.concatenate(
        [
            sums_one[0:1],
            sums_two[0:1],
            sums_three[0:1],
            sums_one[1:2],
            sums_two[1:2],
            sums_three[1:2],
            sums_three[2:3],
            jnp.zeros((1, width), F32),
        ],
        axis=0,
    )
    with jax.named_scope("small"):
        small_there = [swap(small, "tensor", k) for k in (1, 2, 3)]
    with jax.named_scope("adapter"):
        adapter_there = swap(adapter_sum, "dp", 2)
    input_back, result = attention_back(
        after(self_low, small, adapter_sum), self_kept, self_pieces, None, result
    )
    input_back, small_there, adapter_there, encoded_result = lax.optimization_barrier(
        (input_back, small_there, adapter_there, encoded_result)
    )
    input_result = turn_over(input_back.reshape(4, share, width))
    for part in small_there:
        small = small + part
    adapter_sum = add_low(adapter_sum, adapter_there)
    bit = 4
    while bit < lax.axis_size("dp"):
        with jax.named_scope("adapter"):
            adapter_sum = add_low(adapter_sum, swap(adapter_sum, "dp", bit))
        bit *= 2
    bit = 1
    while bit < lax.axis_size("dp"):
        with jax.named_scope("small"):
            small = small + swap(small, "dp", bit)
        bit *= 2
    encoded_result = copied(encoded_result)
    adapter_sum = adapter_sum.astype(F32)
    size = 4 * extra
    return (
        result,
        input_result,
        encoded_result,
        adapter_sum[:size].T,
        adapter_sum[size : 2 * size],
        jnp.sum(adapter_sum[2 * size :, :size], axis=0),
        small[6],
        small[0:3],
        small[3:6],
    )


def gelu_tanh(values):
    return jax.nn.gelu(values, approximate=True)


def multiply(left, right):
    return jnp.dot(left, right, preferred_element_type=jnp.float32)


def multiply_by_transpose(left, right):
    return lax.dot_general(
        left, right, (((1,), (1,)), ((), ())), preferred_element_type=jnp.float32
    )


def multiply_transposed_left(left, right):
    return lax.dot_general(
        left, right, (((0,), (0,)), ((), ())), preferred_element_type=jnp.float32
    )


def layer_norm(values, gain, shift):
    center = values - jnp.mean(values, axis=-1, keepdims=True)
    scale = lax.rsqrt(jnp.mean(center * center, axis=-1, keepdims=True) + 1e-05)
    normed = center * scale
    return (normed * gain + shift, normed, scale)


def norm_back(grad, normed, scale, gain):
    inner = grad * gain
    middle = jnp.mean(inner, axis=-1, keepdims=True)
    along = jnp.mean(inner * normed, axis=-1, keepdims=True)
    return (
        scale * (inner - middle - normed * along),
        jnp.sum(grad * normed, axis=(0, 1)),
        jnp.sum(grad, axis=(0, 1)),
    )


def attend(query_low, key_low, value_low, keep_for):
    count = query_low.shape[1]
    block = min(512, count)
    factor = query_low.shape[-1] ** (-0.5)
    contexts = []
    totals = []
    for first in range(0, count, block):
        scores = (
            jnp.einsum(
                "sqhe,skhe->shqk",
                query_low[:, first : first + block],
                key_low,
                preferred_element_type=jnp.float32,
            )
            * factor
        )
        scores = jnp.where(keep_for(first, block), scores, -1000000000.0)
        top_score = jnp.max(scores, axis=-1, keepdims=True)
        weights = jnp.exp(scores - top_score)
        denom = jnp.sum(weights, axis=-1, keepdims=True)
        probs_low = (weights / denom).astype(jnp.bfloat16)
        contexts.append(
            jnp.einsum("shqk,skhe->sqhe", probs_low, value_low, preferred_element_type=jnp.float32)
        )
        totals.append(top_score + jnp.log(denom))
    return (jnp.concatenate(contexts, axis=1), jnp.concatenate(totals, axis=2))


def attend_back(query_low, key_low, value_low, grad_low, totals, keep_for):
    count = query_low.shape[1]
    block = min(512, count)
    factor = query_low.shape[-1] ** (-0.5)
    key_grad = jnp.zeros(key_low.shape, jnp.float32)
    value_grad = jnp.zeros(value_low.shape, jnp.float32)
    query_grads = []
    for first in range(0, count, block):
        query_part = query_low[:, first : first + block]
        grad_part = grad_low[:, first : first + block]
        scores = (
            jnp.einsum("sqhe,skhe->shqk", query_part, key_low, preferred_element_type=jnp.float32)
            * factor
        )
        scores = jnp.where(keep_for(first, block), scores, -1000000000.0)
        probs = jnp.exp(scores - totals[:, :, first : first + block])
        probs_low = probs.astype(jnp.bfloat16)
        prob_grad = jnp.einsum(
            "sqhe,skhe->shqk", grad_part, value_low, preferred_element_type=jnp.float32
        )
        value_grad = value_grad + jnp.einsum(
            "shqk,sqhe->skhe", probs_low, grad_part, preferred_element_type=jnp.float32
        )
        along = jnp.sum(prob_grad * probs, axis=-1, keepdims=True)
        score_grad = (probs * (prob_grad - along)).astype(jnp.bfloat16)
        query_grads.append(
            jnp.einsum("shqk,skhe->sqhe", score_grad, key_low, preferred_element_type=jnp.float32)
            * factor
        )
        key_grad = (
            key_grad
            + jnp.einsum(
                "shqk,sqhe->skhe", score_grad, query_part, preferred_element_type=jnp.float32
            )
            * factor
        )
    return (jnp.concatenate(query_grads, axis=1), key_grad, value_grad)


def local(
    inputs,
    encoded,
    source_lengths,
    query_weight,
    key_weight,
    value_weight,
    output_weight,
    cross_query,
    cross_key,
    cross_value,
    cross_output,
    up_weight,
    down_weight,
    adapter_in,
    adapter_out,
    adapter_bias,
    adapter_shift,
    norm_gains,
    norm_shifts,
    output_grad,
):
    parts = lax.axis_size("tensor")
    place = lax.axis_index("tensor")
    sequences, share, width = inputs.shape
    length = share * parts
    rows = sequences * length
    heads = query_weight.shape[1] // HEAD
    local_width = heads * HEAD
    whole_inputs, whole_encoded = (
        lax.all_gather(inputs, "tensor", axis=1, tiled=True),
        lax.all_gather(encoded, "tensor", axis=1, tiled=True),
    )
    sources = whole_encoded.shape[1]
    flat_inputs = whole_inputs.reshape(rows, width)
    flat_encoded = whole_encoded.reshape(sequences * sources, width)

    def split_heads(values, count):
        return values.astype(jnp.bfloat16).reshape(sequences, count, heads, HEAD)

    def causal(first, block):
        query_pos = first + lax.broadcasted_iota(jnp.int32, (block, length), 0)
        key_pos = lax.broadcasted_iota(jnp.int32, (block, length), 1)
        return (key_pos <= query_pos)[None, None]

    def padded(first, block):
        key_pos = lax.broadcasted_iota(jnp.int32, (sequences, 1, 1, sources), 3)
        return key_pos < source_lengths[:, None, None, None]

    self_query = split_heads(multiply(flat_inputs, query_weight), length)
    self_key = split_heads(multiply(flat_inputs, key_weight), length)
    self_value = split_heads(multiply(flat_inputs, value_weight), length)
    self_context, self_totals = attend(self_query, self_key, self_value, causal)
    self_context_low = self_context.astype(jnp.bfloat16).reshape(rows, local_width)
    self_partial = multiply(self_context_low, output_weight).reshape(sequences, length, width)
    self_full = lax.psum(self_partial.astype(jnp.bfloat16), "tensor").astype(jnp.float32)
    first_full, normed_full, scale_full = layer_norm(
        whole_inputs.astype(jnp.float32) + self_full, norm_gains[0], norm_shifts[0]
    )
    first_low = first_full.astype(jnp.bfloat16)
    first_share = lax.dynamic_slice_in_dim(first_full, place * share, share, 1)
    normed_one = lax.dynamic_slice_in_dim(normed_full, place * share, share, 1)
    scale_one = lax.dynamic_slice_in_dim(scale_full, place * share, share, 1)
    flat_first = first_low.reshape(rows, width)
    cross_q = split_heads(multiply(flat_first, cross_query), length)
    cross_k = split_heads(multiply(flat_encoded, cross_key), sources)
    cross_v = split_heads(multiply(flat_encoded, cross_value), sources)
    cross_context, cross_totals = attend(cross_q, cross_k, cross_v, padded)
    cross_context_low = cross_context.astype(jnp.bfloat16).reshape(rows, local_width)
    cross_partial = multiply(cross_context_low, cross_output).reshape(sequences, length, width)
    cross_share = lax.psum_scatter(
        cross_partial.astype(jnp.bfloat16), "tensor", scatter_dimension=1, tiled=True
    ).astype(jnp.float32)
    second_share, normed_two, scale_two = layer_norm(
        first_share + cross_share, norm_gains[1], norm_shifts[1]
    )
    second_low = lax.all_gather(second_share.astype(jnp.bfloat16), "tensor", axis=1, tiled=True)
    flat_second = second_low.reshape(rows, width)
    hidden = multiply(flat_second, up_weight)
    hidden_low = gelu_tanh(hidden).astype(jnp.bfloat16)
    adapted = multiply(flat_second, adapter_in) + adapter_bias
    adapted_low = gelu_tanh(adapted).astype(jnp.bfloat16)
    branch_partial = multiply(hidden_low, down_weight) + 4.0 * multiply(adapted_low, adapter_out)
    branch_share = lax.psum_scatter(
        branch_partial.reshape(sequences, length, width).astype(jnp.bfloat16),
        "tensor",
        scatter_dimension=1,
        tiled=True,
    ).astype(jnp.float32)
    third_input = second_share + branch_share + 4.0 * adapter_shift
    outcome, normed_three, scale_three = layer_norm(third_input, norm_gains[2], norm_shifts[2])
    grad_three, gain_grad_three, shift_grad_three = norm_back(
        output_grad.astype(jnp.float32), normed_three, scale_three, norm_gains[2]
    )
    shift_grad_adapter = 4.0 * jnp.sum(grad_three, axis=(0, 1))
    branch_grad = lax.all_gather(
        grad_three.astype(jnp.bfloat16), "tensor", axis=1, tiled=True
    ).reshape(rows, width)
    hidden_grad = multiply_by_transpose(branch_grad, down_weight)
    hidden_unused, hidden_pull = jax.vjp(gelu_tanh, hidden)
    hidden_grad_low = hidden_pull(hidden_grad)[0].astype(jnp.bfloat16)
    adapted_grad = 4.0 * multiply_by_transpose(branch_grad, adapter_out)
    adapted_unused, adapted_pull = jax.vjp(gelu_tanh, adapted)
    adapted_grad = adapted_pull(adapted_grad)[0]
    bias_grad = jnp.sum(adapted_grad, axis=0)
    adapted_grad_low = adapted_grad.astype(jnp.bfloat16)
    in_grad = multiply_transposed_left(flat_second, adapted_grad_low)
    out_grad = 4.0 * multiply_transposed_left(adapted_low, branch_grad)
    second_partial = multiply_by_transpose(hidden_grad_low, up_weight) + multiply_by_transpose(
        adapted_grad_low, adapter_in
    )
    second_grad = grad_three + lax.psum_scatter(
        second_partial.reshape(sequences, length, width).astype(jnp.bfloat16),
        "tensor",
        scatter_dimension=1,
        tiled=True,
    ).astype(jnp.float32)
    grad_two, gain_grad_two, shift_grad_two = norm_back(
        second_grad, normed_two, scale_two, norm_gains[1]
    )
    cross_grad = lax.all_gather(
        grad_two.astype(jnp.bfloat16), "tensor", axis=1, tiled=True
    ).reshape(rows, width)
    cross_context_grad = multiply_by_transpose(cross_grad, cross_output).astype(jnp.bfloat16)
    cross_context_grad = cross_context_grad.reshape(sequences, length, heads, HEAD)
    cq_grad, ck_grad, cv_grad = attend_back(
        cross_q, cross_k, cross_v, cross_context_grad, cross_totals, padded
    )
    first_partial = multiply_by_transpose(
        cq_grad.astype(jnp.bfloat16).reshape(rows, local_width), cross_query
    )
    encoded_partial = multiply_by_transpose(
        ck_grad.astype(jnp.bfloat16).reshape(sequences * sources, local_width), cross_key
    ) + multiply_by_transpose(
        cv_grad.astype(jnp.bfloat16).reshape(sequences * sources, local_width), cross_value
    )
    first_back, encoded_share = (
        lax.psum_scatter(
            first_partial.reshape(sequences, length, width).astype(jnp.bfloat16),
            "tensor",
            scatter_dimension=1,
            tiled=True,
        ).astype(jnp.float32),
        lax.psum_scatter(
            encoded_partial.reshape(sequences, sources, width).astype(jnp.bfloat16),
            "tensor",
            scatter_dimension=1,
            tiled=True,
        ).astype(jnp.float32),
    )
    grad_one, gain_grad_one, shift_grad_one = norm_back(
        grad_two + first_back, normed_one, scale_one, norm_gains[0]
    )
    self_grad = lax.all_gather(grad_one.astype(jnp.bfloat16), "tensor", axis=1, tiled=True).reshape(
        rows, width
    )
    self_context_grad = multiply_by_transpose(self_grad, output_weight).astype(jnp.bfloat16)
    self_context_grad = self_context_grad.reshape(sequences, length, heads, HEAD)
    sq_grad, sk_grad, sv_grad = attend_back(
        self_query, self_key, self_value, self_context_grad, self_totals, causal
    )
    input_partial = (
        multiply_by_transpose(sq_grad.astype(jnp.bfloat16).reshape(rows, local_width), query_weight)
        + multiply_by_transpose(sk_grad.astype(jnp.bfloat16).reshape(rows, local_width), key_weight)
        + multiply_by_transpose(
            sv_grad.astype(jnp.bfloat16).reshape(rows, local_width), value_weight
        )
    )
    small_grads = jnp.stack(
        [
            gain_grad_one,
            gain_grad_two,
            gain_grad_three,
            shift_grad_one,
            shift_grad_two,
            shift_grad_three,
            shift_grad_adapter,
        ]
    )
    spread = jnp.broadcast_to(small_grads[:, None, :], (7, parts, width))
    input_back, small_back = (
        lax.psum_scatter(
            input_partial.reshape(sequences, length, width).astype(jnp.bfloat16),
            "tensor",
            scatter_dimension=1,
            tiled=True,
        ).astype(jnp.float32),
        lax.psum_scatter(
            spread.astype(jnp.bfloat16), "tensor", scatter_dimension=1, tiled=True
        ).astype(jnp.float32),
    )
    input_result = (grad_one + input_back).astype(jnp.bfloat16)
    encoded_result = encoded_share.astype(jnp.bfloat16)
    in_total, out_total, bias_total, small_total = (
        lax.psum(in_grad.astype(jnp.bfloat16), "dp").astype(jnp.float32),
        lax.psum(out_grad.astype(jnp.bfloat16), "dp").astype(jnp.float32),
        lax.psum(bias_grad.astype(jnp.bfloat16), "dp").astype(jnp.float32),
        lax.psum(small_back[:, 0].astype(jnp.bfloat16), "dp").astype(jnp.float32),
    )
    return (
        outcome.astype(jnp.bfloat16),
        input_result,
        encoded_result,
        in_total,
        out_total,
        bias_total,
        small_total[6],
        small_total[0:3],
        small_total[3:6],
    )


def solution(mesh):
    placed = (
        P("dp", "tensor", None),
        P("dp", "tensor", None),
        P("dp"),
        P(None, "tensor"),
        P(None, "tensor"),
        P(None, "tensor"),
        P("tensor", None),
        P(None, "tensor"),
        P(None, "tensor"),
        P(None, "tensor"),
        P("tensor", None),
        P(None, "tensor"),
        P("tensor", None),
        P(None, "tensor"),
        P("tensor", None),
        P("tensor"),
        P(),
        P(),
        P(),
        P("dp", "tensor", None),
    )
    suits = mesh.shape["tensor"] == 4 and mesh.shape["dp"] in (4, 8, 16, 32)

    def layer(*arrays):
        if suits and arrays[0].shape[:2] == (4, ROWS) and arrays[1].shape[:2] == (4, ROWS):
            return whole_sequences(*arrays)
        return local(*arrays)

    return jax.shard_map(
        layer,
        mesh=mesh,
        in_specs=placed,
        out_specs=(
            P("dp", "tensor", None),
            P("dp", "tensor", None),
            P("dp", "tensor", None),
            P(None, "tensor"),
            P("tensor", None),
            P("tensor"),
            P(),
            P(),
            P(),
        ),
        check_vma=False,
    )
```
